32 devices in a mesh: gx: 4 (over z), gy: 4 (over x, core), gz: 2 (over y).
Axes of the slice: x: 2, y: 2, z: 4, core: 2. Of those that a mesh axis runs over, the one named last changes fastest.
Arguments:
- forcing: float32 [128, 128, 256], P('gx', 'gy', 'gz'), may hold values from -6 to 6
- kappa_base: float32 [128, 128, 256], P('gx', 'gy', 'gz'), may hold values from 0.5 to 2
- labels: int32 [128, 128, 256], P('gx', 'gy', 'gz'), may hold values from 0 to 3
- contrast: float32 [4], replicated, may hold values from 1 to 100
- channel_weight: float32 [4], replicated, may hold values from 0.25 to 2
- coarse_coef: float32 [4, 4, 2, 64, 8], P('gx', 'gy', 'gz'), may hold values from -6 to 6
- source_link: int32 [4, 4, 2, 40, 4], P('gx', 'gy', 'gz'), may hold values from 0 to 63, as said below
- offsets: int32 [4, 4, 2, 40, 3], P('gx', 'gy', 'gz'), may hold values from 0 to 120, as said below
- live_pieces: int32 [4, 4, 2], P('gx', 'gy', 'gz'), may hold values from 5 to 40, as said below
- resident_bases: float32 [4, 4, 2, 40, 8, 4096], P('gx', 'gy', 'gz'), may hold values from -5 to 5
Outputs:
- update: float32 [128, 128, 256], P('gx', 'gy', 'gz')
- new_basis: float32 [4, 4, 2, 40, 2, 4096], P('gx', 'gy', 'gz')
The draws below stay inside these ranges and needn't reach their ends.
Inputs may be any that keep to these rules, and one draw needn't show every extreme that they name: `source_link`: each of the three brick offsets of a slot, minus one, leads to a brick inside the mesh; a coefficient slot may be named by several pieces. `offsets`: every piece lies inside its brick's padded frame of (40) x (40) x (136) cells. `live_pieces`: some brick has all 40 slots live in every draw.
All inputs are finite; a program needn't handle non-finite values.
Results may differ from the reference program's by a relative error of at most 0.0003.
Values sent between devices are 32-bit elements; how exact they have to be, the bound alone decides.
No kernel may reach another device: no remote copies, remote signals or barrier semaphores. Data moves between devices by JAX's collectives and lax.ppermute only.
A program may use at most 128 MiB of HBM per device.

```python
import math
import jax
import jax.numpy as jnp
from jax import lax

BX = 32
BY = 32
BZ = 128
MARGIN = 4
PIECE = 16
NB = 8
NP = 40
ND = 64
NCH = 4
SWEEPS = 20
NX = 128
NY = 128
NZ = 256
N_GX = 4
N_GY = 4
N_GZ = 2


def draw_labels(key, part):
    table = jax.random.randint(key, (NX // 2, NY // 2, NZ // 16), 0, NCH)
    spread = jnp.repeat(jnp.repeat(jnp.repeat(table, 2, 0), 2, 1), 16, 2)
    return spread.astype(jnp.int32)


def draw_source_link(key, part):
    key_steps = jax.random.fold_in(key, 11)
    key_slots = jax.random.fold_in(key, 12)
    steps_drawn = jax.random.randint(key_steps, (N_GX, N_GY, N_GZ, NP, 3), -1, 2)
    along_x = jnp.arange(N_GX)[:, None, None, None]
    along_y = jnp.arange(N_GY)[None, :, None, None]
    along_z = jnp.arange(N_GZ)[None, None, :, None]
    columns = []
    for position, extent, column in ((along_x, N_GX, 0), (along_y, N_GY, 1), (along_z, N_GZ, 2)):
        target = jnp.clip(position + steps_drawn[..., column], 0, extent - 1)
        columns.append(target - position + 1)
    slot_column = jax.random.randint(key_slots, (N_GX, N_GY, N_GZ, NP), 0, ND)
    columns.append(slot_column)
    return jnp.stack(columns, -1).astype(jnp.int32)


def draw_offsets(key, part):
    upper = jnp.array([BX + 2 * MARGIN - PIECE + 1, BY + 2 * MARGIN - PIECE + 1, BZ + 2 * MARGIN - PIECE + 1], jnp.int32)
    return jax.random.randint(key, (N_GX, N_GY, N_GZ, NP, 3), 0, upper).astype(jnp.int32)


def draw_live_pieces(key, part):
    key_base = jax.random.fold_in(key, 21)
    key_pick = jax.random.fold_in(key, 22)
    base_counts = jax.random.randint(key_base, (N_GX * N_GY * N_GZ,), NP // 8, NP // 2 + 1)
    chosen = jax.random.randint(key_pick, (), 0, N_GX * N_GY * N_GZ)
    filled = base_counts.at[chosen].set(NP)
    return filled.reshape(N_GX, N_GY, N_GZ).astype(jnp.int32)


def shard_levels(rng, shape, shards, least, largest):
    factor_of, own = 1.0, jax.random.fold_in(rng, 6)
    for dim, parts in shards:
        draws = jnp.exp(jax.random.uniform(jax.random.fold_in(own, dim), (parts,), jnp.float32, least / len(shards), largest / len(shards)))
        factor_of = factor_of * jnp.repeat(draws, shape[dim] // parts).reshape([-1 if axis == dim else 1 for axis in range(len(shape))])
    return factor_of


def normal_values(key, dims, scale, bound, shards=(), held_as=jnp.bfloat16):
    loudness = shard_levels(key, dims, shards, -0.22, 0.18) if shards else 1.0
    result = jax.random.normal(key, dims, jnp.float32) * scale * loudness
    return jnp.minimum(jnp.maximum(result, -bound), bound).astype(held_as)


def setup_inputs(seed: int = 0) -> dict:
    arg_keys = jax.random.split(jax.random.key(seed), 11)
    forcing = normal_values(arg_keys[0], (NX, NY, NZ), 1.0, 6.0, ((0, 4), (1, 4), (2, 2)), jnp.float32)
    kappa_base = jnp.clip(jnp.exp(math.log(2.0) - 1.3862944 * jax.random.uniform(arg_keys[1], (NX, NY, NZ), jnp.float32) ** shard_levels(arg_keys[1], (NX, NY, NZ), ((0, 4), (1, 4), (2, 2)), -0.2, 0.2)), 0.5, 2.0)
    labels = draw_labels(jax.random.fold_in(arg_keys[10], 71), 0)
    contrast = jnp.clip(jnp.exp(jax.random.uniform(arg_keys[3], (NCH,), jnp.float32, math.log(1.0), math.log(100.0))), 1.0, 100.0)
    channel_weight = jnp.clip(jax.random.uniform(arg_keys[4], (NCH,), jnp.float32, 0.25, 2.0), 0.25, 2.0)
    coarse_coef = normal_values(arg_keys[5], (N_GX, N_GY, N_GZ, ND, NB), 1.0, 6.0, ((0, 4), (1, 4), (2, 2)), jnp.float32)
    source_link = draw_source_link(jax.random.fold_in(arg_keys[10], 71), 0)
    offsets = draw_offsets(jax.random.fold_in(arg_keys[10], 71), 0)
    live_pieces = draw_live_pieces(jax.random.fold_in(arg_keys[10], 71), 0)
    resident_bases = normal_values(arg_keys[9], (N_GX, N_GY, N_GZ, NP, NB, PIECE * PIECE * PIECE), 0.35, 5.0, ((0, 4), (1, 4), (2, 2)), jnp.float32)
    return dict(forcing=forcing, kappa_base=kappa_base, labels=labels, contrast=contrast, channel_weight=channel_weight, coarse_coef=coarse_coef, source_link=source_link, offsets=offsets, live_pieces=live_pieces, resident_bases=resident_bases)


damping = 2.0 / 3.0


def lookup(labels, values):
    accumulated = jnp.zeros(labels.shape, values.dtype)
    for channel in range(values.shape[0]):
        accumulated = accumulated + jnp.where(labels == channel, values[channel], 0.0)
    return accumulated


def neighbour(array, axis_number, offset_step):
    selection = [slice(1, -1), slice(1, -1), slice(1, -1)]
    extent = array.shape[axis_number]
    selection[axis_number] = slice(1 + offset_step, extent - 1 + offset_step)
    return array[tuple(selection)]


def apply_operator(values, conductivity, inside):
    centre = values[1:-1, 1:-1, 1:-1]
    centre_kappa = conductivity[1:-1, 1:-1, 1:-1]
    accumulated = jnp.zeros_like(centre)
    for axis_number in range(3):
        for offset_step in (-1, 1):
            beside_values = neighbour(values, axis_number, offset_step)
            beside_kappa = neighbour(conductivity, axis_number, offset_step)
            beside_inside = neighbour(inside, axis_number, offset_step)
            face_value = jnp.where(beside_inside > 0, 0.5 * (centre_kappa + beside_kappa), centre_kappa)
            accumulated = accumulated + face_value * (centre - beside_values)
    return accumulated


def shift_flat(values, stride, upward):
    filler = jnp.zeros(values.shape[:-1] + (stride,), values.dtype)
    if upward:
        return jnp.concatenate([values[..., stride:], filler], -1)
    return jnp.concatenate([filler, values[..., :-stride]], -1)


def local_solve(sources, conductivity, inside):
    flat_index = jnp.arange(PIECE ** 3)
    couplings = []
    diagonal = jnp.zeros_like(conductivity)
    for stride in (PIECE * PIECE, PIECE, 1):
        grid_position = (flat_index // stride) % PIECE
        for upward, allowed in ((True, grid_position < PIECE - 1), (False, grid_position > 0)):
            beside_kappa = shift_flat(conductivity, stride, upward)
            beside_inside = shift_flat(inside, stride, upward) * allowed.astype(inside.dtype)
            face_value = jnp.where(beside_inside > 0, 0.5 * (conductivity + beside_kappa), conductivity)
            diagonal = diagonal + face_value
            couplings.append((stride, upward, jnp.where(beside_inside > 0, face_value, 0.0)))
    divisor = jnp.where(inside > 0, diagonal, 1.0)

    def sweep(sweep_index, solution):
        gathered_terms = jnp.zeros_like(solution)
        for stride, upward, coupling in couplings:
            gathered_terms = gathered_terms + coupling[:, None, :] * shift_flat(solution, stride, upward)
        update_term = sources - (diagonal[:, None, :] * solution - gathered_terms)
        return solution + damping * inside[:, None, :] * update_term / divisor[:, None, :]

    return lax.fori_loop(0, SWEEPS, sweep, jnp.zeros_like(sources))


def tent_weights():
    flat_index = jnp.arange(PIECE ** 3)
    product = jnp.ones((PIECE ** 3,), jnp.float32)
    for stride in (PIECE * PIECE, PIECE, 1):
        grid_position = ((flat_index // stride) % PIECE).astype(jnp.float32)
        product = product * (grid_position + 0.5) * (PIECE - grid_position - 0.5) * (4.0 / (PIECE * PIECE))
    return product


def piece_place(number, live_pieces, offsets):
    device_number = number // NP
    slot_number = number % NP
    brick_x = device_number // (N_GY * N_GZ)
    brick_y = (device_number // N_GZ) % N_GY
    brick_z = device_number % N_GZ
    active = (slot_number < live_pieces[brick_x, brick_y, brick_z]).astype(jnp.float32)
    corner = offsets[brick_x, brick_y, brick_z, slot_number]
    start_cell = ((brick_x * BX + corner[0]).astype(jnp.int32), (brick_y * BY + corner[1]).astype(jnp.int32), (brick_z * BZ + corner[2]).astype(jnp.int32))
    return brick_x, brick_y, brick_z, slot_number, active, start_cell


def reference(forcing, kappa_base, labels, contrast, channel_weight, coarse_coef, source_link, offsets, live_pieces, resident_bases):
    kappa = kappa_base * lookup(labels, contrast)
    weight = lookup(labels, channel_weight)
    cube_shape = (PIECE, PIECE, PIECE)
    total_pieces = N_GX * N_GY * N_GZ * NP
    numbers = jnp.arange(total_pieces, dtype=jnp.int32)
    flat_coef = coarse_coef.reshape(N_GX * N_GY * N_GZ, ND, NB)

    def place_coarse(field_with_halo, number):
        brick_x, brick_y, brick_z, slot_number, active, start_cell = piece_place(number, live_pieces, offsets)
        link_row = source_link[brick_x, brick_y, brick_z, slot_number]
        source_number = ((brick_x + link_row[0] - 1) * N_GY + brick_y + link_row[1] - 1) * N_GZ + brick_z + link_row[2] - 1
        coef_row = flat_coef[source_number, link_row[3]]
        values = jnp.dot(coef_row, resident_bases[brick_x, brick_y, brick_z, slot_number], precision=lax.Precision.HIGHEST) * active
        existing = lax.dynamic_slice(field_with_halo, start_cell, cube_shape)
        return lax.dynamic_update_slice(field_with_halo, existing + values.reshape(cube_shape), start_cell), None

    padded_zero = jnp.zeros((NX + 2 * MARGIN, NY + 2 * MARGIN, NZ + 2 * MARGIN), jnp.float32)
    padded_coarse, _ = lax.scan(place_coarse, padded_zero, numbers)
    coarse_field = padded_coarse[MARGIN:-MARGIN, MARGIN:-MARGIN, MARGIN:-MARGIN]

    ones_field = jnp.ones_like(kappa)
    residual = forcing - apply_operator(jnp.pad(coarse_field, 1), jnp.pad(kappa, 1), jnp.pad(ones_field, 1))

    residual_pad = jnp.pad(residual, MARGIN)
    kappa_pad = jnp.pad(kappa, MARGIN)
    weight_pad = jnp.pad(weight, MARGIN)
    inside_pad = jnp.pad(ones_field, MARGIN)
    tent = tent_weights()

    def enrich(correction, number):
        brick_x, brick_y, brick_z, slot_number, active, start_cell = piece_place(number, live_pieces, offsets)
        residual_piece = lax.dynamic_slice(residual_pad, start_cell, cube_shape).reshape(1, PIECE ** 3)
        kappa_piece = lax.dynamic_slice(kappa_pad, start_cell, cube_shape).reshape(1, PIECE ** 3)
        weight_piece = lax.dynamic_slice(weight_pad, start_cell, cube_shape).reshape(1, PIECE ** 3)
        inside_piece = lax.dynamic_slice(inside_pad, start_cell, cube_shape).reshape(1, PIECE ** 3)
        sources = jnp.stack([residual_piece, residual_piece * weight_piece], 1)
        solved = local_solve(sources, kappa_piece, inside_piece)[0] * active
        spread = (tent * (solved[0] + solved[1])).reshape(cube_shape)
        existing = lax.dynamic_slice(correction, start_cell, cube_shape)
        return lax.dynamic_update_slice(correction, existing + spread, start_cell), solved

    correction, solved_all = lax.scan(enrich, padded_zero, numbers)
    update = coarse_field + correction[MARGIN:-MARGIN, MARGIN:-MARGIN, MARGIN:-MARGIN]
    new_basis = solved_all.reshape(N_GX, N_GY, N_GZ, NP, 2, PIECE ** 3)
    return update, new_basis
```

```python
import functools

import jax
import jax.numpy as jnp
from jax import lax
from jax.experimental import pallas as pl
from jax.experimental.pallas import tpu as pltpu
from jax.sharding import PartitionSpec as P

MARGIN = 4
PIECE = 16
SWEEPS = 20
DAMPING = 2.0 / 3.0

H = MARGIN + 1
LANES = 128
SUB = 8
TOP = 8
GROUP = LANES // PIECE
HALVES = PIECE // SUB
PROWS = PIECE * PIECE
F32 = jnp.float32
VMEM_LIMIT = 48 * 1024 * 1024


def iotas():
    shape = (SUB, LANES)
    return lax.broadcasted_iota(jnp.int32, shape, 0), lax.broadcasted_iota(jnp.int32, shape, 1)


def pack_tiles(tiles, shift, lane):
    packed = jnp.zeros((SUB, LANES), F32)
    for j, tile in enumerate(tiles):
        packed = jnp.where((lane >> 4) == j, pltpu.roll(tile, (shift + PIECE * j) % LANES, 1), packed)
    return packed


def unpack_tile(packed, j, shift):
    return pltpu.roll(packed, (shift - PIECE * j + 2 * LANES) % LANES, 1)


def sum_rows(values, sub):
    for k in (1, 2, 4):
        low = (sub & k) == 0
        values = [
            jnp.where(low, a, b) + pltpu.roll(jnp.where(low, b, a), SUB - k, 0)
            for a, b in zip(values[0::2], values[1::2])
        ]
    return values[0]


def block_transpose(value, sub, lane):
    for k in (4, 2, 1):
        in_group = ((lane >> 4) & k) != 0
        in_sub = (sub & k) != 0
        if k == 4:
            other = pltpu.roll(pltpu.roll(value, 64, 1), 4, 0)
        else:
            q = pltpu.roll(value, 16 * k, 1)
            p = pltpu.roll(value, LANES - 16 * k, 1)
            m = jnp.where(in_group, q, p)
            other = jnp.where(in_sub, pltpu.roll(m, k, 0), pltpu.roll(m, SUB - k, 0))
        value = jnp.where(in_sub != in_group, other, value)
    return value


class Frame:
    def __init__(self, bx, by, bz, nz):
        self.bx, self.by, self.bz, self.nz = bx, by, bz, nz
        self.xf = bx + 2 * H
        self.yf = by + 2 * TOP
        self.tiles = self.yf // SUB
        self.rows = -(-self.xf * self.tiles // GROUP) * GROUP * SUB
        self.live_x = bx + 2 * MARGIN
        self.sides = 1 if nz == 2 else 2

    def arr(self, rows):
        return jax.ShapeDtypeStruct((-(-rows // SUB) * SUB, LANES), F32)

    @property
    def frame(self):
        return jax.ShapeDtypeStruct((self.rows, LANES), F32)


def zero(ref):
    ref[...] = jnp.zeros(ref.shape, ref.dtype)


def call(kernel, out_shape, ins, in_specs=None, scratch=()):
    vm = pl.BlockSpec(memory_space=pltpu.VMEM)
    specs = in_specs or [None] * len(ins)
    return pl.pallas_call(
        kernel,
        out_shape=out_shape,
        in_specs=[s or vm for s in specs],
        out_specs=jax.tree.map(lambda _: vm, out_shape),
        scratch_shapes=list(scratch),
        compiler_params=pltpu.CompilerParams(vmem_limit_bytes=VMEM_LIMIT),
    )(*ins)


SMEM = pl.BlockSpec(memory_space=pltpu.SMEM)
HBM = pl.BlockSpec(memory_space=pl.ANY)


def static_y(fr, core_k, core_f, core_w, xl, xr, k0, f0, w0, up, down):
    for ref in (k0, f0, w0, up, down):
        zero(ref)
    by, yf, w = fr.by, fr.yf, 2 * MARGIN + H

    def put(frame, plane, ref, row):
        for t in range(by // SUB):
            frame[pl.ds(plane * yf + TOP + t * SUB, SUB), :] = ref[pl.ds(row + t * SUB, SUB), :]

    def core(x, _):
        for frame, ref in ((k0, core_k), (f0, core_f), (w0, core_w)):
            put(frame, x + H, ref, x * by)
        return 0

    lax.fori_loop(0, fr.bx, core, 0)
    for i in range(H):
        put(k0, i, xl, i * by)
        put(k0, fr.bx + H + i, xr, i * by)
    for i in range(MARGIN):
        put(f0, i + 1, xl, (H + i) * by)
        put(w0, i + 1, xl, (H + MARGIN + i) * by)
        put(f0, fr.bx + H + i, xr, (H + i) * by)
        put(w0, fr.bx + H + i, xr, (H + MARGIN + i) * by)

    def plane(x, _):
        r, o = x * yf, x * w
        last = TOP + by
        for frame, n, at in ((k0, H, 0), (f0, MARGIN, H), (w0, MARGIN, H + MARGIN)):
            up[pl.ds(o + at, n), :] = frame[pl.ds(r + last - n, n), :]
            down[pl.ds(o + at, n), :] = frame[pl.ds(r + TOP, n), :]
        return 0

    lax.fori_loop(0, fr.xf, plane, 0)


def static_z(fr, info, k_in, f_in, w_in, yl, yr, k0, f0, w0, *slabs):
    sub, lane = iotas()
    by, yf, w = fr.by, fr.yf, 2 * MARGIN + H
    k0[...] = k_in[...]
    f0[...] = f_in[...]
    w0[...] = w_in[...]

    def plane(x, _):
        r, o = x * yf, x * w
        end = TOP + by
        for frame, n, at in ((k0, H, 0), (f0, MARGIN, H), (w0, MARGIN, H + MARGIN)):
            frame[pl.ds(r + TOP - n, n), :] = yl[pl.ds(o + at, n), :]
            frame[pl.ds(r + end, n), :] = yr[pl.ds(o + at, n), :]
        return 0

    lax.fori_loop(0, fr.xf, plane, 0)
    group = lane & 15

    def block(b, _):
        for i, slab in enumerate(slabs):
            upward = info[1] == 0 if fr.sides == 1 else i == 0
            shifts = [pick(upward, a, z) for a, z in ((H, 0), (2 * MARGIN + 1, H), (3 * MARGIN + 1, 2 * MARGIN + 1))]
            packs = []
            for frame, shift in zip((k0, f0, w0), shifts):
                tiles = [frame[pl.ds((b * GROUP + j) * SUB, SUB), :] for j in range(GROUP)]
                packs.append(pack_tiles(tiles, shift, lane))
            mix = jnp.where(group < H, packs[0], jnp.where(group < H + MARGIN, packs[1], packs[2]))
            slab[pl.ds(b * SUB, SUB), :] = mix
        return 0

    lax.fori_loop(0, fr.rows // (GROUP * SUB), block, 0)


def from_z(fr, info, received):
    if fr.sides == 1:
        return [(received[0], info[1] == 1)]
    return [(received[0], True), (received[1], False)]


def pick(flag, a, b):
    if isinstance(flag, bool):
        return a if flag else b
    return jnp.where(flag, a, b)


def place_masks(z0, lane):
    main = (lane >= z0) & (lane < z0 + PIECE)
    beyond = jnp.where(lane < LANES // 2, lane + LANES, lane - LANES)
    return main, (beyond >= z0) & (beyond < z0 + PIECE)


def corner(off, p):
    return off[p * 3] + 1, off[p * 3 + 1] + TOP - MARGIN, off[p * 3 + 2] - MARGIN


def prolong(fr, nb, info, off, link, table, bases, p0, p1, *rest):
    slabs, (buf, sem) = rest[: fr.sides], rest[fr.sides :]
    sub, lane = iotas()
    live = info[0]

    def start(p, _):
        pltpu.make_async_copy(bases.at[p], buf.at[p], sem.at[p]).start()
        return 0

    lax.fori_loop(0, live, start, 0)
    zero(p0)
    zero(p1)

    def piece(p, _):
        pltpu.make_async_copy(bases.at[p], buf.at[p], sem.at[p]).wait()
        at = p * 4
        row = table[(link[at] * 3 + link[at + 1]) * 3 + link[at + 2]]
        slot = lax.broadcasted_iota(jnp.int32, row.shape, 1)
        coef = jnp.sum(jnp.where(slot == link[at + 3], row, 0.0), axis=1, keepdims=True)
        coef = jnp.broadcast_to(coef, (nb, LANES))
        x0, y0, z0 = corner(off, p)
        base = x0 * fr.yf + y0
        values = []
        for first in range(0, PIECE * HALVES, SUB):
            parts = [buf[p, :, c * LANES : (c + 1) * LANES] * coef for c in range(first, first + SUB)]
            rows = block_transpose(sum_rows(parts, sub), sub, lane)
            values += [pltpu.roll(rows, (z0 - PIECE * j + 2 * LANES) % LANES, 1) for j in range(SUB)]
        main, beyond = place_masks(z0, lane)
        places = [pl.ds(base + (c // HALVES) * fr.yf + (c % HALVES) * SUB, SUB) for c in range(len(values))]
        new = [p0[a, :] + jnp.where(main, v, 0.0) for a, v in zip(places, values)]
        for a, v in zip(places, new):
            p0[a, :] = v

        @pl.when((z0 < 0) | (z0 + PIECE > LANES))
        def _():
            new = [p1[a, :] + jnp.where(beyond, v, 0.0) for a, v in zip(places, values)]
            for a, v in zip(places, new):
                p1[a, :] = v

        return 0

    lax.fori_loop(0, live, piece, 0)

    def block(b, _):
        tiles = []
        for j in range(GROUP):
            at = pl.ds(fr.yf + (b * GROUP + j) * SUB, SUB)
            tiles.append((p0[at, :], p1[at, :]))
        for i, slab in enumerate(slabs):
            upward = info[1] == 0 if fr.sides == 1 else i == 0
            near = [jnp.where(lane >= LANES // 2, pick(upward, x, y), pick(upward, y, x)) for x, y in tiles]
            slab[pl.ds(b * SUB, SUB), :] = pack_tiles(near, SUB, lane)
        return 0

    lax.fori_loop(0, fr.live_x * fr.tiles // GROUP, block, 0)


def coarse_y(fr, info, p0_in, p1_in, *rest):
    received, (p0, p1, up, down) = rest[: fr.sides], rest[fr.sides :]
    sub, lane = iotas()
    p0[...] = p0_in[...]
    p1[...] = p1_in[...]
    n = 2 * MARGIN + 1
    packed = fr.live_x * n

    def block(b, _):
        for buf, before in from_z(fr, info, received):
            packed = buf[pl.ds(b * SUB, SUB), :]
            for j in range(GROUP):
                at = pl.ds(fr.yf + (b * GROUP + j) * SUB, SUB)
                v = unpack_tile(packed, j, LANES - SUB)
                high = jnp.where(lane >= LANES - SUB, v, 0.0)
                low = jnp.where(lane < SUB, v, 0.0)
                p1[at, :] = p1[at, :] + pick(before, high, low)
                p0[at, :] = p0[at, :] + pick(before, low, high)
        return 0

    lax.fori_loop(0, fr.live_x * fr.tiles // GROUP, block, 0)

    def plane(x, _):
        r = (x + 1) * fr.yf
        up[pl.ds(x * n, n), :] = p0[pl.ds(r + TOP + fr.by - H, n), :]
        down[pl.ds(x * n, n), :] = p0[pl.ds(r + TOP - MARGIN, n), :]
        return 0

    lax.fori_loop(0, fr.live_x, plane, 0)

    def margin(b, _):
        for slab, first in ((up, fr.tiles - 2), (down, 0)):
            tiles = []
            for j in range(GROUP):
                row = (b * (GROUP // 2) + j // 2 + 1) * fr.yf + (first + j % 2) * SUB
                tiles.append(p1[pl.ds(row, SUB), :])
            slab[pl.ds(packed + b * SUB, SUB), :] = pack_tiles(tiles, SUB, lane)
        return 0

    lax.fori_loop(0, fr.live_x * 2 // GROUP, margin, 0)


def coarse_x(fr, p0_in, p1_in, yl, yr, p0, p1, up, down):
    sub, lane = iotas()
    p0[...] = p0_in[...]
    p1[...] = p1_in[...]
    n = 2 * MARGIN + 1
    packed = fr.live_x * n
    edge = (lane >= 120) | (lane < 8)

    def plane(x, _):
        r = (x + 1) * fr.yf
        for buf, row, first in ((yl, TOP - H, 0), (yr, TOP + fr.by - MARGIN, fr.tiles - 2)):
            at = pl.ds(r + row, n)
            p0[at, :] = p0[at, :] + buf[pl.ds(x * n, n), :]
        return 0

    lax.fori_loop(0, fr.live_x, plane, 0)

    def margin(b, _):
        for buf, first in ((yl, 0), (yr, fr.tiles - 2)):
            pack = buf[pl.ds(packed + b * SUB, SUB), :]
            for j in range(GROUP):
                at = pl.ds((b * (GROUP // 2) + j // 2 + 1) * fr.yf + (first + j % 2) * SUB, SUB)
                p1[at, :] = p1[at, :] + jnp.where(edge, unpack_tile(pack, j, LANES - SUB), 0.0)
        return 0

    lax.fori_loop(0, fr.live_x * 2 // GROUP, margin, 0)
    main = n * fr.yf
    for slab, first in ((up, fr.xf - 1 - n), (down, 1)):
        slab[0:main, :] = p0[first * fr.yf : (first + n) * fr.yf, :]
        for b in range(-(-n * fr.tiles // GROUP)):
            row = first * fr.yf + b * GROUP * SUB
            tiles = [p1[row + j * SUB : row + (j + 1) * SUB, :] for j in range(GROUP)]
            slab[main + b * SUB : main + (b + 1) * SUB, :] = pack_tiles(tiles, SUB, lane)


def enrich(fr, info, off, p0, p1, xl, xr, k0, f0, w0, *rest):
    received, rest = rest[: fr.sides], rest[fr.sides :]
    core, basis, q0, q1, slab = rest[:5]
    c0, c1, k1, r0, r1, w1, kb, rb, wb, wt, base, va, vb = rest[5:]
    sub, lane = iotas()
    yf, tiles = fr.yf, fr.tiles
    live = info[0]
    n = 2 * MARGIN + 1
    main_rows = n * yf
    edge = (lane >= 120) | (lane < 8)

    c0[...] = p0[...]
    c1[...] = p1[...]
    for buf, first in ((xl, 0), (xr, fr.xf - n)):
        a = slice(first * yf, (first + n) * yf)
        c0[a, :] = c0[a, :] + buf[0:main_rows, :]
        for i in range(n * tiles):
            at = slice(first * yf + i * SUB, first * yf + (i + 1) * SUB)
            row = main_rows + i // GROUP * SUB
            v = unpack_tile(buf[row : row + SUB, :], i % GROUP, LANES - SUB)
            c1[at, :] = c1[at, :] + jnp.where(edge, v, 0.0)

    f1 = r1

    def beyond_z(b, _):
        for j in range(GROUP):
            at = pl.ds((b * GROUP + j) * SUB, SUB)
            sums = [0.0, 0.0, 0.0]
            for buf, before in from_z(fr, info, received):
                pack = buf[pl.ds(b * SUB, SUB), :]
                for i, (start, width) in enumerate(((0, H), (H, MARGIN), (H + MARGIN, MARGIN))):
                    v = unpack_tile(pack, j, pick(before, LANES - width - start, LANES - start))
                    low = pick(before, LANES - width, 0)
                    keep = (lane >= low) & (lane < low + width)
                    sums[i] = sums[i] + jnp.where(keep, v, 0.0)
            k1[at, :] = sums[0]
            f1[at, :] = sums[1]
            w1[at, :] = sums[2]
            c0[at, :] = jnp.where(k0[at, :] > 0, c0[at, :], 0.0)
            c1[at, :] = jnp.where(sums[0] > 0, c1[at, :], 0.0)
        return 0

    lax.fori_loop(0, fr.rows // (GROUP * SUB), beyond_z, 0)

    def next_z(a, b):
        return pltpu.roll(jnp.where(lane == 0, b, a), LANES - 1, 1)

    def last_z(a, b):
        return pltpu.roll(jnp.where(lane == LANES - 1, b, a), 1, 1)

    def residual(x, _):
        r = (x + 1) * yf
        for t in range(tiles):
            at = pl.ds(r + t * SUB, SUB)
            for c, k, f, oc, ok, out in ((c0, k0, f0, c1, k1, r0), (c1, k1, f1, c0, k0, r1)):
                cc, kc = c[at, :], k[at, :]
                total = jnp.zeros((SUB, LANES), F32)
                beside = [
                    (c[pl.ds(r + t * SUB + d, SUB), :], k[pl.ds(r + t * SUB + d, SUB), :])
                    for d in (-yf, yf, -1, 1)
                ]
                beside += [(next_z(cc, oc[at, :]), next_z(kc, ok[at, :]))]
                beside += [(last_z(cc, oc[at, :]), last_z(kc, ok[at, :]))]
                for cn, kn in beside:
                    total = total + jnp.where(kn > 0, 0.5 * (kc + kn), kc) * (cc - cn)
                out[at, :] = jnp.where(kc > 0, f[at, :] - total, 0.0)
        return 0

    lax.fori_loop(0, fr.live_x, residual, 0)

    def copy_core(x, _):
        for t in range(fr.by // SUB):
            core[pl.ds(x * fr.by + t * SUB, SUB), :] = c0[pl.ds((x + H) * yf + TOP + t * SUB, SUB), :]
        return 0

    lax.fori_loop(0, fr.bx, copy_core, 0)

    zero(basis)
    zero(q0)
    zero(q1)
    for ref in (kb, va, vb):
        zero(ref)

    first_y, last_y = sub == 0, sub == SUB - 1
    z_in = lane & (PIECE - 1)

    def tent(t):
        return (t + 0.5) * (PIECE - t - 0.5) * (4.0 / (PIECE * PIECE))

    def one_group(group, _):
        first = group * GROUP
        bases, shifts, spans, slots = [], [], [], []
        for g in range(GROUP):
            x0, y0, z0 = corner(off, first + g)
            bases.append(x0 * yf + y0)
            shifts.append((g * PIECE - z0 + LANES) % LANES)
            spans.append(z0)
            slots.append(jnp.where(first + g < live, g, -1))

        def gather(x, _):
            for h in range(HALVES):
                accs = [jnp.zeros((SUB, LANES), F32) for _ in range(3)]
                for g in range(GROUP):
                    at = pl.ds(bases[g] + x * yf + h * SUB, SUB)
                    main = (lane >= spans[g]) & (lane < spans[g] + PIECE)
                    keep = (lane >> 4) == slots[g]
                    for j, (a, b) in enumerate(((k0, k1), (r0, r1), (w0, w1))):
                        v = pltpu.roll(jnp.where(main, a[at, :], b[at, :]), shifts[g], 1)
                        accs[j] = jnp.where(keep, v, accs[j])
                r = x * PIECE + h * SUB
                kb[pl.ds(PIECE + r, SUB), :] = accs[0]
                rb[pl.ds(r, SUB), :] = accs[1]
                wb[pl.ds(r, SUB), :] = accs[2]
            return 0

        lax.fori_loop(0, PIECE, gather, 0)

        def setup(x, _):
            for h in range(HALVES):
                r = x * PIECE + h * SUB
                kc = kb[pl.ds(PIECE + r, SUB), :]
                kn = [kb[pl.ds(PIECE + r + d, SUB), :] for d in (PIECE, -PIECE, 1, -1)]
                kn += [pltpu.roll(kc, LANES - 1, 1), pltpu.roll(kc, 1, 1)]
                if h == HALVES - 1:
                    kn[2] = jnp.where(last_y, 0.0, kn[2])
                if h == 0:
                    kn[3] = jnp.where(first_y, 0.0, kn[3])
                kn[4] = jnp.where(z_in == PIECE - 1, 0.0, kn[4])
                kn[5] = jnp.where(z_in == 0, 0.0, kn[5])
                faces, diag = [], jnp.zeros((SUB, LANES), F32)
                for k in kn:
                    there = k > 0
                    half = 0.5 * (kc + k)
                    faces.append(jnp.where(there, half, 0.0))
                    diag = diag + jnp.where(there, half, kc)
                inside = kc > 0
                scale = jnp.where(inside, DAMPING / jnp.where(inside, diag, 1.0), 0.0)
                for j, face in enumerate(faces):
                    wt[j, pl.ds(r, SUB), :] = face * scale
                s = rb[pl.ds(r, SUB), :] * scale
                s2 = s * wb[pl.ds(r, SUB), :]
                base[0, pl.ds(r, SUB), :] = s
                base[1, pl.ds(r, SUB), :] = s2
                va[0, pl.ds(PIECE + r, SUB), :] = s
                va[1, pl.ds(PIECE + r, SUB), :] = s2
            return 0

        lax.fori_loop(0, PIECE, setup, 0)

        def sweep(src, dst):
            for x in range(PIECE):
                for h in range(HALVES):
                    r = x * PIECE + h * SUB
                    a = PIECE + r
                    w = [wt[j, r : r + SUB, :] for j in range(6)]
                    for s in range(2):
                        v = src[s, a : a + SUB, :]
                        total = base[s, r : r + SUB, :] + v * (1.0 - DAMPING)
                        if x < PIECE - 1:
                            total = total + w[0] * src[s, a + PIECE : a + PIECE + SUB, :]
                        if x > 0:
                            total = total + w[1] * src[s, a - PIECE : a - PIECE + SUB, :]
                        total = total + w[2] * src[s, a + 1 : a + 1 + SUB, :]
                        total = total + w[3] * src[s, a - 1 : a - 1 + SUB, :]
                        total = total + w[4] * pltpu.roll(v, LANES - 1, 1)
                        total = total + w[5] * pltpu.roll(v, 1, 1)
                        dst[s, a : a + SUB, :] = total

        def two(i, _):
            sweep(va, vb)
            sweep(vb, va)
            return 0

        lax.fori_loop(0, (SWEEPS - 1) // 2, two, 0)
        if (SWEEPS - 1) % 2:
            sweep(va, vb)
            done = vb
        else:
            done = va

        ty = [tent(sub.astype(F32) + float(SUB * h)) for h in range(HALVES)]
        tz = tent(z_in.astype(F32))
        for c in range(PIECE * HALVES):
            r = c * SUB
            v0, v1 = done[0, PIECE + r : PIECE + r + SUB, :], done[1, PIECE + r : PIECE + r + SUB, :]
            weight = ty[c % HALVES] * tz * float(tent(c // HALVES))
            rb[r : r + SUB, :] = (v0 + v1) * weight
            for s, v in enumerate((v0, v1)):
                at = first * PIECE * HALVES * 2 + c * 2 + s
                basis[pl.ds(at, GROUP, stride=PIECE * HALVES * 2), :] = block_transpose(v, sub, lane)

        def spread(g, _):
            x0, y0, z0 = corner(off, first + g)
            origin = x0 * yf + y0
            shift = (z0 - g * PIECE + 2 * LANES) % LANES
            values = [pltpu.roll(rb[c * SUB : (c + 1) * SUB, :], shift, 1) for c in range(PIECE * HALVES)]
            main, beyond = place_masks(z0, lane)
            places = [pl.ds(origin + (c // HALVES) * yf + (c % HALVES) * SUB, SUB) for c in range(len(values))]
            new = [q0[a, :] + jnp.where(main, v, 0.0) for a, v in zip(places, values)]
            for a, v in zip(places, new):
                q0[a, :] = v

            @pl.when((z0 < 0) | (z0 + PIECE > LANES))
            def _():
                new = [q1[a, :] + jnp.where(beyond, v, 0.0) for a, v in zip(places, values)]
                for a, v in zip(places, new):
                    q1[a, :] = v

            return 0

        lax.fori_loop(0, jnp.minimum(live - first, GROUP), spread, 0)
        return 0

    lax.fori_loop(0, (live + GROUP - 1) // GROUP, one_group, 0)

    def block(b, _):
        tiles = [q1[pl.ds(yf + (b * GROUP + j) * SUB, SUB), :] for j in range(GROUP)]
        slab[pl.ds(b * SUB, SUB), :] = pack_tiles(tiles, SUB, lane)
        return 0

    lax.fori_loop(0, fr.live_x * tiles // GROUP, block, 0)


def z_part(fr, info, received, x, t, lane):
    total = 0.0
    for buf, before in from_z(fr, info, received):
        i = x * fr.tiles + t
        v = unpack_tile(buf[pl.ds(i // GROUP * SUB, SUB), :], i % GROUP, LANES - SUB)
        keep = pick(before, jnp.where(lane < 8, 1, 0), jnp.where(lane >= 120, 1, 0))
        total = total + jnp.where(keep > 0, v, 0.0)
    return total


def fold_y(fr, info, q0, *rest):
    received, (up, down, tmp) = rest[: fr.sides], rest[fr.sides :]
    _, lane = iotas()

    def plane(x, _):
        r = (x + 1) * fr.yf
        for slab, t, a in ((up, fr.tiles - 1, 0), (down, 0, MARGIN)):
            at = r + t * SUB
            tmp[...] = q0[pl.ds(at, SUB), :] + z_part(fr, info, received, x, t, lane)
            slab[pl.ds(x * MARGIN, MARGIN), :] = tmp[a : a + MARGIN, :]
        return 0

    lax.fori_loop(0, fr.live_x, plane, 0)


def core_plane(fr, info, q0, received, yl, yr, x, lane):
    out = []
    for t in range(fr.by // SUB):
        tile = q0[pl.ds((x + 1) * fr.yf + TOP + t * SUB, SUB), :]
        out.append(tile + z_part(fr, info, received, x, t + 1, lane))
    return out


def fold_x(fr, info, q0, *rest):
    received, (yl, yr, up, down) = rest[: fr.sides], rest[fr.sides :]
    _, lane = iotas()
    by = fr.by
    for slab, first in ((up, fr.live_x - MARGIN), (down, 0)):
        for i in range(MARGIN):
            x = first + i
            for t, tile in enumerate(core_plane(fr, info, q0, received, yl, yr, x, lane)):
                slab[i * by + t * SUB : i * by + (t + 1) * SUB, :] = tile
            a = slice(i * by, i * by + MARGIN)
            slab[a, :] = slab[a, :] + yl[x * MARGIN : (x + 1) * MARGIN, :]
            a = slice((i + 1) * by - MARGIN, (i + 1) * by)
            slab[a, :] = slab[a, :] + yr[x * MARGIN : (x + 1) * MARGIN, :]


def finish(fr, info, core, q0, *rest):
    received, (yl, yr, xl, xr, out) = rest[: fr.sides], rest[fr.sides :]
    _, lane = iotas()
    by = fr.by

    def plane(i, _):
        x = i + MARGIN
        for t, tile in enumerate(core_plane(fr, info, q0, received, yl, yr, x, lane)):
            at = pl.ds(i * by + t * SUB, SUB)
            out[at, :] = core[at, :] + tile
        a = pl.ds(i * by, MARGIN)
        out[a, :] = out[a, :] + yl[pl.ds(x * MARGIN, MARGIN), :]
        a = pl.ds(i * by + by - MARGIN, MARGIN)
        out[a, :] = out[a, :] + yr[pl.ds(x * MARGIN, MARGIN), :]
        return 0

    lax.fori_loop(0, fr.bx, plane, 0)
    n = MARGIN * by
    out[0:n, :] = out[0:n, :] + xl[...]
    a = slice((fr.bx - MARGIN) * by, fr.bx * by)
    out[a, :] = out[a, :] + xr[...]


def swap(axis, up, down):
    count = lax.axis_size(axis)
    pairs = [(i, i + 1) for i in range(count - 1)]
    return lax.ppermute(up, axis, pairs), lax.ppermute(down, axis, [(j, i) for i, j in pairs])


def swap_z(fr, slabs):
    if fr.sides == 1:
        return [lax.ppermute(slabs[0], "gz", [(0, 1), (1, 0)])]
    return list(swap("gz", slabs[0], slabs[1]))


def lookup(labels, values):
    accumulated = jnp.zeros(labels.shape, values.dtype)
    for channel in range(values.shape[0]):
        accumulated = accumulated + jnp.where(labels == channel, values[channel], 0.0)
    return accumulated


def local(
    forcing,
    kappa_base,
    labels,
    contrast,
    channel_weight,
    coarse_coef,
    source_link,
    offsets,
    live_pieces,
    resident_bases,
):
    bx, by, bz = forcing.shape
    fr = Frame(bx, by, bz, lax.axis_size("gz"))
    slots, nb = resident_bases.shape[3], resident_bases.shape[4]
    nd = coarse_coef.shape[3]
    cells = PIECE**3
    part = functools.partial

    info = jnp.stack([live_pieces[0, 0, 0], lax.axis_index("gz").astype(jnp.int32)])
    off = offsets.reshape(slots * 3)
    link = source_link.reshape(slots * 4)
    bases = resident_bases.reshape(slots, nb, cells)

    table = jnp.swapaxes(coarse_coef.reshape(nd, nb), 0, 1)[None]
    if fr.sides == 1:
        other = lax.ppermute(table, "gz", [(0, 1), (1, 0)])
        before, after = other, other
    else:
        before, after = swap("gz", table, table)
    table = jnp.concatenate([before, table, after], 0)
    for axis in ("gy", "gx"):
        before, after = swap(axis, table, table)
        table = jnp.concatenate([before, table, after], 0)

    kappa = kappa_base * lookup(labels, contrast)
    weight = lookup(labels, channel_weight)
    up = jnp.concatenate([kappa[-H:], forcing[-MARGIN:], weight[-MARGIN:]], 0)
    down = jnp.concatenate([kappa[:H], forcing[:MARGIN], weight[:MARGIN]], 0)
    xl, xr = swap("gx", up.reshape(-1, bz), down.reshape(-1, bz))
    frames = [fr.frame] * 3
    flat = [a.reshape(bx * by, bz) for a in (kappa, forcing, weight)]
    y_slab = fr.arr(fr.xf * (2 * MARGIN + H))
    k0, f0, w0, up, down = call(part(static_y, fr), frames + [y_slab] * 2, [*flat, xl, xr])
    yl, yr = swap("gy", up, down)
    z_slab = fr.arr(fr.rows // SUB)
    k0, f0, w0, *slabs = call(
        part(static_z, fr),
        frames + [z_slab] * fr.sides,
        [info, k0, f0, w0, yl, yr],
        [SMEM] + [None] * 5,
    )
    static_beyond = swap_z(fr, slabs)

    z_slab = fr.arr(fr.live_x * fr.tiles)
    p0, p1, *slabs = call(
        part(prolong, fr, nb),
        [fr.frame] * 2 + [z_slab] * fr.sides,
        [info, off, link, table, bases],
        [SMEM, SMEM, SMEM, None, HBM],
        [pltpu.VMEM((slots, nb, cells), F32), pltpu.SemaphoreType.DMA((slots,))],
    )
    beyond = swap_z(fr, slabs)
    y_slab = fr.arr(fr.live_x * (2 * MARGIN + 1 + 2))
    p0, p1, up, down = call(
        part(coarse_y, fr),
        [fr.frame] * 2 + [y_slab] * 2,
        [info, p0, p1, *beyond],
        [SMEM] + [None] * (2 + fr.sides),
    )
    yl, yr = swap("gy", up, down)
    x_slab = fr.arr((2 * MARGIN + 1) * (fr.yf + fr.tiles) + SUB)
    p0, p1, up, down = call(part(coarse_x, fr), [fr.frame] * 2 + [x_slab] * 2, [p0, p1, yl, yr])
    xl, xr = swap("gx", up, down)

    frame = pltpu.VMEM((fr.rows, LANES), F32)
    padded = PROWS + 2 * PIECE
    core, basis, q0, q1, slab = call(
        part(enrich, fr),
        [fr.arr(bx * by), fr.arr(slots * PIECE * HALVES * 2)] + [fr.frame] * 2 + [z_slab],
        [info, off, p0, p1, xl, xr, k0, f0, w0, *static_beyond],
        [SMEM] * 2 + [None] * (7 + fr.sides),
        [frame] * 6
        + [
            pltpu.VMEM((padded, LANES), F32),
            pltpu.VMEM((PROWS, LANES), F32),
            pltpu.VMEM((PROWS, LANES), F32),
            pltpu.VMEM((6, PROWS, LANES), F32),
            pltpu.VMEM((2, PROWS, LANES), F32),
            pltpu.VMEM((2, padded, LANES), F32),
            pltpu.VMEM((2, padded, LANES), F32),
        ],
    )

    beyond = swap_z(fr, [slab] * fr.sides)
    y_slab = fr.arr(fr.live_x * MARGIN)
    up, down = call(
        part(fold_y, fr),
        [y_slab] * 2,
        [info, q0, *beyond],
        [SMEM] + [None] * (1 + fr.sides),
        [pltpu.VMEM((SUB, LANES), F32)],
    )
    yl, yr = swap("gy", up, down)
    x_slab = fr.arr(MARGIN * by)
    up, down = call(
        part(fold_x, fr),
        [x_slab] * 2,
        [info, q0, *beyond, yl, yr],
        [SMEM] + [None] * (3 + fr.sides),
    )
    xl, xr = swap("gx", up, down)
    update = call(
        part(finish, fr),
        fr.arr(bx * by),
        [info, core, q0, *beyond, yl, yr, xl, xr],
        [SMEM] + [None] * (6 + fr.sides),
    )
    new_basis = basis.reshape(slots, PIECE * HALVES, 2, LANES).swapaxes(1, 2)
    return update.reshape(bx, by, bz), new_basis.reshape(1, 1, 1, slots, 2, cells)


def solution(mesh):
    brick = ("gx", "gy", "gz")
    return jax.shard_map(
        local,
        mesh=mesh,
        in_specs=(
            P(*brick),
            P(*brick),
            P(*brick),
            P(),
            P(),
            P(*brick, None, None),
            P(*brick, None, None),
            P(*brick, None, None),
            P(*brick),
            P(*brick, None, None, None),
        ),
        out_specs=(P(*brick), P(*brick, None, None, None)),
        check_vma=False,
    )
```

```python
import functools

import jax
import jax.numpy as jnp
from jax import lax
from jax.experimental import pallas as pl
from jax.experimental.pallas import tpu as pltpu
from jax.sharding import PartitionSpec as P

MARGIN = 4
PIECE = 16
SWEEPS = 20
DAMPING = 2.0 / 3.0

H = MARGIN + 1
WIDE = 2 * MARGIN + 1
LANES = 128
SUB = 8
TOP = 8
GROUP = LANES // PIECE
HALVES = PIECE // SUB
CHUNKS = PIECE * HALVES
PROWS = PIECE * PIECE
F32 = jnp.float32


def iotas():
    shape = (SUB, LANES)
    return lax.broadcasted_iota(jnp.int32, shape, 0), lax.broadcasted_iota(jnp.int32, shape, 1)


def loop(count, body, unroll=1):
    while count % unroll:
        unroll -= 1

    def step(i, _):
        for j in range(unroll):
            body(i * unroll + j)
        return 0

    lax.fori_loop(0, count // unroll, step, 0)


def pick(flag, a, b):
    return jnp.where(flag, a, b)


def pack_tiles(tiles, shift, lane):
    packed = jnp.zeros((SUB, LANES), F32)
    for j, tile in enumerate(tiles):
        packed = jnp.where((lane >> 4) == j, pltpu.roll(tile, (shift + PIECE * j) % LANES, 1), packed)
    return packed


def unpack_tile(packed, j, shift):
    return pltpu.roll(packed, (shift - PIECE * j + 2 * LANES) % LANES, 1)


def sum_rows(values, sub):
    for k in (1, 2, 4):
        low = (sub & k) == 0
        values = [
            jnp.where(low, a, b) + pltpu.roll(jnp.where(low, b, a), SUB - k, 0)
            for a, b in zip(values[0::2], values[1::2])
        ]
    return values[0]


def block_transpose(values, sub, lane):
    for k in (4, 2, 1):
        in_group = ((lane >> 4) & k) != 0
        in_sub = (sub & k) != 0
        moves = in_sub != in_group
        if k == 4:
            others = [pltpu.roll(v, 64, 1) for v in values]
            others = [pltpu.roll(v, 4, 0) for v in others]
        else:
            pairs = [(pltpu.roll(v, PIECE * k, 1), pltpu.roll(v, LANES - PIECE * k, 1)) for v in values]
            others = [jnp.where(in_group, q, p) for q, p in pairs]
            others = [jnp.where(in_sub, pltpu.roll(m, k, 0), pltpu.roll(m, SUB - k, 0)) for m in others]
        values = [jnp.where(moves, o, v) for o, v in zip(others, values)]
    return values


class Frame:
    def __init__(self, bx, by, bz, counts):
        self.bx, self.by, self.bz = bx, by, bz
        self.xf = bx + 2 * H
        self.yf = by + 2 * TOP
        self.tiles = self.yf // SUB
        self.blocks = -(-self.xf * self.tiles // GROUP)
        self.rows = self.blocks * GROUP * SUB
        self.live_x = bx + 2 * MARGIN
        self.live_blocks = self.live_x * self.tiles // GROUP
        self.sides = [1 if n == 2 else 2 for n in counts]

    @property
    def frame(self):
        return rows_of(self.rows)


def rows_of(count):
    return jax.ShapeDtypeStruct((-(-count // SUB) * SUB, LANES), F32)


def zero(ref):
    ref[...] = jnp.zeros(ref.shape, ref.dtype)


VMEM = pl.BlockSpec(memory_space=pltpu.VMEM)
SMEM = pl.BlockSpec(memory_space=pltpu.SMEM)
HBM = pl.BlockSpec(memory_space=pl.ANY)


def call(kernel, outs, ins, specs=(), scratch=(), alias=None, limit=12):
    specs = list(specs) + [VMEM] * (len(ins) - len(specs))
    return pl.pallas_call(
        kernel,
        out_shape=outs,
        in_specs=specs,
        out_specs=jax.tree.map(lambda _: VMEM, outs),
        scratch_shapes=list(scratch),
        input_output_aliases=alias or {},
        compiler_params=pltpu.CompilerParams(vmem_limit_bytes=limit * 1024 * 1024),
    )(*ins)


def is_lower(info, axis, phase):
    return ((info[1 + axis] + phase) & 1) == 0


def swap(axis, slabs):
    count = lax.axis_size(axis)
    received = []
    for phase, slab in enumerate(slabs):
        pairs = [(i, i + 1) for i in range(phase, count - 1, 2)]
        received.append(lax.ppermute(slab, axis, pairs + [(j, i) for i, j in pairs]))
    return received


def look_up(labels, values):
    out = jnp.zeros(labels.shape, F32)
    for c in range(values.shape[0]):
        out = out + jnp.where(labels == c, values[c], 0.0)
    return out


def static_x(fr, info, contrast, channel, kappa, labels, forcing, coef, *rest):
    n = fr.sides[0]
    slabs, (k_buf, l_buf, sem) = rest[:n], rest[n:]
    by = fr.by
    f_row, w_row, c_row = H * by, (H + MARGIN) * by, (H + 2 * MARGIN) * by
    copies = []
    for i, slab in enumerate(slabs):
        lower = is_lower(info, 0, i)
        first = pl.multiple_of(pick(lower, (fr.bx - H) * by, 0), SUB)
        four = pl.multiple_of(pick(lower, (fr.bx - MARGIN) * by, 0), SUB)
        for j, (src, dst) in enumerate(
            (
                (kappa.at[pl.ds(first, H * by)], k_buf.at[i]),
                (labels.at[pl.ds(first, H * by)], l_buf.at[i]),
                (forcing.at[pl.ds(four, MARGIN * by)], slab.at[pl.ds(f_row, MARGIN * by)]),
            )
        ):
            copies.append(pltpu.make_async_copy(src, dst, sem.at[i, j]))
    for copy in copies:
        copy.start()
    for slab in slabs:
        slab[c_row : c_row + SUB, :] = jnp.zeros((SUB, LANES), F32)
        slab[c_row : c_row + coef.shape[0], 0 : coef.shape[1]] = coef[...]
    for copy in copies:
        copy.wait()
    for i, slab in enumerate(slabs):
        skip = pl.multiple_of(pick(is_lower(info, 0, i), by, 0), SUB)
        slab[0:f_row, :] = k_buf[i] * look_up(l_buf[i], contrast)
        slab[w_row:c_row, :] = look_up(l_buf[i, pl.ds(skip, MARGIN * by), :], channel)


def static_y(fr, info, contrast, channel, kappa, labels, forcing, coef, *rest):
    n = fr.sides[0]
    received, (k0, f0, w0, coef3), slabs = rest[:n], rest[n : n + 4], rest[n + 4 :]
    by, yf, w = fr.by, fr.yf, 2 * MARGIN + H
    c_in = w * by
    for ref in (k0, f0, w0, coef3):
        zero(ref)

    def core(x):
        for t in range(by // SUB):
            src = pl.ds(x * by + t * SUB, SUB)
            dst = pl.ds((x + H) * yf + TOP + t * SUB, SUB)
            label = labels[src, :]
            k0[dst, :] = kappa[src, :] * look_up(label, contrast)
            w0[dst, :] = look_up(label, channel)
            f0[dst, :] = forcing[src, :]

    loop(fr.bx, core, 4)
    coef3[SUB : SUB + coef.shape[0], 0 : coef.shape[1]] = coef[...]
    for i, buf in enumerate(received):
        lower = is_lower(info, 0, i)
        for frame, count, at, low in ((k0, H, 0, 0), (f0, MARGIN, H, 1), (w0, MARGIN, H + MARGIN, 1)):
            first = pick(lower, fr.bx + H, low)
            for j in range(count):
                for t in range(by // SUB):
                    row = (at + j) * by + t * SUB
                    frame[pl.ds(pl.multiple_of((first + j) * yf + TOP + t * SUB, SUB), SUB), :] = buf[row : row + SUB, :]
        coef3[pl.ds(pl.multiple_of(pick(lower, 2 * SUB, 0), SUB), SUB), :] = buf[c_in : c_in + SUB, :]

    def plane(x):
        r, o = x * yf, x * w
        for i, slab in enumerate(slabs):
            lower = is_lower(info, 1, i)
            for frame, count, at in ((k0, H, 0), (f0, MARGIN, H), (w0, MARGIN, H + MARGIN)):
                first = r + pick(lower, TOP + by - count, TOP)
                slab[pl.ds(o + at, count), :] = frame[pl.ds(first, count), :]

    loop(fr.xf, plane, 6)
    c_out = -(-fr.xf * w // SUB) * SUB
    for slab in slabs:
        slab[c_out : c_out + 3 * SUB, :] = coef3[...]


def static_z(fr, info, k_in, f_in, w_in, coef3, *rest):
    n = fr.sides[1]
    received, (k0, f0, w0, coef9), slabs = rest[:n], rest[n : n + 4], rest[n + 4 :]
    del k_in, f_in, w_in
    _, lane = iotas()
    by, yf, w = fr.by, fr.yf, 2 * MARGIN + H
    c_in = -(-fr.xf * w // SUB) * SUB

    def plane(x):
        r, o = x * yf, x * w
        for i, buf in enumerate(received):
            lower = is_lower(info, 1, i)
            for frame, count, at in ((k0, H, 0), (f0, MARGIN, H), (w0, MARGIN, H + MARGIN)):
                first = r + pick(lower, TOP + by, TOP - count)
                frame[pl.ds(first, count), :] = buf[pl.ds(o + at, count), :]

    loop(fr.xf, plane, 6)
    zero(coef9)
    for x in range(3):
        coef9[(x * 3 + 1) * SUB : (x * 3 + 2) * SUB, :] = coef3[x * SUB : (x + 1) * SUB, :]
        for i, buf in enumerate(received):
            to = pl.multiple_of((x * 3 + pick(is_lower(info, 1, i), 2, 0)) * SUB, SUB)
            coef9[pl.ds(to, SUB), :] = buf[c_in + x * SUB : c_in + (x + 1) * SUB, :]
    group = lane & (PIECE - 1)

    def block(b):
        for i, slab in enumerate(slabs):
            lower = is_lower(info, 2, i)
            packs = []
            for frame, high, low in ((k0, H, 0), (f0, WIDE, H), (w0, WIDE + MARGIN, WIDE)):
                tiles = [frame[pl.ds((b * GROUP + j) * SUB, SUB), :] for j in range(GROUP)]
                packs.append(pack_tiles(tiles, pick(lower, high, low), lane))
            mix = jnp.where(group < H, packs[0], jnp.where(group < WIDE, packs[1], packs[2]))
            slab[pl.ds(b * SUB, SUB), :] = mix

    loop(fr.blocks, block, 4)
    c_out = fr.blocks * SUB
    for slab in slabs:
        slab[c_out : c_out + 9 * SUB, :] = coef9[...]


def place_masks(z0, lane):
    main = (lane >= z0) & (lane < z0 + PIECE)
    beyond = jnp.where(lane < LANES // 2, lane + LANES, lane - LANES)
    return main, (beyond >= z0) & (beyond < z0 + PIECE)


def corner(off, p):
    return off[0, p] + 1, off[1, p] + TOP - MARGIN, off[2, p] - MARGIN


def add_piece(fr, off, p, valid, values, lane, main_ref, beyond_ref):
    x0, y0, z0 = corner(off, p)
    base = x0 * fr.yf + y0
    main, beyond = place_masks(z0, lane)
    places = [pl.ds(base + (c // HALVES) * fr.yf + (c % HALVES) * SUB, SUB) for c in range(CHUNKS)]
    main = main & valid
    new = [main_ref[a, :] + jnp.where(main, v, 0.0) for a, v in zip(places, values)]
    for a, v in zip(places, new):
        main_ref[a, :] = v

    @pl.when(valid & ((z0 < 0) | (z0 + PIECE > LANES)))
    def _():
        new = [beyond_ref[a, :] + jnp.where(beyond, v, 0.0) for a, v in zip(places, values)]
        for a, v in zip(places, new):
            beyond_ref[a, :] = v


def prolong(fr, shape, info, off, link, bases, coef9, *rest):
    slots, nb, together = shape
    n = fr.sides[2]
    received, (p0, p1), slabs, (table, buf, sem) = rest[:n], rest[n : n + 2], rest[n + 2 : 2 * n + 2], rest[2 * n + 2 :]
    sub, lane = iotas()
    live = info[0]

    def start(p, _):
        pltpu.make_async_copy(bases.at[p], buf.at[p], sem.at[p]).start()
        return 0

    lax.fori_loop(0, live, start, 0)
    zero(p0)
    zero(p1)
    for xy in range(9):
        table[xy * 3 + 1] = coef9[xy * SUB : (xy + 1) * SUB, :]
        for i, part in enumerate(received):
            at = (fr.blocks + xy) * SUB
            table[xy * 3 + pick(is_lower(info, 2, i), 2, 0)] = part[at : at + SUB, :]

    def some(step, _):
        numbers, valids, spread = [], [], []
        for i in range(together):
            p = step * together + i
            valids.append(p < live)
            numbers.append(p)

            @pl.when(p < live)
            def _():
                pltpu.make_async_copy(bases.at[p], buf.at[p], sem.at[p]).wait()

        for p in numbers:
            row = table[(link[0, p] * 3 + link[1, p]) * 3 + link[2, p]]
            coef = jnp.sum(jnp.where(lane == link[3, p], row, 0.0), axis=1, keepdims=True)
            coef = jnp.broadcast_to(coef, (SUB, LANES))[0:nb]
            for first in range(0, CHUNKS, SUB):
                parts = [buf[p, :, c * LANES : (c + 1) * LANES] * coef for c in range(first, first + SUB)]
                spread.append(sum_rows(parts, sub))
        spread = block_transpose(spread, sub, lane)
        per = CHUNKS // SUB
        for i, (p, valid) in enumerate(zip(numbers, valids)):
            z0 = off[2, p] - MARGIN
            values = [
                pltpu.roll(rows, (z0 - PIECE * j + 2 * LANES) % LANES, 1)
                for rows in spread[i * per : (i + 1) * per]
                for j in range(SUB)
            ]
            add_piece(fr, off, p, valid, values, lane, p0, p1)
        return 0

    lax.fori_loop(0, (live + together - 1) // together, some, 0)

    def block(b):
        tiles = []
        for j in range(GROUP):
            at = pl.ds(fr.yf + (b * GROUP + j) * SUB, SUB)
            tiles.append((p0[at, :], p1[at, :]))
        for i, slab in enumerate(slabs):
            lower = is_lower(info, 2, i)
            main = (lane >= LANES // 2) == lower
            near = [jnp.where(main, x, y) for x, y in tiles]
            slab[pl.ds(b * SUB, SUB), :] = pack_tiles(near, SUB, lane)

    loop(fr.live_blocks, block, 3)


def coarse_y(fr, info, p0_in, p1_in, *rest):
    n = fr.sides[2]
    received, (p0, p1), slabs = rest[:n], rest[n : n + 2], rest[n + 2 :]
    del p0_in, p1_in
    _, lane = iotas()
    packed = fr.live_x * WIDE

    def block(b):
        for i, buf in enumerate(received):
            lower = is_lower(info, 2, i)
            pack = buf[pl.ds(b * SUB, SUB), :]
            places = [pl.ds(fr.yf + (b * GROUP + j) * SUB, SUB) for j in range(GROUP)]
            values = [unpack_tile(pack, j, LANES - SUB) for j in range(GROUP)]
            to_main = ((lane >= LANES - SUB) & lower) | ((lane < SUB) & jnp.logical_not(lower))
            to_beyond = ((lane >= LANES - SUB) & jnp.logical_not(lower)) | ((lane < SUB) & lower)
            main = [p0[a, :] + jnp.where(to_main, v, 0.0) for a, v in zip(places, values)]
            beyond = [p1[a, :] + jnp.where(to_beyond, v, 0.0) for a, v in zip(places, values)]
            for a, v0, v1 in zip(places, main, beyond):
                p0[a, :] = v0
                p1[a, :] = v1

    loop(fr.live_blocks, block, 3)

    def plane(x):
        r = (x + 1) * fr.yf
        for i, slab in enumerate(slabs):
            first = r + pick(is_lower(info, 1, i), TOP + fr.by - H, TOP - MARGIN)
            slab[pl.ds(x * WIDE, WIDE), :] = p0[pl.ds(first, WIDE), :]

    loop(fr.live_x, plane, 8)

    def margin(b):
        for i, slab in enumerate(slabs):
            first = pick(is_lower(info, 1, i), fr.tiles - 2, 0)
            tiles = []
            for j in range(GROUP):
                row = (b * (GROUP // 2) + j // 2 + 1) * fr.yf + (first + j % 2) * SUB
                tiles.append(p1[pl.ds(row, SUB), :])
            slab[pl.ds(packed + b * SUB, SUB), :] = pack_tiles(tiles, SUB, lane)

    loop(fr.live_x * 2 // GROUP, margin, 5)


def coarse_x(fr, info, p0_in, p1_in, *rest):
    n = fr.sides[1]
    received, (p0, p1), slabs = rest[:n], rest[n : n + 2], rest[n + 2 :]
    del p0_in, p1_in
    _, lane = iotas()
    packed = fr.live_x * WIDE
    edge = (lane >= LANES - SUB) | (lane < SUB)

    def plane(x):
        r = (x + 1) * fr.yf
        for i, buf in enumerate(received):
            at = pl.ds(r + pick(is_lower(info, 1, i), TOP + fr.by - MARGIN, TOP - H), WIDE)
            p0[at, :] = p0[at, :] + buf[pl.ds(x * WIDE, WIDE), :]

    loop(fr.live_x, plane, 8)

    def margin(b):
        for i, buf in enumerate(received):
            first = pick(is_lower(info, 1, i), fr.tiles - 2, 0)
            pack = buf[pl.ds(packed + b * SUB, SUB), :]
            places = [
                pl.ds((b * (GROUP // 2) + j // 2 + 1) * fr.yf + (first + j % 2) * SUB, SUB) for j in range(GROUP)
            ]
            values = [jnp.where(edge, unpack_tile(pack, j, LANES - SUB), 0.0) for j in range(GROUP)]
            values = [p1[a, :] + v for a, v in zip(places, values)]
            for a, v in zip(places, values):
                p1[a, :] = v

    loop(fr.live_x * 2 // GROUP, margin, 5)
    main = WIDE * fr.yf
    for i, slab in enumerate(slabs):
        row = pl.multiple_of(pick(is_lower(info, 0, i), fr.xf - 1 - WIDE, 1) * fr.yf, SUB)
        slab[0:main, :] = p0[pl.ds(row, main), :]
        for b in range(-(-WIDE * fr.tiles // GROUP)):
            tiles = [p1[pl.ds(row + (b * GROUP + j) * SUB, SUB), :] for j in range(GROUP)]
            slab[main + b * SUB : main + (b + 1) * SUB, :] = pack_tiles(tiles, SUB, lane)


def enrich(fr, info, off, p0, p1, k0, f0, w0, *rest):
    n0, n2 = fr.sides[0], fr.sides[2]
    x_in, z_in, rest = rest[:n0], rest[n0 : n0 + n2], rest[n0 + n2 :]
    core, basis, y_edge, x_edge, slab = rest[:5]
    c0, c1, k1, r0, r1, w1, q0, q1, kb, rb, wb, wt, base, va, vb = rest[5:]
    sub, lane = iotas()
    yf, tiles = fr.yf, fr.tiles
    live = info[0]
    main_rows = WIDE * yf
    edge = (lane >= LANES - SUB) | (lane < SUB)

    c0[...] = p0[...]
    c1[...] = p1[...]
    for i, buf in enumerate(x_in):
        row = pl.multiple_of(pick(is_lower(info, 0, i), fr.xf - WIDE, 0) * yf, SUB)
        a = pl.ds(row, main_rows)
        c0[a, :] = c0[a, :] + buf[0:main_rows, :]
        for b in range(-(-WIDE * tiles // GROUP)):
            pack = buf[main_rows + b * SUB : main_rows + (b + 1) * SUB, :]
            count = min(GROUP, WIDE * tiles - b * GROUP)
            places = [pl.ds(row + (b * GROUP + j) * SUB, SUB) for j in range(count)]
            values = [jnp.where(edge, unpack_tile(pack, j, LANES - SUB), 0.0) for j in range(count)]
            for a, v in zip(places, [c1[a, :] + v for a, v in zip(places, values)]):
                c1[a, :] = v

    f1 = r1

    def beyond_z(b):
        sums = [[0.0] * GROUP for _ in range(3)]
        for i, buf in enumerate(z_in):
            lower = is_lower(info, 2, i)
            pack = buf[pl.ds(b * SUB, SUB), :]
            for m, (start, width) in enumerate(((0, H), (H, MARGIN), (H + MARGIN, MARGIN))):
                shift = pick(lower, LANES - start, LANES - width - start)
                low = pick(lower, 0, LANES - width)
                keep = (lane >= low) & (lane < low + width)
                for j in range(GROUP):
                    sums[m][j] = sums[m][j] + jnp.where(keep, unpack_tile(pack, j, shift), 0.0)
        for j in range(GROUP):
            at = pl.ds((b * GROUP + j) * SUB, SUB)
            k1[at, :] = sums[0][j]
            f1[at, :] = sums[1][j]
            w1[at, :] = sums[2][j]
            c0[at, :] = jnp.where(k0[at, :] > 0, c0[at, :], 0.0)
            c1[at, :] = jnp.where(sums[0][j] > 0, c1[at, :], 0.0)

    loop(fr.blocks, beyond_z, 2)

    def next_z(a, b):
        return pltpu.roll(jnp.where(lane == 0, b, a), LANES - 1, 1)

    def last_z(a, b):
        return pltpu.roll(jnp.where(lane == LANES - 1, b, a), 1, 1)

    def residual(x):
        r = (x + 1) * yf
        for t in range(tiles):
            at = pl.ds(r + t * SUB, SUB)
            for c, k, f, oc, ok, out in ((c0, k0, f0, c1, k1, r0), (c1, k1, f1, c0, k0, r1)):
                cc, kc = c[at, :], k[at, :]
                total = jnp.zeros((SUB, LANES), F32)
                beside = [
                    (c[pl.ds(r + t * SUB + d, SUB), :], k[pl.ds(r + t * SUB + d, SUB), :])
                    for d in (-yf, yf, -1, 1)
                ]
                beside += [(next_z(cc, oc[at, :]), next_z(kc, ok[at, :]))]
                beside += [(last_z(cc, oc[at, :]), last_z(kc, ok[at, :]))]
                for cn, kn in beside:
                    total = total + jnp.where(kn > 0, 0.5 * (kc + kn), kc) * (cc - cn)
                out[at, :] = jnp.where(kc > 0, f[at, :] - total, 0.0)

    loop(fr.live_x, residual, 1)

    zero(q0)
    zero(q1)
    for ref in (kb, va, vb):
        zero(ref)

    first_y, last_y = sub == 0, sub == SUB - 1
    z_cell = lane & (PIECE - 1)

    def tent(t):
        return (t + 0.5) * (PIECE - t - 0.5) * (4.0 / (PIECE * PIECE))

    def one_group(group, _):
        first = group * GROUP
        bases, shifts, spans, slots = [], [], [], []
        for g in range(GROUP):
            x0, y0, z0 = corner(off, first + g)
            bases.append(x0 * yf + y0)
            shifts.append((g * PIECE - z0 + LANES) % LANES)
            spans.append(z0)
            slots.append(jnp.where(first + g < live, g, -1))

        def gather(x):
            for h in range(HALVES):
                accs = [jnp.zeros((SUB, LANES), F32) for _ in range(3)]
                for g in range(GROUP):
                    at = pl.ds(bases[g] + x * yf + h * SUB, SUB)
                    main = (lane >= spans[g]) & (lane < spans[g] + PIECE)
                    keep = (lane >> 4) == slots[g]
                    for j, (a, b) in enumerate(((k0, k1), (r0, r1), (w0, w1))):
                        v = pltpu.roll(jnp.where(main, a[at, :], b[at, :]), shifts[g], 1)
                        accs[j] = jnp.where(keep, v, accs[j])
                r = x * PIECE + h * SUB
                kb[pl.ds(PIECE + r, SUB), :] = accs[0]
                rb[pl.ds(r, SUB), :] = accs[1]
                wb[pl.ds(r, SUB), :] = accs[2]

        loop(PIECE, gather, 4)

        def setup(x):
            for h in range(HALVES):
                r = x * PIECE + h * SUB
                kc = kb[pl.ds(PIECE + r, SUB), :]
                kn = [kb[pl.ds(PIECE + r + d, SUB), :] for d in (PIECE, -PIECE, 1, -1)]
                kn += [pltpu.roll(kc, LANES - 1, 1), pltpu.roll(kc, 1, 1)]
                if h == HALVES - 1:
                    kn[2] = jnp.where(last_y, 0.0, kn[2])
                if h == 0:
                    kn[3] = jnp.where(first_y, 0.0, kn[3])
                kn[4] = jnp.where(z_cell == PIECE - 1, 0.0, kn[4])
                kn[5] = jnp.where(z_cell == 0, 0.0, kn[5])
                faces, diag = [], jnp.zeros((SUB, LANES), F32)
                for k in kn:
                    there = k > 0
                    half = 0.5 * (kc + k)
                    faces.append(jnp.where(there, half, 0.0))
                    diag = diag + jnp.where(there, half, kc)
                inside = kc > 0
                scale = jnp.where(inside, DAMPING / jnp.where(inside, diag, 1.0), 0.0)
                for j, face in enumerate(faces):
                    wt[j, pl.ds(r, SUB), :] = face * scale
                s = rb[pl.ds(r, SUB), :] * scale
                s2 = s * wb[pl.ds(r, SUB), :]
                base[0, pl.ds(r, SUB), :] = s
                base[1, pl.ds(r, SUB), :] = s2
                va[0, pl.ds(PIECE + r, SUB), :] = s
                va[1, pl.ds(PIECE + r, SUB), :] = s2

        loop(PIECE, setup, 8)

        def sweep(src, dst):
            for x in range(PIECE):
                for h in range(HALVES):
                    r = x * PIECE + h * SUB
                    a = PIECE + r
                    w = [wt[j, r : r + SUB, :] for j in range(6)]
                    for s in range(2):
                        v = src[s, a : a + SUB, :]
                        total = base[s, r : r + SUB, :] + v * (1.0 - DAMPING)
                        if x < PIECE - 1:
                            total = total + w[0] * src[s, a + PIECE : a + PIECE + SUB, :]
                        if x > 0:
                            total = total + w[1] * src[s, a - PIECE : a - PIECE + SUB, :]
                        total = total + w[2] * src[s, a + 1 : a + 1 + SUB, :]
                        total = total + w[3] * src[s, a - 1 : a - 1 + SUB, :]
                        total = total + w[4] * pltpu.roll(v, LANES - 1, 1)
                        total = total + w[5] * pltpu.roll(v, 1, 1)
                        dst[s, a : a + SUB, :] = total

        def two(i, _):
            sweep(va, vb)
            sweep(vb, va)
            return 0

        lax.fori_loop(0, (SWEEPS - 1) // 2, two, 0)
        if (SWEEPS - 1) % 2:
            sweep(va, vb)
            done = vb
        else:
            done = va

        tz = tent(z_cell.astype(F32))
        ty = [tent(sub.astype(F32) + float(SUB * h)) * tz for h in range(HALVES)]
        for c in range(0, CHUNKS, SUB):
            values = []
            for i in range(SUB):
                r = (c + i) * SUB
                v0, v1 = done[0, PIECE + r : PIECE + r + SUB, :], done[1, PIECE + r : PIECE + r + SUB, :]
                rb[r : r + SUB, :] = (v0 + v1) * (ty[(c + i) % HALVES] * float(tent((c + i) // HALVES)))
                values += [v0, v1]
            for i, v in enumerate(block_transpose(values, sub, lane)):
                at = first * CHUNKS * 2 + c * 2 + i
                basis[pl.ds(at, GROUP, stride=CHUNKS * 2), :] = v

        for g in range(GROUP):
            z0 = off[2, first + g] - MARGIN
            shift = (z0 - g * PIECE + 2 * LANES) % LANES
            values = [pltpu.roll(rb[c * SUB : (c + 1) * SUB, :], shift, 1) for c in range(CHUNKS)]
            add_piece(fr, off, first + g, first + g < live, values, lane, q0, q1)
        return 0

    groups = (live + GROUP - 1) // GROUP
    lax.fori_loop(0, groups, one_group, 0)

    def clear(group, _):
        count = GROUP * CHUNKS * 2
        basis[pl.ds(pl.multiple_of(group * count, SUB), count), :] = jnp.zeros((count, LANES), F32)
        return 0

    lax.fori_loop(groups, basis.shape[0] // (GROUP * CHUNKS * 2), clear, 0)

    def block(b):
        part = [q1[pl.ds(yf + (b * GROUP + j) * SUB, SUB), :] for j in range(GROUP)]
        slab[pl.ds(b * SUB, SUB), :] = pack_tiles(part, SUB, lane)

    loop(fr.live_blocks, block, 5)

    def core_rows(x):
        for t in range(fr.by // SUB):
            at = pl.ds((x + H) * yf + TOP + t * SUB, SUB)
            core[pl.ds(x * fr.by + t * SUB, SUB), :] = c0[at, :] + q0[at, :]

    loop(fr.bx, core_rows, 4)

    def edge_rows(x):
        for j, t in enumerate((tiles - 1, 0)):
            y_edge[pl.ds((2 * x + j) * SUB, SUB), :] = q0[pl.ds((x + 1) * yf + t * SUB, SUB), :]

    loop(fr.live_x, edge_rows, 8)
    for i, x in enumerate(edge_planes(fr)):
        row = (x + 1) * yf + TOP
        x_edge[i * fr.by : (i + 1) * fr.by, :] = q0[row : row + fr.by, :]


def edge_planes(fr):
    return [*range(fr.live_x - MARGIN, fr.live_x), *range(MARGIN)]


def z_part(info, sides, received, pack, j, lane):
    total = 0.0
    for i, buf in enumerate(received):
        lower = is_lower(info, 2, i)
        keep = ((lane >= LANES - SUB) & lower) | ((lane < SUB) & jnp.logical_not(lower))
        v = unpack_tile(buf[pl.ds(pack * SUB, SUB), :], j, LANES - SUB)
        total = total + jnp.where(keep, v, 0.0)
    return total


def fold_y(fr, info, y_edge, *rest):
    n = fr.sides[2]
    received, slabs, tmp = rest[:n], rest[n:-1], rest[-1]
    _, lane = iotas()

    def planes(b):
        for i in range(4):
            for j, t in enumerate((fr.tiles - 1, 0)):
                m = i * fr.tiles + t
                at = pl.ds(((4 * b + i) * 2 + j) * SUB, SUB)
                part = z_part(info, n, received, b * (4 * fr.tiles // GROUP) + m // GROUP, m % GROUP, lane)
                tmp[at, :] = y_edge[at, :] + part

    loop(fr.live_x // 4, planes, 5)

    def plane(x):
        for i, slab in enumerate(slabs):
            first = x * 2 * SUB + pick(is_lower(info, 1, i), 0, SUB + MARGIN)
            slab[pl.ds(x * MARGIN, MARGIN), :] = tmp[pl.ds(first, MARGIN), :]

    loop(fr.live_x, plane, 8)


def fold_x(fr, info, x_edge, *rest):
    n1, n2 = fr.sides[1], fr.sides[2]
    z_in, y_in, slabs, tmp = rest[:n2], rest[n2 : n1 + n2], rest[n1 + n2 : -1], rest[-1]
    _, lane = iotas()
    by = fr.by
    for i, x in enumerate(edge_planes(fr)):
        for t in range(by // SUB):
            m = x * fr.tiles + t + 1
            a = slice(i * by + t * SUB, i * by + (t + 1) * SUB)
            tmp[a, :] = x_edge[a, :] + z_part(info, n2, z_in, m // GROUP, m % GROUP, lane)
        for k, buf in enumerate(y_in):
            a = pl.ds(i * by + pick(is_lower(info, 1, k), by - MARGIN, 0), MARGIN)
            tmp[a, :] = tmp[a, :] + buf[x * MARGIN : (x + 1) * MARGIN, :]
    count = MARGIN * by
    for i, slab in enumerate(slabs):
        slab[...] = tmp[pl.ds(pl.multiple_of(pick(is_lower(info, 0, i), 0, count), SUB), count), :]


def finish(fr, info, core, *rest):
    n0, n1, n2 = fr.sides
    z_in, y_in, x_in, out = rest[:n2], rest[n2 : n1 + n2], rest[n1 + n2 : -1], rest[-1]
    _, lane = iotas()
    by = fr.by

    def planes(b):
        for i in range(4):
            row = (4 * b + i) * by
            for t in range(by // SUB):
                m = i * fr.tiles + t + 1
                at = pl.ds(row + t * SUB, SUB)
                pack = (b + MARGIN // 4) * (4 * fr.tiles // GROUP) + m // GROUP
                out[at, :] = core[at, :] + z_part(info, n2, z_in, pack, m % GROUP, lane)
            for k, buf in enumerate(y_in):
                a = pl.ds(row + pick(is_lower(info, 1, k), by - MARGIN, 0), MARGIN)
                out[a, :] = out[a, :] + buf[pl.ds((4 * b + i + MARGIN) * MARGIN, MARGIN), :]

    loop(fr.bx // 4, planes, 4)
    count = MARGIN * by
    for i, buf in enumerate(x_in):
        a = pl.ds(pl.multiple_of(pick(is_lower(info, 0, i), (fr.bx - MARGIN) * by, 0), SUB), count)
        out[a, :] = out[a, :] + buf[...]


def local(
    forcing,
    kappa_base,
    labels,
    contrast,
    channel_weight,
    coarse_coef,
    source_link,
    offsets,
    live_pieces,
    resident_bases,
):
    bx, by, bz = forcing.shape
    axes = ("gx", "gy", "gz")
    fr = Frame(bx, by, bz, [lax.axis_size(a) for a in axes])
    slots, nb = resident_bases.shape[3], resident_bases.shape[4]
    nd = coarse_coef.shape[3]
    cells = PIECE**3
    part = functools.partial
    n0, n1, n2 = fr.sides
    live_rows = fr.live_blocks * SUB

    info = jnp.stack([live_pieces[0, 0, 0]] + [lax.axis_index(a).astype(jnp.int32) for a in axes])
    off = jnp.swapaxes(offsets.reshape(slots, 3), 0, 1)
    link = jnp.swapaxes(source_link.reshape(slots, 4), 0, 1)
    coef = jnp.swapaxes(coarse_coef.reshape(nd, nb), 0, 1)
    bases = resident_bases.reshape(slots, nb, cells)
    raw = [a.reshape(bx * by, bz) for a in (kappa_base, labels, forcing)]

    width = 2 * MARGIN + H
    slab = rows_of(width * by + SUB)
    slabs = call(
        part(static_x, fr),
        [slab] * n0,
        [info, contrast, channel_weight, *raw, coef],
        [SMEM] * 3 + [HBM] * 3,
        [
            pltpu.VMEM((n0, H * by, LANES), F32),
            pltpu.VMEM((n0, H * by, LANES), jnp.int32),
            pltpu.SemaphoreType.DMA((n0, 3)),
        ],
    )
    received = swap("gx", slabs)
    slab = rows_of(-(-fr.xf * width // SUB) * SUB + 3 * SUB)
    k0, f0, w0, coef3, *slabs = call(
        part(static_y, fr),
        [fr.frame] * 3 + [rows_of(3 * SUB)] + [slab] * n1,
        [info, contrast, channel_weight, *raw, coef, *received],
        [SMEM] * 3,
    )
    received = swap("gy", slabs)
    slab = rows_of((fr.blocks + 9) * SUB)
    k0, f0, w0, coef9, *slabs = call(
        part(static_z, fr),
        [fr.frame] * 3 + [rows_of(9 * SUB)] + [slab] * n2,
        [info, k0, f0, w0, coef3, *received],
        [SMEM],
        alias={1: 0, 2: 1, 3: 2},
    )
    static_z_in = swap("gz", slabs)

    p0, p1, *slabs = call(
        part(prolong, fr, (slots, nb, 4 if slots % 4 == 0 else 1)),
        [fr.frame] * 2 + [rows_of(live_rows)] * n2,
        [info, off, link, bases, coef9, *static_z_in],
        [SMEM] * 3 + [HBM],
        [
            pltpu.VMEM((27, SUB, LANES), F32),
            pltpu.VMEM((slots, nb, cells), F32),
            pltpu.SemaphoreType.DMA((slots,)),
        ],
        limit=16,
    )
    received = swap("gz", slabs)
    p0, p1, *slabs = call(
        part(coarse_y, fr),
        [fr.frame] * 2 + [rows_of(fr.live_x * (WIDE + 2))] * n1,
        [info, p0, p1, *received],
        [SMEM],
        alias={1: 0, 2: 1},
    )
    received = swap("gy", slabs)
    p0, p1, *slabs = call(
        part(coarse_x, fr),
        [fr.frame] * 2 + [rows_of(WIDE * fr.yf + -(-WIDE * fr.tiles // GROUP) * SUB)] * n0,
        [info, p0, p1, *received],
        [SMEM],
        alias={1: 0, 2: 1},
    )
    received = swap("gx", slabs)

    frame = pltpu.VMEM((fr.rows, LANES), F32)
    padded = PROWS + 2 * PIECE
    core, basis, y_edge, x_edge, slab = call(
        part(enrich, fr),
        [
            rows_of(bx * by),
            rows_of(slots * CHUNKS * 2),
            rows_of(fr.live_x * 2 * SUB),
            rows_of(2 * MARGIN * by),
            rows_of(live_rows),
        ],
        [info, off, p0, p1, k0, f0, w0, *received, *static_z_in],
        [SMEM] * 2,
        [frame] * 8
        + [
            pltpu.VMEM((padded, LANES), F32),
            pltpu.VMEM((PROWS, LANES), F32),
            pltpu.VMEM((PROWS, LANES), F32),
            pltpu.VMEM((6, PROWS, LANES), F32),
            pltpu.VMEM((2, PROWS, LANES), F32),
            pltpu.VMEM((2, padded, LANES), F32),
            pltpu.VMEM((2, padded, LANES), F32),
        ],
        limit=32,
    )

    z_in = swap("gz", [slab] * n2)
    slabs = call(
        part(fold_y, fr),
        [rows_of(fr.live_x * MARGIN)] * n1,
        [info, y_edge, *z_in],
        [SMEM],
        [pltpu.VMEM((fr.live_x * 2 * SUB, LANES), F32)],
    )
    y_in = swap("gy", slabs)
    slabs = call(
        part(fold_x, fr),
        [rows_of(MARGIN * by)] * n0,
        [info, x_edge, *z_in, *y_in],
        [SMEM],
        [pltpu.VMEM((2 * MARGIN * by, LANES), F32)],
    )
    x_in = swap("gx", slabs)
    update = call(part(finish, fr), rows_of(bx * by), [info, core, *z_in, *y_in, *x_in], [SMEM])
    new_basis = basis.reshape(slots, CHUNKS, 2, LANES).swapaxes(1, 2)
    return update.reshape(bx, by, bz), new_basis.reshape(1, 1, 1, slots, 2, cells)


def solution(mesh):
    brick = ("gx", "gy", "gz")
    return jax.shard_map(
        local,
        mesh=mesh,
        in_specs=(
            P(*brick),
            P(*brick),
            P(*brick),
            P(),
            P(),
            P(*brick, None, None),
            P(*brick, None, None),
            P(*brick, None, None),
            P(*brick),
            P(*brick, None, None, None),
        ),
        out_specs=(P(*brick), P(*brick, None, None, None)),
        check_vma=False,
    )
```

```python
import functools

import jax
import jax.numpy as jnp
from jax import lax
from jax.experimental import pallas as pl
from jax.experimental.pallas import tpu as pltpu
from jax.sharding import PartitionSpec as P

MARGIN = 4
PIECE = 16
SWEEPS = 20
DAMPING = 2.0 / 3.0

H = MARGIN + 1
WIDE = 2 * MARGIN + 1
LANES = 128
SUB = 8
TOP = 8
GROUP = LANES // PIECE
HALVES = PIECE // SUB
CHUNKS = PIECE * HALVES
PROWS = PIECE * PIECE
F32 = jnp.float32


def iotas():
    shape = (SUB, LANES)
    return lax.broadcasted_iota(jnp.int32, shape, 0), lax.broadcasted_iota(jnp.int32, shape, 1)


def loop(count, body, unroll=1):
    while count % unroll:
        unroll -= 1

    def step(i, _):
        for j in range(unroll):
            body(i * unroll + j)
        return 0

    lax.fori_loop(0, count // unroll, step, 0)


def pick(flag, a, b):
    return jnp.where(flag, a, b)


def pack_tiles(tiles, shift, lane):
    packed = jnp.zeros((SUB, LANES), F32)
    for j, tile in enumerate(tiles):
        packed = jnp.where((lane >> 4) == j, pltpu.roll(tile, (shift + PIECE * j) % LANES, 1), packed)
    return packed


def unpack_tile(packed, j, shift):
    return pltpu.roll(packed, (shift - PIECE * j + 2 * LANES) % LANES, 1)


def sum_rows(values, sub):
    for k in (1, 2, 4):
        low = (sub & k) == 0
        values = [
            jnp.where(low, a, b) + pltpu.roll(jnp.where(low, b, a), SUB - k, 0)
            for a, b in zip(values[0::2], values[1::2])
        ]
    return values[0]


def block_transpose(values, sub, lane):
    for k in (4, 2, 1):
        in_group = ((lane >> 4) & k) != 0
        in_sub = (sub & k) != 0
        moves = in_sub != in_group
        if k == 4:
            others = [pltpu.roll(v, 64, 1) for v in values]
            others = [pltpu.roll(v, 4, 0) for v in others]
        else:
            pairs = [(pltpu.roll(v, PIECE * k, 1), pltpu.roll(v, LANES - PIECE * k, 1)) for v in values]
            others = [jnp.where(in_group, q, p) for q, p in pairs]
            others = [jnp.where(in_sub, pltpu.roll(m, k, 0), pltpu.roll(m, SUB - k, 0)) for m in others]
        values = [jnp.where(moves, o, v) for o, v in zip(others, values)]
    return values


class Frame:
    def __init__(self, bx, by, bz, counts):
        self.bx, self.by, self.bz = bx, by, bz
        self.xf = bx + 2 * H
        self.yf = by + 2 * TOP
        self.tiles = self.yf // SUB
        self.blocks = -(-self.xf * self.tiles // GROUP)
        self.rows = self.blocks * GROUP * SUB
        self.live_x = bx + 2 * MARGIN
        self.live_blocks = self.live_x * self.tiles // GROUP
        self.counts = counts
        self.sides = [1 if n == 2 else 2 for n in counts]

    @property
    def frame(self):
        return rows_of(self.rows)


def rows_of(count):
    return jax.ShapeDtypeStruct((-(-count // SUB) * SUB, LANES), F32)


def zero(ref):
    ref[...] = jnp.zeros(ref.shape, ref.dtype)


VMEM = pl.BlockSpec(memory_space=pltpu.VMEM)
SMEM = pl.BlockSpec(memory_space=pltpu.SMEM)
HBM = pl.BlockSpec(memory_space=pltpu.HBM)


def call(kernel, outs, ins, specs=(), scratch=(), alias=None, limit=12):
    specs = list(specs) + [VMEM] * (len(ins) - len(specs))
    return pl.pallas_call(
        kernel,
        out_shape=outs,
        in_specs=specs,
        out_specs=jax.tree.map(lambda _: VMEM, outs),
        scratch_shapes=list(scratch),
        input_output_aliases=alias or {},
        compiler_params=pltpu.CompilerParams(vmem_limit_bytes=limit * 1024 * 1024),
    )(*ins)


def is_lower(info, axis, phase):
    return ((info[1 + axis] + phase) & 1) == 0


def swap(axis, slabs):
    count = lax.axis_size(axis)
    received = []
    for phase, slab in enumerate(slabs):
        pairs = [(i, i + 1) for i in range(phase, count - 1, 2)]
        received.append(lax.ppermute(slab, axis, pairs + [(j, i) for i, j in pairs]))
    return received


def look_up(labels, values, which):
    out = jnp.zeros(labels.shape, F32)
    for c in range(values.shape[1]):
        out = out + jnp.where(labels == c, values[which, c], 0.0)
    return out


def static_x(fr, info, contrast, channel, kappa, labels, forcing, *rest):
    n = fr.sides[0]
    slabs, (k_buf, l_buf, t_buf, sem, t_sem) = rest[:n], rest[n:]
    by = fr.by
    f_row, w_row, c_row = H * by, (H + MARGIN) * by, (H + 2 * MARGIN) * by
    copies = [
        pltpu.make_async_copy(contrast, t_buf.at[0], t_sem.at[0]),
        pltpu.make_async_copy(channel, t_buf.at[1], t_sem.at[1]),
    ]
    for i, slab in enumerate(slabs):
        lower = is_lower(info, 0, i)
        first = pl.multiple_of(pick(lower, (fr.bx - H) * by, 0), SUB)
        four = pl.multiple_of(pick(lower, (fr.bx - MARGIN) * by, 0), SUB)
        for j, (src, dst) in enumerate(
            (
                (kappa.at[pl.ds(first, H * by)], k_buf.at[i]),
                (labels.at[pl.ds(first, H * by)], l_buf.at[i]),
                (forcing.at[pl.ds(four, MARGIN * by)], slab.at[pl.ds(f_row, MARGIN * by)]),
            )
        ):
            copies.append(pltpu.make_async_copy(src, dst, sem.at[i, j]))
    for copy in copies:
        copy.start()
    for copy in copies:
        copy.wait()
    for i, slab in enumerate(slabs):
        skip = pl.multiple_of(pick(is_lower(info, 0, i), by, 0), SUB)
        slab[0:f_row, :] = k_buf[i] * look_up(l_buf[i], t_buf, 0)
        slab[w_row:c_row, :] = look_up(l_buf[i, pl.ds(skip, MARGIN * by), :], t_buf, 1)


def static_y(fr, info, tables, kappa, labels, forcing, *rest):
    n = fr.sides[0]
    received, (k0, f0, w0), slabs = rest[:n], rest[n : n + 3], rest[n + 3 :]
    by, yf, w = fr.by, fr.yf, 2 * MARGIN + H
    for ref in (k0, f0, w0):
        zero(ref)

    def core(x):
        for t in range(by // SUB):
            src = pl.ds(x * by + t * SUB, SUB)
            dst = pl.ds((x + H) * yf + TOP + t * SUB, SUB)
            label = labels[src, :]
            k0[dst, :] = kappa[src, :] * look_up(label, tables, 0)
            w0[dst, :] = look_up(label, tables, 1)
            f0[dst, :] = forcing[src, :]

    loop(fr.bx, core, 4)
    for i, buf in enumerate(received):
        lower = is_lower(info, 0, i)
        for frame, count, at, low in ((k0, H, 0, 0), (f0, MARGIN, H, 1), (w0, MARGIN, H + MARGIN, 1)):
            first = pick(lower, fr.bx + H, low)
            for j in range(count):
                for t in range(by // SUB):
                    row = (at + j) * by + t * SUB
                    frame[pl.ds(pl.multiple_of((first + j) * yf + TOP + t * SUB, SUB), SUB), :] = buf[row : row + SUB, :]

    def plane(x):
        r, o = x * yf, x * w
        for i, slab in enumerate(slabs):
            lower = is_lower(info, 1, i)
            for frame, count, at in ((k0, H, 0), (f0, MARGIN, H), (w0, MARGIN, H + MARGIN)):
                first = r + pick(lower, TOP + by - count, TOP)
                slab[pl.ds(o + at, count), :] = frame[pl.ds(first, count), :]

    loop(fr.xf, plane, 6)


def static_z(fr, info, k_in, f_in, w_in, *rest):
    n = fr.sides[1]
    received, (k0, f0, w0), slabs = rest[:n], rest[n : n + 3], rest[n + 3 :]
    del k_in, f_in, w_in
    _, lane = iotas()
    by, yf, w = fr.by, fr.yf, 2 * MARGIN + H

    def plane(x):
        r, o = x * yf, x * w
        for i, buf in enumerate(received):
            lower = is_lower(info, 1, i)
            for frame, count, at in ((k0, H, 0), (f0, MARGIN, H), (w0, MARGIN, H + MARGIN)):
                first = r + pick(lower, TOP + by, TOP - count)
                frame[pl.ds(first, count), :] = buf[pl.ds(o + at, count), :]

    loop(fr.xf, plane, 6)
    group = lane & (PIECE - 1)

    def block(b):
        for i, slab in enumerate(slabs):
            lower = is_lower(info, 2, i)
            packs = []
            for frame, high, low in ((k0, H, 0), (f0, WIDE, H), (w0, WIDE + MARGIN, WIDE)):
                tiles = [frame[pl.ds((b * GROUP + j) * SUB, SUB), :] for j in range(GROUP)]
                packs.append(pack_tiles(tiles, pick(lower, high, low), lane))
            mix = jnp.where(group < H, packs[0], jnp.where(group < WIDE, packs[1], packs[2]))
            slab[pl.ds(b * SUB, SUB), :] = mix

    loop(fr.blocks, block, 4)


def place_masks(z0, lane):
    main = (lane >= z0) & (lane < z0 + PIECE)
    beyond = jnp.where(lane < LANES // 2, lane + LANES, lane - LANES)
    return main, (beyond >= z0) & (beyond < z0 + PIECE)


def corner(off, p):
    return off[0, p] + 1, off[1, p] + TOP - MARGIN, off[2, p] - MARGIN


def piece_rows(fr, off, p):
    x0, y0, _ = corner(off, p)
    base = x0 * fr.yf + y0
    return [pl.ds(base + (c // HALVES) * fr.yf + (c % HALVES) * SUB, SUB) for c in range(CHUNKS)]


def add_main(fr, off, p, valid, values, lane, ref):
    main, _ = place_masks(off[2, p] - MARGIN, lane)
    main = main & valid
    places = piece_rows(fr, off, p)
    new = [ref[a, :] + jnp.where(main, v, 0.0) for a, v in zip(places, values)]
    for a, v in zip(places, new):
        ref[a, :] = v


def add_beyond(fr, off, p, valid, get_values, lane, ref):
    z0 = off[2, p] - MARGIN

    @pl.when(valid & ((z0 < 0) | (z0 + PIECE > LANES)))
    def _():
        _, beyond = place_masks(z0, lane)
        places = piece_rows(fr, off, p)
        new = [ref[a, :] + jnp.where(beyond, v, 0.0) for a, v in zip(places, get_values())]
        for a, v in zip(places, new):
            ref[a, :] = v


def stack(own, *rest):
    received, out = rest[:-1], rest[-1]
    zero(out)
    count = own.shape[0]
    for i, ref in enumerate((own, *received)):
        out[i * count : (i + 1) * count, 0 : ref.shape[1]] = ref[...]


def prolong(fr, shape, info, off, link, bases, own, *rest):
    nb, together = shape
    n, m = fr.sides[0], fr.sides[2]
    received, (p0, p1), slabs, (table, keep) = rest[:n], rest[n : n + 2], rest[n + 2 : n + m + 2], rest[n + m + 2 :]
    sub, lane = iotas()
    live = info[0]
    zero(p0)
    zero(p1)
    each = (1 + fr.sides[1]) * (1 + m)
    for i, ref in enumerate((own, *received)):
        for j in range(each):
            table[i * each + j] = ref[j * SUB : (j + 1) * SUB, :]

    def position(axis, step):
        came = 1 + ((info[1 + axis] + jnp.where(step == 0, 1, 0)) & 1)
        return jnp.where(step == 1, 0, came)

    def some(step, _):
        numbers = [step * together + i for i in range(together)]
        per = CHUNKS // SUB
        rows = []
        for p in numbers:
            at = [position(axis, link[axis, p]) for axis in range(3)]
            row = table[(at[0] * (1 + fr.sides[1]) + at[1]) * (1 + m) + at[2]]
            coef = jnp.sum(jnp.where(lane == link[3, p], row, 0.0), axis=1, keepdims=True)
            coef = jnp.broadcast_to(coef, (SUB, LANES))[0:nb]
            for first in range(0, CHUNKS, SUB):
                parts = [bases[p, :, c * LANES : (c + 1) * LANES] * coef for c in range(first, first + SUB)]
                rows.append(sum_rows(parts, sub))
        rows = block_transpose(rows, sub, lane)
        for i, v in enumerate(rows):
            keep[i] = v

        def placed(i, p):
            z0 = off[2, p] - MARGIN
            return [
                pltpu.roll(keep[i * per + c // SUB], (z0 - PIECE * (c % SUB) + 2 * LANES) % LANES, 1)
                for c in range(CHUNKS)
            ]

        for i, p in enumerate(numbers):
            add_main(fr, off, p, p < live, placed(i, p), lane, p0)
        for i, p in enumerate(numbers):
            add_beyond(fr, off, p, p < live, functools.partial(placed, i, p), lane, p1)
        return 0

    lax.fori_loop(0, (live + together - 1) // together, some, 0)

    def block(b):
        tiles = []
        for j in range(GROUP):
            at = pl.ds(fr.yf + (b * GROUP + j) * SUB, SUB)
            tiles.append((p0[at, :], p1[at, :]))
        for i, slab in enumerate(slabs):
            lower = is_lower(info, 2, i)
            main = (lane >= LANES // 2) == lower
            near = [jnp.where(main, x, y) for x, y in tiles]
            slab[pl.ds(b * SUB, SUB), :] = pack_tiles(near, SUB, lane)

    loop(fr.live_blocks, block, 3)


def coarse_y(fr, info, p0_in, p1_in, *rest):
    n = fr.sides[2]
    received, (p0, p1), slabs = rest[:n], rest[n : n + 2], rest[n + 2 :]
    del p0_in, p1_in
    _, lane = iotas()
    packed = fr.live_x * WIDE

    def block(b):
        for i, buf in enumerate(received):
            lower = is_lower(info, 2, i)
            pack = buf[pl.ds(b * SUB, SUB), :]
            places = [pl.ds(fr.yf + (b * GROUP + j) * SUB, SUB) for j in range(GROUP)]
            values = [unpack_tile(pack, j, LANES - SUB) for j in range(GROUP)]
            to_main = ((lane >= LANES - SUB) & lower) | ((lane < SUB) & jnp.logical_not(lower))
            to_beyond = ((lane >= LANES - SUB) & jnp.logical_not(lower)) | ((lane < SUB) & lower)
            main = [p0[a, :] + jnp.where(to_main, v, 0.0) for a, v in zip(places, values)]
            beyond = [p1[a, :] + jnp.where(to_beyond, v, 0.0) for a, v in zip(places, values)]
            for a, v0, v1 in zip(places, main, beyond):
                p0[a, :] = v0
                p1[a, :] = v1

    loop(fr.live_blocks, block, 3)

    def plane(x):
        r = (x + 1) * fr.yf
        for i, slab in enumerate(slabs):
            first = r + pick(is_lower(info, 1, i), TOP + fr.by - H, TOP - MARGIN)
            slab[pl.ds(x * WIDE, WIDE), :] = p0[pl.ds(first, WIDE), :]

    loop(fr.live_x, plane, 8)

    def margin(b):
        for i, slab in enumerate(slabs):
            first = pick(is_lower(info, 1, i), fr.tiles - 2, 0)
            tiles = []
            for j in range(GROUP):
                row = (b * (GROUP // 2) + j // 2 + 1) * fr.yf + (first + j % 2) * SUB
                tiles.append(p1[pl.ds(row, SUB), :])
            slab[pl.ds(packed + b * SUB, SUB), :] = pack_tiles(tiles, SUB, lane)

    loop(fr.live_x * 2 // GROUP, margin, 5)


def coarse_x(fr, info, p0_in, p1_in, *rest):
    n = fr.sides[1]
    received, (p0, p1), slabs = rest[:n], rest[n : n + 2], rest[n + 2 :]
    del p0_in, p1_in
    _, lane = iotas()
    packed = fr.live_x * WIDE
    edge = (lane >= LANES - SUB) | (lane < SUB)

    def plane(x):
        r = (x + 1) * fr.yf
        for i, buf in enumerate(received):
            at = pl.ds(r + pick(is_lower(info, 1, i), TOP + fr.by - MARGIN, TOP - H), WIDE)
            p0[at, :] = p0[at, :] + buf[pl.ds(x * WIDE, WIDE), :]

    loop(fr.live_x, plane, 8)

    def margin(b):
        for i, buf in enumerate(received):
            first = pick(is_lower(info, 1, i), fr.tiles - 2, 0)
            pack = buf[pl.ds(packed + b * SUB, SUB), :]
            places = [
                pl.ds((b * (GROUP // 2) + j // 2 + 1) * fr.yf + (first + j % 2) * SUB, SUB) for j in range(GROUP)
            ]
            values = [jnp.where(edge, unpack_tile(pack, j, LANES - SUB), 0.0) for j in range(GROUP)]
            values = [p1[a, :] + v for a, v in zip(places, values)]
            for a, v in zip(places, values):
                p1[a, :] = v

    loop(fr.live_x * 2 // GROUP, margin, 5)
    main = WIDE * fr.yf
    for i, slab in enumerate(slabs):
        row = pl.multiple_of(pick(is_lower(info, 0, i), fr.xf - 1 - WIDE, 1) * fr.yf, SUB)
        slab[0:main, :] = p0[pl.ds(row, main), :]
        for b in range(-(-WIDE * fr.tiles // GROUP)):
            tiles = [p1[pl.ds(row + (b * GROUP + j) * SUB, SUB), :] for j in range(GROUP)]
            slab[main + b * SUB : main + (b + 1) * SUB, :] = pack_tiles(tiles, SUB, lane)


def beyond(fr, info, *rest):
    n2 = fr.sides[2]
    z_in, outs = rest[:n2], rest[n2:]
    _, lane = iotas()

    def block(b):
        sums = [[0.0] * GROUP for _ in range(3)]
        for i, buf in enumerate(z_in):
            lower = is_lower(info, 2, i)
            pack = buf[pl.ds(b * SUB, SUB), :]
            for m, (start, width) in enumerate(((0, H), (H, MARGIN), (H + MARGIN, MARGIN))):
                shift = pick(lower, LANES - start, LANES - width - start)
                low = pick(lower, 0, LANES - width)
                keep = (lane >= low) & (lane < low + width)
                for j in range(GROUP):
                    sums[m][j] = sums[m][j] + jnp.where(keep, unpack_tile(pack, j, shift), 0.0)
        for m, out in enumerate(outs):
            for j in range(GROUP):
                out[pl.ds((b * GROUP + j) * SUB, SUB), :] = sums[m][j]

    loop(fr.blocks, block, 4)


def gather_group(fr, off, first, live, fields, lane):
    places = []
    for g in range(GROUP):
        x0, y0, z0 = corner(off, first + g)
        slot = jnp.where(first + g < live, g, -1)
        places.append((x0 * fr.yf + y0, z0, (g * PIECE - z0 + LANES) % LANES, slot))

    def tiles_at(x, h):
        accs = [jnp.zeros((SUB, LANES), F32) for _ in fields]
        for base, z0, shift, slot in places:
            at = pl.ds(base + x * fr.yf + h * SUB, SUB)
            main = (lane >= z0) & (lane < z0 + PIECE)
            keep = (lane >> 4) == slot
            for j, (a, b) in enumerate(fields):
                v = pltpu.roll(jnp.where(main, a[at, :], b[at, :]), shift, 1)
                accs[j] = jnp.where(keep, v, accs[j])
        return accs

    return tiles_at


def couple(fr, info, off, k0, k1, w0, w1, wt, scales, weights, kb):
    sub, lane = iotas()
    live = info[0]
    first_y, last_y = sub == 0, sub == SUB - 1
    z_cell = lane & (PIECE - 1)
    zero(kb)

    def one_group(group, _):
        tiles_at = gather_group(fr, off, group * GROUP, live, ((k0, k1), (w0, w1)), lane)

        def gather(x):
            for h in range(HALVES):
                r = x * PIECE + h * SUB
                kb[pl.ds(PIECE + r, SUB), :], weights[group, pl.ds(r, SUB), :] = tiles_at(x, h)

        loop(PIECE, gather, 4)

        def setup(x):
            for h in range(HALVES):
                r = x * PIECE + h * SUB
                kc = kb[pl.ds(PIECE + r, SUB), :]
                kn = [kb[pl.ds(PIECE + r + d, SUB), :] for d in (PIECE, -PIECE, 1, -1)]
                kn += [pltpu.roll(kc, LANES - 1, 1), pltpu.roll(kc, 1, 1)]
                if h == HALVES - 1:
                    kn[2] = jnp.where(last_y, 0.0, kn[2])
                if h == 0:
                    kn[3] = jnp.where(first_y, 0.0, kn[3])
                kn[4] = jnp.where(z_cell == PIECE - 1, 0.0, kn[4])
                kn[5] = jnp.where(z_cell == 0, 0.0, kn[5])
                faces, diag = [], jnp.zeros((SUB, LANES), F32)
                for k in kn:
                    there = k > 0
                    half = 0.5 * (kc + k)
                    faces.append(jnp.where(there, half, 0.0))
                    diag = diag + jnp.where(there, half, kc)
                inside = kc > 0
                scale = jnp.where(inside, DAMPING / jnp.where(inside, diag, 1.0), 0.0)
                for j, face in enumerate(faces):
                    wt[group, j, pl.ds(r, SUB), :] = face * scale
                scales[group, pl.ds(r, SUB), :] = scale

        loop(PIECE, setup, 8)
        return 0

    lax.fori_loop(0, (live + GROUP - 1) // GROUP, one_group, 0)


def enrich(fr, info, off, p0, p1, k0, f0, k1, f1, wt, scales, weights, *rest):
    n0 = fr.sides[0]
    x_in, rest = rest[:n0], rest[n0:]
    core, solved, y_edge, x_edge, slab = rest[:5]
    c0, c1, r0, r1, q0, q1, rb, base, va, vb, here = rest[5:]
    sub, lane = iotas()
    yf, tiles = fr.yf, fr.tiles
    live = info[0]
    main_rows = WIDE * yf
    edge = (lane >= LANES - SUB) | (lane < SUB)

    c0[...] = p0[...]
    c1[...] = p1[...]
    for i, buf in enumerate(x_in):
        row = pl.multiple_of(pick(is_lower(info, 0, i), fr.xf - WIDE, 0) * yf, SUB)
        a = pl.ds(row, main_rows)
        c0[a, :] = c0[a, :] + buf[0:main_rows, :]
        for b in range(-(-WIDE * tiles // GROUP)):
            pack = buf[main_rows + b * SUB : main_rows + (b + 1) * SUB, :]
            count = min(GROUP, WIDE * tiles - b * GROUP)
            places = [pl.ds(row + (b * GROUP + j) * SUB, SUB) for j in range(count)]
            values = [jnp.where(edge, unpack_tile(pack, j, LANES - SUB), 0.0) for j in range(count)]
            for a, v in zip(places, [c1[a, :] + v for a, v in zip(places, values)]):
                c1[a, :] = v

    def mask(b):
        for j in range(GROUP):
            at = pl.ds((b * GROUP + j) * SUB, SUB)
            c0[at, :] = jnp.where(k0[at, :] > 0, c0[at, :], 0.0)
            c1[at, :] = jnp.where(k1[at, :] > 0, c1[at, :], 0.0)

    loop(fr.blocks, mask, 4)

    def next_z(a, b):
        return pltpu.roll(jnp.where(lane == 0, b, a), LANES - 1, 1)

    def last_z(a, b):
        return pltpu.roll(jnp.where(lane == LANES - 1, b, a), 1, 1)

    def at_edge(axis, count, first, last, position):
        low = (position == first) & (info[1 + axis] == 0)
        high = (position == last) & (info[1 + axis] == count - 1)
        return jnp.where(low, 1.0, 0.0) + jnp.where(high, 1.0, 0.0)

    out_y = [at_edge(1, fr.counts[1], TOP, TOP + fr.by - 1, sub + t * SUB) for t in range(tiles)]
    out_z = at_edge(2, fr.counts[2], 0, LANES - 1, lane)

    def flux_x(x):
        fluxes = []
        for t in range(tiles):
            at, to = pl.ds(x * yf + t * SUB, SUB), pl.ds((x + 1) * yf + t * SUB, SUB)
            fluxes += [(k[at, :] + k[to, :]) * (c[at, :] - c[to, :]) for c, k in ((c0, k0), (c1, k1))]
        return fluxes

    def residual(x, before):
        r = x * yf
        after = flux_x(x)
        out_x = at_edge(0, fr.counts[0], H, H + fr.bx - 1, x)
        last_y = [jnp.zeros((SUB, LANES), F32)] * 2
        for t in range(tiles):
            at, to = pl.ds(r + t * SUB, SUB), pl.ds(r + t * SUB + 1, SUB)
            cs, ks = (c0[at, :], c1[at, :]), (k0[at, :], k1[at, :])
            fz = []
            for i in range(2):
                cn, kn = next_z(cs[i], cs[1 - i]), next_z(ks[i], ks[1 - i])
                fz.append((ks[i] + kn) * (cs[i] - cn))
            for i, (c, k, f, out) in enumerate(((c0, k0, f0, r0), (c1, k1, f1, r1))):
                fy = pltpu.roll((ks[i] + k[to, :]) * (cs[i] - c[to, :]), 1, 0)
                fy_next = (ks[i] + k[to, :]) * (cs[i] - c[to, :])
                fy_last = jnp.where(sub == 0, last_y[i], fy)
                last_y[i] = fy
                outside = out_x + out_y[t] + (out_z if i == 0 else 0.0)
                total = (after[2 * t + i] - before[2 * t + i]) + (fy_next - fy_last)
                total = total + (fz[i] - last_z(fz[i], fz[1 - i])) + outside * (ks[i] * cs[i])
                out[at, :] = jnp.where(ks[i] > 0, f[at, :] - 0.5 * total, 0.0)
        return tuple(after)

    def residuals(i, before):
        for j in range(4):
            before = residual(4 * i + j + 1, before)
        return before

    lax.fori_loop(0, fr.live_x // 4, residuals, tuple(flux_x(0)))

    zero(q0)
    zero(q1)
    for ref in (va, vb):
        zero(ref)

    z_cell = lane & (PIECE - 1)
    tz = tent(z_cell.astype(F32))
    ty = [tent(sub.astype(F32) + float(SUB * h)) * tz for h in range(HALVES)]

    def one_group(group, _):
        first = group * GROUP
        tiles_at = gather_group(fr, off, first, live, ((r0, r1),), lane)

        def gather(x):
            for h in range(HALVES):
                r = x * PIECE + h * SUB
                at = pl.ds(r, SUB)
                s = tiles_at(x, h)[0] * scales[group, at, :]
                s2 = s * weights[group, at, :]
                for i, v in enumerate((s, s2)):
                    base[i, at, :] = v
                    va[i, pl.ds(PIECE + r, SUB), :] = v

        loop(PIECE, gather, 8)
        here[...] = wt[group]

        def sweep(src, dst, out=None):
            for x in range(PIECE):
                for h in range(HALVES):
                    r = x * PIECE + h * SUB
                    a = PIECE + r
                    w = [here[j, r : r + SUB, :] for j in range(6)]
                    for s in range(2):
                        v = src[s, a : a + SUB, :]
                        total = base[s, r : r + SUB, :] + v * (1.0 - DAMPING)
                        if x < PIECE - 1:
                            total = total + w[0] * src[s, a + PIECE : a + PIECE + SUB, :]
                        if x > 0:
                            total = total + w[1] * src[s, a - PIECE : a - PIECE + SUB, :]
                        total = total + w[2] * src[s, a + 1 : a + 1 + SUB, :]
                        total = total + w[3] * src[s, a - 1 : a - 1 + SUB, :]
                        total = total + w[4] * pltpu.roll(v, LANES - 1, 1)
                        total = total + w[5] * pltpu.roll(v, 1, 1)
                        if out is None:
                            dst[s, a : a + SUB, :] = total
                        else:
                            out[group, s, r : r + SUB, :] = total

        def two(i, _):
            sweep(va, vb)
            sweep(vb, va)
            return 0

        lax.fori_loop(0, (SWEEPS - 2) // 2, two, 0)
        if SWEEPS % 2:
            sweep(va, vb)
            sweep(vb, None, solved)
        else:
            sweep(va, None, solved)

        for c in range(CHUNKS):
            a = slice(c * SUB, (c + 1) * SUB)
            weight = ty[c % HALVES] * float(tent(c // HALVES))
            rb[a, :] = (solved[group, 0, a, :] + solved[group, 1, a, :]) * weight

        def placed(g):
            shift = (off[2, first + g] - MARGIN - g * PIECE + 2 * LANES) % LANES
            return [pltpu.roll(rb[c * SUB : (c + 1) * SUB, :], shift, 1) for c in range(CHUNKS)]

        for g in range(GROUP):
            add_main(fr, off, first + g, first + g < live, placed(g), lane, q0)
        for g in range(GROUP):
            add_beyond(fr, off, first + g, first + g < live, functools.partial(placed, g), lane, q1)
        return 0

    lax.fori_loop(0, (live + GROUP - 1) // GROUP, one_group, 0)

    def block(b):
        part = [q1[pl.ds(yf + (b * GROUP + j) * SUB, SUB), :] for j in range(GROUP)]
        slab[pl.ds(b * SUB, SUB), :] = pack_tiles(part, SUB, lane)

    loop(fr.live_blocks, block, 5)

    def core_rows(x):
        for t in range(fr.by // SUB):
            at = pl.ds((x + H) * yf + TOP + t * SUB, SUB)
            core[pl.ds(x * fr.by + t * SUB, SUB), :] = c0[at, :] + q0[at, :]

    loop(fr.bx, core_rows, 4)

    def edge_rows(x):
        for j, t in enumerate((tiles - 1, 0)):
            y_edge[pl.ds((2 * x + j) * SUB, SUB), :] = q0[pl.ds((x + 1) * yf + t * SUB, SUB), :]

    loop(fr.live_x, edge_rows, 8)
    for i, x in enumerate(edge_planes(fr)):
        row = (x + 1) * yf + TOP
        x_edge[i * fr.by : (i + 1) * fr.by, :] = q0[row : row + fr.by, :]


def tent(t):
    return (t + 0.5) * (PIECE - t - 0.5) * (4.0 / (PIECE * PIECE))


def lay_out(info, solved, basis):
    sub, lane = iotas()
    groups = (info[0] + GROUP - 1) // GROUP
    count = GROUP * CHUNKS * 2

    def one_group(group, _):
        for c in range(0, CHUNKS, SUB):
            values = []
            for i in range(c, c + SUB):
                values += [solved[group, s, i * SUB : (i + 1) * SUB, :] for s in range(2)]
            for i, v in enumerate(block_transpose(values, sub, lane)):
                basis[pl.ds(group * count + c * 2 + i, GROUP, stride=CHUNKS * 2), :] = v
        return 0

    lax.fori_loop(0, groups, one_group, 0)

    def clear(group, _):
        basis[pl.ds(pl.multiple_of(group * count, SUB), count), :] = jnp.zeros((count, LANES), F32)
        return 0

    lax.fori_loop(groups, basis.shape[0] // count, clear, 0)


def edge_planes(fr):
    return [*range(fr.live_x - MARGIN, fr.live_x), *range(MARGIN)]


def z_part(info, sides, received, pack, j, lane):
    total = 0.0
    for i, buf in enumerate(received):
        lower = is_lower(info, 2, i)
        keep = ((lane >= LANES - SUB) & lower) | ((lane < SUB) & jnp.logical_not(lower))
        v = unpack_tile(buf[pl.ds(pack * SUB, SUB), :], j, LANES - SUB)
        total = total + jnp.where(keep, v, 0.0)
    return total


def fold_y(fr, info, y_edge, *rest):
    n = fr.sides[2]
    received, slabs, tmp = rest[:n], rest[n:-1], rest[-1]
    _, lane = iotas()

    def planes(b):
        for i in range(4):
            for j, t in enumerate((fr.tiles - 1, 0)):
                m = i * fr.tiles + t
                at = pl.ds(((4 * b + i) * 2 + j) * SUB, SUB)
                part = z_part(info, n, received, b * (4 * fr.tiles // GROUP) + m // GROUP, m % GROUP, lane)
                tmp[at, :] = y_edge[at, :] + part

    loop(fr.live_x // 4, planes, 5)

    def plane(x):
        for i, slab in enumerate(slabs):
            first = x * 2 * SUB + pick(is_lower(info, 1, i), 0, SUB + MARGIN)
            slab[pl.ds(x * MARGIN, MARGIN), :] = tmp[pl.ds(first, MARGIN), :]

    loop(fr.live_x, plane, 8)


def fold_x(fr, info, x_edge, *rest):
    n1, n2 = fr.sides[1], fr.sides[2]
    z_in, y_in, slabs, tmp = rest[:n2], rest[n2 : n1 + n2], rest[n1 + n2 : -1], rest[-1]
    _, lane = iotas()
    by = fr.by
    for i, x in enumerate(edge_planes(fr)):
        for t in range(by // SUB):
            m = x * fr.tiles + t + 1
            a = slice(i * by + t * SUB, i * by + (t + 1) * SUB)
            tmp[a, :] = x_edge[a, :] + z_part(info, n2, z_in, m // GROUP, m % GROUP, lane)
        for k, buf in enumerate(y_in):
            a = pl.ds(i * by + pick(is_lower(info, 1, k), by - MARGIN, 0), MARGIN)
            tmp[a, :] = tmp[a, :] + buf[x * MARGIN : (x + 1) * MARGIN, :]
    count = MARGIN * by
    for i, slab in enumerate(slabs):
        slab[...] = tmp[pl.ds(pl.multiple_of(pick(is_lower(info, 0, i), 0, count), SUB), count), :]


def finish(fr, info, core, *rest):
    n0, n1, n2 = fr.sides
    z_in, y_in, x_in, out = rest[:n2], rest[n2 : n1 + n2], rest[n1 + n2 : -1], rest[-1]
    _, lane = iotas()
    by = fr.by

    def planes(b):
        for i in range(4):
            row = (4 * b + i) * by
            for t in range(by // SUB):
                m = i * fr.tiles + t + 1
                at = pl.ds(row + t * SUB, SUB)
                pack = (b + MARGIN // 4) * (4 * fr.tiles // GROUP) + m // GROUP
                out[at, :] = core[at, :] + z_part(info, n2, z_in, pack, m % GROUP, lane)
            for k, buf in enumerate(y_in):
                a = pl.ds(row + pick(is_lower(info, 1, k), by - MARGIN, 0), MARGIN)
                out[a, :] = out[a, :] + buf[pl.ds((4 * b + i + MARGIN) * MARGIN, MARGIN), :]

    loop(fr.bx // 4, planes, 4)
    count = MARGIN * by
    for i, buf in enumerate(x_in):
        a = pl.ds(pl.multiple_of(pick(is_lower(info, 0, i), (fr.bx - MARGIN) * by, 0), SUB), count)
        out[a, :] = out[a, :] + buf[...]


def local(
    forcing,
    kappa_base,
    labels,
    contrast,
    channel_weight,
    coarse_coef,
    source_link,
    offsets,
    live_pieces,
    resident_bases,
):
    bx, by, bz = forcing.shape
    axes = ("gx", "gy", "gz")
    fr = Frame(bx, by, bz, [lax.axis_size(a) for a in axes])
    slots, nb = resident_bases.shape[3], resident_bases.shape[4]
    nd = coarse_coef.shape[3]
    cells = PIECE**3
    part = functools.partial
    n0, n1, n2 = fr.sides
    live_rows = fr.live_blocks * SUB

    info = jnp.stack([live_pieces[0, 0, 0]] + [lax.axis_index(a).astype(jnp.int32) for a in axes])
    off = jnp.swapaxes(offsets.reshape(slots, 3), 0, 1)
    link = jnp.swapaxes(source_link.reshape(slots, 4), 0, 1)
    coef = jnp.swapaxes(coarse_coef.reshape(nd, nb), 0, 1)
    bases = resident_bases.reshape(slots, nb, cells)
    raw = [a.reshape(bx * by, bz) for a in (kappa_base, labels, forcing)]

    def stacked(own, received):
        return call(stack, rows_of(own.shape[0] * (1 + len(received))), [own, *received], limit=4)

    after_z = swap("gz", [coef] * n2)
    width = 2 * MARGIN + H
    slab = rows_of(width * by)
    slabs = call(
        part(static_x, fr),
        [slab] * n0,
        [info, contrast, channel_weight, *raw],
        [SMEM] + [HBM] * 5,
        [
            pltpu.VMEM((n0, H * by, LANES), F32),
            pltpu.VMEM((n0, H * by, LANES), jnp.int32),
            pltpu.SMEM((2, contrast.shape[0]), F32),
            pltpu.SemaphoreType.DMA((n0, 3)),
            pltpu.SemaphoreType.DMA((2,)),
        ],
    )
    after_z, slabs = lax.optimization_barrier((after_z, slabs))
    coef = stacked(coef, after_z)
    after_y = swap("gy", [coef] * n1)
    static_x_in = swap("gx", slabs)
    coef = stacked(coef, after_y)
    after_x = swap("gx", [coef] * n0)
    tables, raw, _ = lax.optimization_barrier((jnp.stack([contrast, channel_weight]), raw, slabs))
    slab = rows_of(fr.xf * width)
    k0, f0, w0, *slabs = call(
        part(static_y, fr),
        [fr.frame] * 3 + [slab] * n1,
        [info, tables, *raw, *static_x_in],
        [SMEM] * 2,
    )
    after_x, slabs = lax.optimization_barrier((after_x, slabs))
    static_y_in = swap("gy", slabs)

    together = 4 if slots % 4 == 0 else 1
    p0, p1, *slabs = call(
        part(prolong, fr, (nb, together)),
        [fr.frame] * 2 + [rows_of(live_rows)] * n2,
        [info, off, link, bases, coef, *after_x],
        [SMEM] * 3,
        [pltpu.VMEM((27, SUB, LANES), F32), pltpu.VMEM((together * CHUNKS // SUB, SUB, LANES), F32)],
        limit=16,
    )
    received = swap("gz", slabs)
    k0, f0, w0, *slabs = call(
        part(static_z, fr),
        [fr.frame] * 3 + [rows_of(fr.blocks * SUB)] * n2,
        [info, k0, f0, w0, *static_y_in],
        [SMEM],
        alias={1: 0, 2: 1, 3: 2},
    )
    received, slabs = lax.optimization_barrier((received, slabs))
    static_z_in = swap("gz", slabs)
    p0, p1, *slabs = call(
        part(coarse_y, fr),
        [fr.frame] * 2 + [rows_of(fr.live_x * (WIDE + 2))] * n1,
        [info, p0, p1, *received],
        [SMEM],
        alias={1: 0, 2: 1},
    )
    received = swap("gy", slabs)
    k1, f1, w1 = call(part(beyond, fr), [fr.frame] * 3, [info, *static_z_in], [SMEM])
    received, k1 = lax.optimization_barrier((received, k1))
    p0, p1, *slabs = call(
        part(coarse_x, fr),
        [fr.frame] * 2 + [rows_of(WIDE * fr.yf + -(-WIDE * fr.tiles // GROUP) * SUB)] * n0,
        [info, p0, p1, *received],
        [SMEM],
        alias={1: 0, 2: 1},
    )
    received = swap("gx", slabs)
    groups = slots // GROUP
    wt, scales, weights = call(
        part(couple, fr),
        [
            jax.ShapeDtypeStruct((groups, 6, PROWS, LANES), F32),
            jax.ShapeDtypeStruct((groups, PROWS, LANES), F32),
            jax.ShapeDtypeStruct((groups, PROWS, LANES), F32),
        ],
        [info, off, k0, k1, w0, w1],
        [SMEM] * 2,
        [pltpu.VMEM((PROWS + 2 * PIECE, LANES), F32)],
        limit=16,
    )

    solve = pltpu.VMEM((2, PROWS, LANES), F32)
    padded = pltpu.VMEM((2, PROWS + 2 * PIECE, LANES), F32)
    core, solved, y_edge, x_edge, slab = call(
        part(enrich, fr),
        [
            rows_of(bx * by),
            jax.ShapeDtypeStruct((groups, 2, PROWS, LANES), F32),
            rows_of(fr.live_x * 2 * SUB),
            rows_of(2 * MARGIN * by),
            rows_of(live_rows),
        ],
        [info, off, p0, p1, k0, f0, k1, f1, wt, scales, weights, *received],
        [SMEM] * 2,
        [pltpu.VMEM((fr.rows, LANES), F32)] * 6 + [pltpu.VMEM((PROWS, LANES), F32), solve, padded, padded, pltpu.VMEM((6, PROWS, LANES), F32)],
        limit=32,
    )

    z_in = swap("gz", [slab] * n2)
    basis = call(lay_out, rows_of(slots * CHUNKS * 2), [info, solved], [SMEM])
    z_in, basis = lax.optimization_barrier((z_in, basis))
    slabs = call(
        part(fold_y, fr),
        [rows_of(fr.live_x * MARGIN)] * n1,
        [info, y_edge, *z_in],
        [SMEM],
        [pltpu.VMEM((fr.live_x * 2 * SUB, LANES), F32)],
    )
    y_in = swap("gy", slabs)
    slabs = call(
        part(fold_x, fr),
        [rows_of(MARGIN * by)] * n0,
        [info, x_edge, *z_in, *y_in],
        [SMEM],
        [pltpu.VMEM((2 * MARGIN * by, LANES), F32)],
    )
    x_in = swap("gx", slabs)
    update = call(part(finish, fr), rows_of(bx * by), [info, core, *z_in, *y_in, *x_in], [SMEM])
    new_basis = basis.reshape(slots, CHUNKS, 2, LANES).swapaxes(1, 2)
    return update.reshape(bx, by, bz), new_basis.reshape(1, 1, 1, slots, 2, cells)


def solution(mesh):
    brick = ("gx", "gy", "gz")
    return jax.shard_map(
        local,
        mesh=mesh,
        in_specs=(
            P(*brick),
            P(*brick),
            P(*brick),
            P(),
            P(),
            P(*brick, None, None),
            P(*brick, None, None),
            P(*brick, None, None),
            P(*brick),
            P(*brick, None, None, None),
        ),
        out_specs=(P(*brick), P(*brick, None, None, None)),
        check_vma=False,
    )
```

```python
import functools

import jax
import jax.numpy as jnp
from jax import lax
from jax.experimental import pallas as pl
from jax.experimental.pallas import tpu as pltpu
from jax.sharding import PartitionSpec as P

MARGIN = 4
PIECE = 16
SWEEPS = 20
DAMPING = 2.0 / 3.0

H = MARGIN + 1
WIDE = 2 * MARGIN + 1
LANES = 128
SUB = 8
TOP = 8
GROUP = LANES // PIECE
HALVES = PIECE // SUB
CHUNKS = PIECE * HALVES
PROWS = PIECE * PIECE
F32 = jnp.float32


def iotas():
    shape = (SUB, LANES)
    return lax.broadcasted_iota(jnp.int32, shape, 0), lax.broadcasted_iota(jnp.int32, shape, 1)


def loop(count, body, unroll=1):
    while count % unroll:
        unroll -= 1

    def step(i, _):
        for j in range(unroll):
            body(i * unroll + j)
        return 0

    lax.fori_loop(0, count // unroll, step, 0)


def pick(flag, a, b):
    return jnp.where(flag, a, b)


def pack_tiles(tiles, shift, lane):
    packed = jnp.zeros((SUB, LANES), F32)
    for j, tile in enumerate(tiles):
        packed = jnp.where((lane >> 4) == j, pltpu.roll(tile, (shift + PIECE * j) % LANES, 1), packed)
    return packed


def unpack_tile(packed, j, shift):
    return pltpu.roll(packed, (shift - PIECE * j + 2 * LANES) % LANES, 1)


def sum_rows(values, sub):
    for k in (1, 2, 4):
        low = (sub & k) == 0
        values = [
            jnp.where(low, a, b) + pltpu.roll(jnp.where(low, b, a), SUB - k, 0)
            for a, b in zip(values[0::2], values[1::2])
        ]
    return values[0]


def block_transpose(values, sub, lane):
    for k in (4, 2, 1):
        in_group = ((lane >> 4) & k) != 0
        in_sub = (sub & k) != 0
        moves = in_sub != in_group
        if k == 4:
            others = [pltpu.roll(v, 64, 1) for v in values]
            others = [pltpu.roll(v, 4, 0) for v in others]
        else:
            pairs = [(pltpu.roll(v, PIECE * k, 1), pltpu.roll(v, LANES - PIECE * k, 1)) for v in values]
            others = [jnp.where(in_group, q, p) for q, p in pairs]
            others = [jnp.where(in_sub, pltpu.roll(m, k, 0), pltpu.roll(m, SUB - k, 0)) for m in others]
        values = [jnp.where(moves, o, v) for o, v in zip(others, values)]
    return values


class Frame:
    def __init__(self, bx, by, bz, counts):
        self.bx, self.by, self.bz = bx, by, bz
        self.xf = bx + 2 * H
        self.yf = by + 2 * TOP
        self.tiles = self.yf // SUB
        self.blocks = -(-self.xf * self.tiles // GROUP)
        self.rows = self.blocks * GROUP * SUB
        self.live_x = bx + 2 * MARGIN
        self.live_blocks = self.live_x * self.tiles // GROUP
        self.counts = counts
        self.sides = [1 if n == 2 else 2 for n in counts]

        per = by // SUB
        self.z_rows = bx * per // GROUP * SUB
        self.x_pack = (H + 1) * per // GROUP * SUB
        self.y_rows = -(-self.xf * (2 * MARGIN + H) // SUB) * SUB
        self.y_pack = -(-self.xf // GROUP) * SUB

    @property
    def frame(self):
        return rows_of(self.rows)


def rows_of(count):
    return jax.ShapeDtypeStruct((-(-count // SUB) * SUB, LANES), F32)


def zero(ref):
    ref[...] = jnp.zeros(ref.shape, ref.dtype)


VMEM = pl.BlockSpec(memory_space=pltpu.VMEM)
SMEM = pl.BlockSpec(memory_space=pltpu.SMEM)
HBM = pl.BlockSpec(memory_space=pltpu.HBM)
ANY = pl.BlockSpec(memory_space=pl.ANY)


def call(kernel, outs, ins, specs=(), scratch=(), alias=None, limit=12, out_spec=VMEM):
    specs = list(specs) + [VMEM] * (len(ins) - len(specs))
    return pl.pallas_call(
        kernel,
        out_shape=outs,
        in_specs=specs,
        out_specs=jax.tree.map(lambda _: out_spec, outs),
        scratch_shapes=list(scratch),
        input_output_aliases=alias or {},
        compiler_params=pltpu.CompilerParams(vmem_limit_bytes=limit * 1024 * 1024),
    )(*ins)


def is_lower(info, axis, phase):
    return ((info[1 + axis] + phase) & 1) == 0


def swap(axis, slabs):
    count = lax.axis_size(axis)
    received = []
    for phase, slab in enumerate(slabs):
        pairs = [(i, i + 1) for i in range(phase, count - 1, 2)]
        received.append(lax.ppermute(slab, axis, pairs + [(j, i) for i, j in pairs]))
    return received


def look_up(labels, values, which):
    out = jnp.zeros(labels.shape, F32)
    for c in range(values.shape[1]):
        out = out + jnp.where(labels == c, values[which, c], 0.0)
    return out


FIELDS = ((0, H, H, 0), (1, MARGIN, WIDE, H), (2, MARGIN, WIDE + MARGIN, WIDE))
FIRST = (0, H, H + MARGIN)
DEPTH = (H, MARGIN, MARGIN)
WIDTH = H + 2 * MARGIN


def static_first(fr, info, contrast, channel, kappa, labels, forcing, coef, offsets, links, *rest):
    n = fr.sides[2]
    (kap, frc, wgt, own, table), slabs = rest[:5], rest[5 : 5 + n]
    k_buf, l_buf, c_buf, o_buf, i_buf, t_buf, sem = rest[5 + n :]
    _, lane = iotas()
    moves = (
        (contrast, t_buf.at[0]),
        (channel, t_buf.at[1]),
        (labels, l_buf),
        (kappa, k_buf),
        (forcing, frc),
        (coef, c_buf),
        (offsets, o_buf),
        (links, i_buf),
    )
    copies = [pltpu.make_async_copy(src, dst, sem.at[i]) for i, (src, dst) in enumerate(moves)]
    for copy in copies:
        copy.start()
    zero(own)
    zero(table)
    for copy in copies:
        copy.wait()
    own[0 : coef.shape[0], 0 : coef.shape[1]] = c_buf[...]
    for i in range(3):
        table[i : i + 1, 0 : offsets.shape[2]] = o_buf[i]
    table[4:8, 0 : links.shape[1]] = i_buf[...]
    group = lane & (PIECE - 1)

    def block(b):
        tiles = [[], [], []]
        for j in range(GROUP):
            at = pl.ds((b * GROUP + j) * SUB, SUB)
            label = l_buf[at, :]
            k, w = k_buf[at, :] * look_up(label, t_buf, 0), look_up(label, t_buf, 1)
            kap[at, :] = k
            wgt[at, :] = w
            for some, v in zip(tiles, (k, frc[at, :], w)):
                some.append(v)
        for i, slab in enumerate(slabs):
            lower = is_lower(info, 2, i)
            packs = [pack_tiles(tiles[m], pick(lower, high, low), lane) for m, _, high, low in FIELDS]
            mix = jnp.where(group < H, packs[0], jnp.where(group < WIDE, packs[1], packs[2]))
            slab[pl.ds(b * SUB, SUB), :] = mix

    count = fr.bx * fr.by // (GROUP * SUB)
    loop(count, block, 2)
    for slab in slabs:
        slab[count * SUB : (count + 1) * SUB, :] = own[...]


def static_x(fr, info, kap, frc, wgt, own, *rest):
    n0, n2 = fr.sides[0], fr.sides[2]
    z_in, coefs, slabs = rest[:n2], rest[n2], rest[n2 + 1 :]
    by = fr.by
    coefs[0:SUB, :] = own[...]
    for s, buf in enumerate(z_in):
        coefs[(1 + s) * SUB : (2 + s) * SUB, :] = buf[fr.z_rows : fr.z_rows + SUB, :]
    for i, slab in enumerate(slabs):
        lower = is_lower(info, 0, i)
        for ref, at, count in zip((kap, frc, wgt), FIRST, DEPTH):
            first = pl.multiple_of(pick(lower, (fr.bx - count) * by, 0), SUB)
            slab[at * by : (at + count) * by, :] = ref[pl.ds(first, count * by), :]
        first = pl.multiple_of(pick(lower, fr.z_rows - fr.x_pack, 0), SUB)
        row = WIDTH * by
        for buf in z_in:
            slab[row : row + fr.x_pack, :] = buf[pl.ds(first, fr.x_pack), :]
            row += fr.x_pack
        slab[row : row + coefs.shape[0], :] = coefs[...]


def x_margin(fr, info, phase):
    lower = is_lower(info, 0, phase)
    return pick(lower, fr.bx + H, 0), pick(lower, 0, 1)


def static_y(fr, info, kap, frc, wgt, coefs_in, *rest):
    n0, n1, n2 = fr.sides
    z_in, x_in, (k0, f0, w0, coefs), rest = rest[:n2], rest[n2 : n0 + n2], rest[n0 + n2 : n0 + n2 + 4], rest[n0 + n2 + 4 :]
    slabs, tall = rest[:n1], rest[n1]
    _, lane = iotas()
    by, yf, per = fr.by, fr.yf, fr.by // SUB
    for ref in (k0, f0, w0):
        zero(ref)

    def core(x):
        for t in range(per):
            src = pl.ds(x * by + t * SUB, SUB)
            dst = pl.ds((x + H) * yf + TOP + t * SUB, SUB)
            for frame, ref in ((k0, kap), (f0, frc), (w0, wgt)):
                frame[dst, :] = ref[src, :]

    loop(fr.bx, core, 4)
    each = coefs_in.shape[0]
    coefs[0:each, :] = coefs_in[...]
    c_in = WIDTH * by + n2 * fr.x_pack
    for i, buf in enumerate(x_in):
        coefs[(1 + i) * each : (2 + i) * each, :] = buf[c_in : c_in + each, :]
        lower = is_lower(info, 0, i)
        for frame, count, at in zip((k0, f0, w0), DEPTH, FIRST):
            first = pick(lower, fr.bx + H, H - count)
            for j in range(count):
                for t in range(per):
                    row = (at + j) * by + t * SUB
                    frame[pl.ds(pl.multiple_of((first + j) * yf + TOP + t * SUB, SUB), SUB), :] = buf[row : row + SUB, :]

    def plane(x):
        r, o = x * yf, x * WIDTH
        for i, slab in enumerate(slabs):
            lower = is_lower(info, 1, i)
            for frame, count, at in zip((k0, f0, w0), DEPTH, FIRST):
                first = r + pick(lower, TOP + by - count, TOP)
                slab[pl.ds(o + at, count), :] = frame[pl.ds(first, count), :]

    loop(fr.xf, plane, 6)

    narrow = lane < PIECE
    for i, slab in enumerate(slabs):
        t = pick(is_lower(info, 1, i), per - 1, 0)
        row = fr.y_rows
        for s, buf in enumerate(z_in):
            zero(tall)
            for x in range(fr.bx):
                pack, group = x * per // GROUP, x * per % GROUP + t
                v = unpack_tile(buf[pack * SUB : (pack + 1) * SUB, :], group, 0)
                tall[(x + H) * SUB : (x + H + 1) * SUB, :] = jnp.where(narrow, v, 0.0)
            for k, part in enumerate(x_in):
                first, skip = x_margin(fr, info, k)
                for j in range(H):
                    at = (j + skip) * per
                    start = WIDTH * by + s * fr.x_pack + (at // GROUP) * SUB
                    v = unpack_tile(part[pl.ds(pl.multiple_of(start, SUB), SUB), :], at % GROUP + t, 0)
                    to = pl.multiple_of((first + j) * SUB, SUB)
                    tall[pl.ds(to, SUB), :] = jnp.where(narrow, v, 0.0)
            for b in range(fr.y_pack // SUB):
                tiles = [tall[(b * GROUP + j) * SUB : (b * GROUP + j + 1) * SUB, :] for j in range(GROUP)]
                slab[row : row + SUB, :] = pack_tiles(tiles, 0, lane)
                row += SUB
        slab[row : row + coefs.shape[0], :] = coefs[...]


def static_end(fr, info, k_in, f_in, w_in, *rest):
    n0, n1, n2 = fr.sides
    z_in, x_in, y_in = rest[:n2], rest[n2 : n0 + n2], rest[n0 + n2 : n0 + n1 + n2]
    k0, f0, w0, k1, f1, w1 = rest[n0 + n1 + n2 :]
    del k_in, f_in, w_in
    _, lane = iotas()
    by, yf, per = fr.by, fr.yf, fr.by // SUB

    def plane(x):
        r, o = x * yf, x * WIDTH
        for i, buf in enumerate(y_in):
            lower = is_lower(info, 1, i)
            for frame, count, at in zip((k0, f0, w0), DEPTH, FIRST):
                first = r + pick(lower, TOP + by, TOP - count)
                frame[pl.ds(first, count), :] = buf[pl.ds(o + at, count), :]

    loop(fr.xf, plane, 6)
    for ref in (k1, f1, w1):
        zero(ref)
    keeps, shifts = [], []
    for s in range(n2):
        lower = is_lower(info, 2, s)
        lows = [pick(lower, 0, LANES - width) for width in DEPTH]
        keeps.append([(lane >= low) & (lane < low + width) for low, width in zip(lows, DEPTH)])
        shifts.append([pick(lower, LANES - at, LANES - width - at) for at, width in zip(FIRST, DEPTH)])

    def put(row, packs, group):
        for m, ref in enumerate((k1, f1, w1)):
            value = 0.0
            for s, pack in enumerate(packs):
                value = value + jnp.where(keeps[s][m], unpack_tile(pack, group, shifts[s][m]), 0.0)
            ref[pl.ds(pl.multiple_of(row, SUB), SUB), :] = value

    def core(b):
        for i in range(4):
            at = i * per
            packs = [buf[pl.ds((b * 4 * per // GROUP + at // GROUP) * SUB, SUB), :] for buf in z_in]
            for t in range(per):
                put((4 * b + i + H) * yf + TOP + t * SUB, packs, at % GROUP + t)

    loop(fr.bx // 4, core, 2)
    for k, part in enumerate(x_in):
        first, skip = x_margin(fr, info, k)
        for j in range(H):
            at = (j + skip) * per
            starts = [WIDTH * by + s * fr.x_pack + (at // GROUP) * SUB for s in range(n2)]
            packs = [part[pl.ds(pl.multiple_of(start, SUB), SUB), :] for start in starts]
            for t in range(per):
                put((first + j) * yf + TOP + t * SUB, packs, at % GROUP + t)
    for i, part in enumerate(y_in):
        t = pick(is_lower(info, 1, i), fr.tiles - 1, 0)
        for x in range(fr.xf):
            starts = [fr.y_rows + s * fr.y_pack + x // GROUP * SUB for s in range(n2)]
            put(x * yf + t * SUB, [part[start : start + SUB, :] for start in starts], x % GROUP)


def place_masks(z0, lane):
    main = (lane >= z0) & (lane < z0 + PIECE)
    beyond = jnp.where(lane < LANES // 2, lane + LANES, lane - LANES)
    return main, (beyond >= z0) & (beyond < z0 + PIECE)


def corner(off, p):
    return off[0, p] + 1, off[1, p] + TOP - MARGIN, off[2, p] - MARGIN


def piece_rows(fr, off, p):
    x0, y0, _ = corner(off, p)
    base = x0 * fr.yf + y0
    return [pl.ds(base + (c // HALVES) * fr.yf + (c % HALVES) * SUB, SUB) for c in range(CHUNKS)]


def add_main(fr, off, p, valid, values, lane, ref):
    main, _ = place_masks(off[2, p] - MARGIN, lane)
    main = main & valid
    places = piece_rows(fr, off, p)
    new = [ref[a, :] + jnp.where(main, v, 0.0) for a, v in zip(places, values)]
    for a, v in zip(places, new):
        ref[a, :] = v


def add_beyond(fr, off, p, valid, get_values, lane, ref):
    z0 = off[2, p] - MARGIN

    @pl.when(valid & ((z0 < 0) | (z0 + PIECE > LANES)))
    def _():
        _, beyond = place_masks(z0, lane)
        places = piece_rows(fr, off, p)
        new = [ref[a, :] + jnp.where(beyond, v, 0.0) for a, v in zip(places, get_values())]
        for a, v in zip(places, new):
            ref[a, :] = v


def prolong(fr, shape, info, off, bases, own, *rest):
    nb, together = shape
    n, m = fr.sides[1], fr.sides[2]
    received, (p0, p1), slabs = rest[:n], rest[n : n + 2], rest[n + 2 : n + m + 2]
    table, keep, buf, sem = rest[n + m + 2 :]
    sub, lane = iotas()
    live = info[0]

    def copy(p):
        return pltpu.make_async_copy(bases.at[p], buf.at[p], sem.at[p])

    def start(p, _):
        copy(p).start()
        return 0

    lax.fori_loop(0, live, start, 0)
    zero(p0)
    zero(p1)
    each = (1 + fr.sides[0]) * (1 + m)
    for i, ref in enumerate((own, *received)):
        for j in range(each):
            row = j * SUB + (fr.y_rows + m * fr.y_pack if i else 0)
            table[i * each + j] = ref[row : row + SUB, :]

    def position(axis, step):
        came = 1 + ((info[1 + axis] + jnp.where(step == 0, 1, 0)) & 1)
        return jnp.where(step == 1, 0, came)

    def some(step, _):
        numbers = [step * together + i for i in range(together)]
        per = CHUNKS // SUB
        for p in numbers:

            @pl.when(p < live)
            def _():
                copy(p).wait()

        rows = []
        for p in numbers:
            at = [position(axis, off[4 + axis, p]) for axis in range(3)]
            row = table[(at[1] * (1 + fr.sides[0]) + at[0]) * (1 + m) + at[2]]
            coef = jnp.sum(jnp.where(lane == off[7, p], row, 0.0), axis=1, keepdims=True)
            coef = jnp.broadcast_to(coef, (SUB, LANES))[0:nb]
            for first in range(0, CHUNKS, SUB):
                parts = [buf[p, :, c * LANES : (c + 1) * LANES] * coef for c in range(first, first + SUB)]
                rows.append(sum_rows(parts, sub))
        rows = block_transpose(rows, sub, lane)
        for i, v in enumerate(rows):
            keep[i] = v

        def placed(i, p):
            z0 = off[2, p] - MARGIN
            return [
                pltpu.roll(keep[i * per + c // SUB], (z0 - PIECE * (c % SUB) + 2 * LANES) % LANES, 1)
                for c in range(CHUNKS)
            ]

        for i, p in enumerate(numbers):
            add_main(fr, off, p, p < live, placed(i, p), lane, p0)
        for i, p in enumerate(numbers):
            add_beyond(fr, off, p, p < live, functools.partial(placed, i, p), lane, p1)
        return 0

    lax.fori_loop(0, (live + together - 1) // together, some, 0)

    def block(b):
        tiles = []
        for j in range(GROUP):
            at = pl.ds(fr.yf + (b * GROUP + j) * SUB, SUB)
            tiles.append((p0[at, :], p1[at, :]))
        for i, slab in enumerate(slabs):
            lower = is_lower(info, 2, i)
            main = (lane >= LANES // 2) == lower
            near = [jnp.where(main, x, y) for x, y in tiles]
            slab[pl.ds(b * SUB, SUB), :] = pack_tiles(near, SUB, lane)

    loop(fr.live_blocks, block, 3)


def coarse_y(fr, info, p0_in, p1_in, *rest):
    n = fr.sides[2]
    received, (p0, p1), slabs = rest[:n], rest[n : n + 2], rest[n + 2 :]
    del p0_in, p1_in
    _, lane = iotas()
    packed = fr.live_x * WIDE

    def block(b):
        for i, buf in enumerate(received):
            lower = is_lower(info, 2, i)
            pack = buf[pl.ds(b * SUB, SUB), :]
            places = [pl.ds(fr.yf + (b * GROUP + j) * SUB, SUB) for j in range(GROUP)]
            values = [unpack_tile(pack, j, LANES - SUB) for j in range(GROUP)]
            to_main = ((lane >= LANES - SUB) & lower) | ((lane < SUB) & jnp.logical_not(lower))
            to_beyond = ((lane >= LANES - SUB) & jnp.logical_not(lower)) | ((lane < SUB) & lower)
            main = [p0[a, :] + jnp.where(to_main, v, 0.0) for a, v in zip(places, values)]
            beyond = [p1[a, :] + jnp.where(to_beyond, v, 0.0) for a, v in zip(places, values)]
            for a, v0, v1 in zip(places, main, beyond):
                p0[a, :] = v0
                p1[a, :] = v1

    loop(fr.live_blocks, block, 3)

    def plane(x):
        r = (x + 1) * fr.yf
        for i, slab in enumerate(slabs):
            first = r + pick(is_lower(info, 1, i), TOP + fr.by - H, TOP - MARGIN)
            slab[pl.ds(x * WIDE, WIDE), :] = p0[pl.ds(first, WIDE), :]

    loop(fr.live_x, plane, 8)

    def margin(b):
        for i, slab in enumerate(slabs):
            first = pick(is_lower(info, 1, i), fr.tiles - 2, 0)
            tiles = []
            for j in range(GROUP):
                row = (b * (GROUP // 2) + j // 2 + 1) * fr.yf + (first + j % 2) * SUB
                tiles.append(p1[pl.ds(row, SUB), :])
            slab[pl.ds(packed + b * SUB, SUB), :] = pack_tiles(tiles, SUB, lane)

    loop(fr.live_x * 2 // GROUP, margin, 5)


def coarse_x(fr, info, p0_in, p1_in, *rest):
    n = fr.sides[1]
    received, (p0, p1), slabs = rest[:n], rest[n : n + 2], rest[n + 2 :]
    del p0_in, p1_in
    _, lane = iotas()
    packed = fr.live_x * WIDE
    edge = (lane >= LANES - SUB) | (lane < SUB)

    def plane(x):
        r = (x + 1) * fr.yf
        for i, buf in enumerate(received):
            at = pl.ds(r + pick(is_lower(info, 1, i), TOP + fr.by - MARGIN, TOP - H), WIDE)
            p0[at, :] = p0[at, :] + buf[pl.ds(x * WIDE, WIDE), :]

    loop(fr.live_x, plane, 8)

    def margin(b):
        for i, buf in enumerate(received):
            first = pick(is_lower(info, 1, i), fr.tiles - 2, 0)
            pack = buf[pl.ds(packed + b * SUB, SUB), :]
            places = [
                pl.ds((b * (GROUP // 2) + j // 2 + 1) * fr.yf + (first + j % 2) * SUB, SUB) for j in range(GROUP)
            ]
            values = [jnp.where(edge, unpack_tile(pack, j, LANES - SUB), 0.0) for j in range(GROUP)]
            values = [p1[a, :] + v for a, v in zip(places, values)]
            for a, v in zip(places, values):
                p1[a, :] = v

    loop(fr.live_x * 2 // GROUP, margin, 5)
    main = WIDE * fr.yf
    for i, slab in enumerate(slabs):
        row = pl.multiple_of(pick(is_lower(info, 0, i), fr.xf - 1 - WIDE, 1) * fr.yf, SUB)
        slab[0:main, :] = p0[pl.ds(row, main), :]
        for b in range(-(-WIDE * fr.tiles // GROUP)):
            tiles = [p1[pl.ds(row + (b * GROUP + j) * SUB, SUB), :] for j in range(GROUP)]
            slab[main + b * SUB : main + (b + 1) * SUB, :] = pack_tiles(tiles, SUB, lane)


def gather_group(fr, off, first, live, fields, lane):
    places = []
    for g in range(GROUP):
        x0, y0, z0 = corner(off, first + g)
        slot = jnp.where(first + g < live, g, -1)
        places.append((x0 * fr.yf + y0, z0, (g * PIECE - z0 + LANES) % LANES, slot))

    def tiles_at(x, h):
        accs = [jnp.zeros((SUB, LANES), F32) for _ in fields]
        for base, z0, shift, slot in places:
            at = pl.ds(base + x * fr.yf + h * SUB, SUB)
            main = (lane >= z0) & (lane < z0 + PIECE)
            keep = (lane >> 4) == slot
            for j, (a, b) in enumerate(fields):
                v = pltpu.roll(jnp.where(main, a[at, :], b[at, :]), shift, 1)
                accs[j] = jnp.where(keep, v, accs[j])
        return accs

    return tiles_at


def couple(fr, info, off, k0, k1, w0, w1, wt, scales, weights, kb):
    sub, lane = iotas()
    live = info[0]
    first_y, last_y = sub == 0, sub == SUB - 1
    z_cell = lane & (PIECE - 1)
    zero(kb)

    def one_group(group, _):
        tiles_at = gather_group(fr, off, group * GROUP, live, ((k0, k1), (w0, w1)), lane)

        def gather(x):
            for h in range(HALVES):
                r = x * PIECE + h * SUB
                kb[pl.ds(PIECE + r, SUB), :], weights[group, pl.ds(r, SUB), :] = tiles_at(x, h)

        loop(PIECE, gather, 4)

        def setup(x):
            for h in range(HALVES):
                r = x * PIECE + h * SUB
                kc = kb[pl.ds(PIECE + r, SUB), :]
                kn = [kb[pl.ds(PIECE + r + d, SUB), :] for d in (PIECE, -PIECE, 1, -1)]
                kn += [pltpu.roll(kc, LANES - 1, 1), pltpu.roll(kc, 1, 1)]
                if h == HALVES - 1:
                    kn[2] = jnp.where(last_y, 0.0, kn[2])
                if h == 0:
                    kn[3] = jnp.where(first_y, 0.0, kn[3])
                kn[4] = jnp.where(z_cell == PIECE - 1, 0.0, kn[4])
                kn[5] = jnp.where(z_cell == 0, 0.0, kn[5])
                faces, diag = [], jnp.zeros((SUB, LANES), F32)
                for k in kn:
                    there = k > 0
                    half = 0.5 * (kc + k)
                    faces.append(jnp.where(there, half, 0.0))
                    diag = diag + jnp.where(there, half, kc)
                inside = kc > 0
                scale = jnp.where(inside, DAMPING / jnp.where(inside, diag, 1.0), 0.0)
                for j, face in enumerate(faces):
                    wt[group, j, pl.ds(r, SUB), :] = face * scale
                scales[group, pl.ds(r, SUB), :] = scale

        loop(PIECE, setup, 8)
        return 0

    lax.fori_loop(0, (live + GROUP - 1) // GROUP, one_group, 0)


def enrich(fr, info, off, p0, p1, k0, f0, k1, f1, wt, scales, weights, *rest):
    n0 = fr.sides[0]
    x_in, rest = rest[:n0], rest[n0:]
    core, solved, y_edge, x_edge, slab = rest[:5]
    c0, c1, r0, r1, q0, q1, rb, base, va, vb, here = rest[5:]
    sub, lane = iotas()
    yf, tiles = fr.yf, fr.tiles
    live = info[0]
    main_rows = WIDE * yf
    edge = (lane >= LANES - SUB) | (lane < SUB)

    c0[...] = p0[...]
    c1[...] = p1[...]
    for i, buf in enumerate(x_in):
        row = pl.multiple_of(pick(is_lower(info, 0, i), fr.xf - WIDE, 0) * yf, SUB)
        a = pl.ds(row, main_rows)
        c0[a, :] = c0[a, :] + buf[0:main_rows, :]
        for b in range(-(-WIDE * tiles // GROUP)):
            pack = buf[main_rows + b * SUB : main_rows + (b + 1) * SUB, :]
            count = min(GROUP, WIDE * tiles - b * GROUP)
            places = [pl.ds(row + (b * GROUP + j) * SUB, SUB) for j in range(count)]
            values = [jnp.where(edge, unpack_tile(pack, j, LANES - SUB), 0.0) for j in range(count)]
            for a, v in zip(places, [c1[a, :] + v for a, v in zip(places, values)]):
                c1[a, :] = v

    def mask(b):
        for j in range(GROUP):
            at = pl.ds((b * GROUP + j) * SUB, SUB)
            c0[at, :] = jnp.where(k0[at, :] > 0, c0[at, :], 0.0)
            c1[at, :] = jnp.where(k1[at, :] > 0, c1[at, :], 0.0)

    loop(fr.blocks, mask, 4)

    def next_z(a, b):
        return pltpu.roll(jnp.where(lane == 0, b, a), LANES - 1, 1)

    def last_z(a, b):
        return pltpu.roll(jnp.where(lane == LANES - 1, b, a), 1, 1)

    def at_edge(axis, count, first, last, position):
        low = (position == first) & (info[1 + axis] == 0)
        high = (position == last) & (info[1 + axis] == count - 1)
        return jnp.where(low, 1.0, 0.0) + jnp.where(high, 1.0, 0.0)

    out_y = [at_edge(1, fr.counts[1], TOP, TOP + fr.by - 1, sub + t * SUB) for t in range(tiles)]
    out_z = at_edge(2, fr.counts[2], 0, LANES - 1, lane)

    def flux_x(x):
        fluxes = []
        for t in range(tiles):
            at, to = pl.ds(x * yf + t * SUB, SUB), pl.ds((x + 1) * yf + t * SUB, SUB)
            fluxes += [(k[at, :] + k[to, :]) * (c[at, :] - c[to, :]) for c, k in ((c0, k0), (c1, k1))]
        return fluxes

    def residual(x, before):
        r = x * yf
        after = flux_x(x)
        out_x = at_edge(0, fr.counts[0], H, H + fr.bx - 1, x)
        last_y = [jnp.zeros((SUB, LANES), F32)] * 2
        for t in range(tiles):
            at, to = pl.ds(r + t * SUB, SUB), pl.ds(r + t * SUB + 1, SUB)
            cs, ks = (c0[at, :], c1[at, :]), (k0[at, :], k1[at, :])
            fz = []
            for i in range(2):
                cn, kn = next_z(cs[i], cs[1 - i]), next_z(ks[i], ks[1 - i])
                fz.append((ks[i] + kn) * (cs[i] - cn))
            for i, (c, k, f, out) in enumerate(((c0, k0, f0, r0), (c1, k1, f1, r1))):
                fy = pltpu.roll((ks[i] + k[to, :]) * (cs[i] - c[to, :]), 1, 0)
                fy_next = (ks[i] + k[to, :]) * (cs[i] - c[to, :])
                fy_last = jnp.where(sub == 0, last_y[i], fy)
                last_y[i] = fy
                outside = out_x + out_y[t] + (out_z if i == 0 else 0.0)
                total = (after[2 * t + i] - before[2 * t + i]) + (fy_next - fy_last)
                total = total + (fz[i] - last_z(fz[i], fz[1 - i])) + outside * (ks[i] * cs[i])
                out[at, :] = jnp.where(ks[i] > 0, f[at, :] - 0.5 * total, 0.0)
        return tuple(after)

    def residuals(i, before):
        for j in range(4):
            before = residual(4 * i + j + 1, before)
        return before

    lax.fori_loop(0, fr.live_x // 4, residuals, tuple(flux_x(0)))

    zero(q0)
    zero(q1)
    for ref in (va, vb):
        zero(ref)

    z_cell = lane & (PIECE - 1)
    tz = tent(z_cell.astype(F32))
    ty = [tent(sub.astype(F32) + float(SUB * h)) * tz for h in range(HALVES)]

    def one_group(group, _):
        first = group * GROUP
        tiles_at = gather_group(fr, off, first, live, ((r0, r1),), lane)

        def gather(x):
            for h in range(HALVES):
                r = x * PIECE + h * SUB
                at = pl.ds(r, SUB)
                s = tiles_at(x, h)[0] * scales[group, at, :]
                s2 = s * weights[group, at, :]
                for i, v in enumerate((s, s2)):
                    base[i, at, :] = v
                    va[i, pl.ds(PIECE + r, SUB), :] = v

        loop(PIECE, gather, 8)
        here[...] = wt[group]

        def sweep(src, dst, out=None):
            for x in range(PIECE):
                for h in range(HALVES):
                    r = x * PIECE + h * SUB
                    a = PIECE + r
                    w = [here[j, r : r + SUB, :] for j in range(6)]
                    for s in range(2):
                        v = src[s, a : a + SUB, :]
                        total = base[s, r : r + SUB, :] + v * (1.0 - DAMPING)
                        if x < PIECE - 1:
                            total = total + w[0] * src[s, a + PIECE : a + PIECE + SUB, :]
                        if x > 0:
                            total = total + w[1] * src[s, a - PIECE : a - PIECE + SUB, :]
                        total = total + w[2] * src[s, a + 1 : a + 1 + SUB, :]
                        total = total + w[3] * src[s, a - 1 : a - 1 + SUB, :]
                        total = total + w[4] * pltpu.roll(v, LANES - 1, 1)
                        total = total + w[5] * pltpu.roll(v, 1, 1)
                        if out is None:
                            dst[s, a : a + SUB, :] = total
                        else:
                            out[group, s, r : r + SUB, :] = total

        def two(i, _):
            sweep(va, vb)
            sweep(vb, va)
            return 0

        lax.fori_loop(0, (SWEEPS - 2) // 2, two, 0)
        if SWEEPS % 2:
            sweep(va, vb)
            sweep(vb, None, solved)
        else:
            sweep(va, None, solved)

        for c in range(CHUNKS):
            a = slice(c * SUB, (c + 1) * SUB)
            weight = ty[c % HALVES] * float(tent(c // HALVES))
            rb[a, :] = (solved[group, 0, a, :] + solved[group, 1, a, :]) * weight

        def placed(g):
            shift = (off[2, first + g] - MARGIN - g * PIECE + 2 * LANES) % LANES
            return [pltpu.roll(rb[c * SUB : (c + 1) * SUB, :], shift, 1) for c in range(CHUNKS)]

        for g in range(GROUP):
            add_main(fr, off, first + g, first + g < live, placed(g), lane, q0)
        for g in range(GROUP):
            add_beyond(fr, off, first + g, first + g < live, functools.partial(placed, g), lane, q1)
        return 0

    lax.fori_loop(0, (live + GROUP - 1) // GROUP, one_group, 0)

    def block(b):
        part = [q1[pl.ds(yf + (b * GROUP + j) * SUB, SUB), :] for j in range(GROUP)]
        slab[pl.ds(b * SUB, SUB), :] = pack_tiles(part, SUB, lane)

    loop(fr.live_blocks, block, 5)

    def core_rows(x):
        for t in range(fr.by // SUB):
            at = pl.ds((x + H) * yf + TOP + t * SUB, SUB)
            core[pl.ds(x * fr.by + t * SUB, SUB), :] = c0[at, :] + q0[at, :]

    loop(fr.bx, core_rows, 4)

    def edge_rows(x):
        for j, t in enumerate((tiles - 1, 0)):
            y_edge[pl.ds((2 * x + j) * SUB, SUB), :] = q0[pl.ds((x + 1) * yf + t * SUB, SUB), :]

    loop(fr.live_x, edge_rows, 8)
    for i, x in enumerate(edge_planes(fr)):
        row = (x + 1) * yf + TOP
        x_edge[i * fr.by : (i + 1) * fr.by, :] = q0[row : row + fr.by, :]


def tent(t):
    return (t + 0.5) * (PIECE - t - 0.5) * (4.0 / (PIECE * PIECE))


def lay_out(info, solved, basis, buf, sem):
    sub, lane = iotas()
    count = GROUP * CHUNKS * 2
    copies = []
    for group in range(solved.shape[0]):
        some = group * GROUP < info[0]

        @pl.when(some)
        def _():
            for c in range(0, CHUNKS, SUB):
                values = []
                for i in range(c, c + SUB):
                    values += [solved[group, s, i * SUB : (i + 1) * SUB, :] for s in range(2)]
                for i, v in enumerate(block_transpose(values, sub, lane)):
                    buf[group, pl.ds(c * 2 + i, GROUP, stride=CHUNKS * 2), :] = v

        @pl.when(jnp.logical_not(some))
        def _():
            buf[group] = jnp.zeros((count, LANES), F32)

        copies.append(pltpu.make_async_copy(buf.at[group], basis.at[pl.ds(group * count, count)], sem.at[group]))
        copies[-1].start()
    for copy in copies:
        copy.wait()


def edge_planes(fr):
    return [*range(fr.live_x - MARGIN, fr.live_x), *range(MARGIN)]


def z_part(info, sides, received, pack, j, lane):
    total = 0.0
    for i, buf in enumerate(received):
        lower = is_lower(info, 2, i)
        keep = ((lane >= LANES - SUB) & lower) | ((lane < SUB) & jnp.logical_not(lower))
        v = unpack_tile(buf[pl.ds(pack * SUB, SUB), :], j, LANES - SUB)
        total = total + jnp.where(keep, v, 0.0)
    return total


def fold_y(fr, info, y_edge, *rest):
    n = fr.sides[2]
    received, slabs, tmp = rest[:n], rest[n:-1], rest[-1]
    _, lane = iotas()

    def planes(b):
        for i in range(4):
            for j, t in enumerate((fr.tiles - 1, 0)):
                m = i * fr.tiles + t
                at = pl.ds(((4 * b + i) * 2 + j) * SUB, SUB)
                part = z_part(info, n, received, b * (4 * fr.tiles // GROUP) + m // GROUP, m % GROUP, lane)
                tmp[at, :] = y_edge[at, :] + part

    loop(fr.live_x // 4, planes, 5)

    def plane(x):
        for i, slab in enumerate(slabs):
            first = x * 2 * SUB + pick(is_lower(info, 1, i), 0, SUB + MARGIN)
            slab[pl.ds(x * MARGIN, MARGIN), :] = tmp[pl.ds(first, MARGIN), :]

    loop(fr.live_x, plane, 8)


def fold_x(fr, info, x_edge, *rest):
    n1, n2 = fr.sides[1], fr.sides[2]
    z_in, y_in, slabs, tmp = rest[:n2], rest[n2 : n1 + n2], rest[n1 + n2 : -1], rest[-1]
    _, lane = iotas()
    by = fr.by
    for i, x in enumerate(edge_planes(fr)):
        for t in range(by // SUB):
            m = x * fr.tiles + t + 1
            a = slice(i * by + t * SUB, i * by + (t + 1) * SUB)
            tmp[a, :] = x_edge[a, :] + z_part(info, n2, z_in, m // GROUP, m % GROUP, lane)
        for k, buf in enumerate(y_in):
            a = pl.ds(i * by + pick(is_lower(info, 1, k), by - MARGIN, 0), MARGIN)
            tmp[a, :] = tmp[a, :] + buf[x * MARGIN : (x + 1) * MARGIN, :]
    count = MARGIN * by
    for i, slab in enumerate(slabs):
        slab[...] = tmp[pl.ds(pl.multiple_of(pick(is_lower(info, 0, i), 0, count), SUB), count), :]


def finish(fr, info, core, *rest):
    n0, n1, n2 = fr.sides
    z_in, y_in, x_in, out = rest[:n2], rest[n2 : n1 + n2], rest[n1 + n2 : -1], rest[-1]
    _, lane = iotas()
    by = fr.by

    def planes(b):
        for i in range(4):
            row = (4 * b + i) * by
            for t in range(by // SUB):
                m = i * fr.tiles + t + 1
                at = pl.ds(row + t * SUB, SUB)
                pack = (b + MARGIN // 4) * (4 * fr.tiles // GROUP) + m // GROUP
                out[at, :] = core[at, :] + z_part(info, n2, z_in, pack, m % GROUP, lane)
            for k, buf in enumerate(y_in):
                a = pl.ds(row + pick(is_lower(info, 1, k), by - MARGIN, 0), MARGIN)
                out[a, :] = out[a, :] + buf[pl.ds((4 * b + i + MARGIN) * MARGIN, MARGIN), :]

    loop(fr.bx // 4, planes, 4)
    count = MARGIN * by
    for i, buf in enumerate(x_in):
        a = pl.ds(pl.multiple_of(pick(is_lower(info, 0, i), (fr.bx - MARGIN) * by, 0), SUB), count)
        out[a, :] = out[a, :] + buf[...]


def local(
    forcing,
    kappa_base,
    labels,
    contrast,
    channel_weight,
    coarse_coef,
    source_link,
    offsets,
    live_pieces,
    resident_bases,
):
    bx, by, bz = forcing.shape
    axes = ("gx", "gy", "gz")
    fr = Frame(bx, by, bz, [lax.axis_size(a) for a in axes])
    slots, nb = resident_bases.shape[3], resident_bases.shape[4]
    nd = coarse_coef.shape[3]
    cells = PIECE**3
    part = functools.partial
    n0, n1, n2 = fr.sides
    live_rows = fr.live_blocks * SUB

    info = jnp.stack([live_pieces[0, 0, 0]] + [lax.axis_index(a).astype(jnp.int32) for a in axes])

    def stays(a):
        return pltpu.with_memory_space_constraint(a, pltpu.HBM)

    raw = [stays(a.reshape(bx * by, bz)) for a in (kappa_base, labels, forcing)]
    raw += [
        stays(jnp.swapaxes(coarse_coef.reshape(nd, nb), 0, 1)),
        stays(jnp.swapaxes(offsets.reshape(slots, 1, 3), 0, 2).reshape(3, 1, slots)),
        stays(jnp.swapaxes(source_link.reshape(slots, 4), 0, 1)),
    ]
    bases = stays(resident_bases.reshape(slots, nb, cells))

    core = rows_of(bx * by)
    kap, frc, wgt, coefs, off, *slabs = call(
        part(static_first, fr),
        [core] * 3 + [rows_of(SUB), jax.ShapeDtypeStruct((SUB, LANES), jnp.int32)] + [rows_of(fr.z_rows + SUB)] * n2,
        [info, stays(contrast), stays(channel_weight), *raw],
        [SMEM] + [HBM] * 8,
        [
            pltpu.VMEM((bx * by, LANES), F32),
            pltpu.VMEM((bx * by, LANES), jnp.int32),
            pltpu.VMEM((nb, nd), F32),
            pltpu.VMEM((3, 1, slots), jnp.int32),
            pltpu.VMEM((4, slots), jnp.int32),
            pltpu.SMEM((2, contrast.shape[0]), F32),
            pltpu.SemaphoreType.DMA((8,)),
        ],
    )
    z_static = swap("gz", slabs)
    each = (1 + n2) * SUB
    coefs, *slabs = call(
        part(static_x, fr),
        [rows_of(each)] + [rows_of(WIDTH * by + n2 * fr.x_pack + each)] * n0,
        [info, kap, frc, wgt, coefs, *z_static],
        [SMEM],
    )
    x_static = swap("gx", slabs)
    each *= 1 + n0
    k0, f0, w0, coefs, *slabs = call(
        part(static_y, fr),
        [fr.frame] * 3 + [rows_of(each)] + [rows_of(fr.y_rows + n2 * fr.y_pack + each)] * n1,
        [info, kap, frc, wgt, coefs, *z_static, *x_static],
        [SMEM],
        [pltpu.VMEM((fr.y_pack * GROUP, LANES), F32)],
    )
    y_static = swap("gy", slabs)

    together = 4 if slots % 4 == 0 else 1
    p0, p1, *slabs = call(
        part(prolong, fr, (nb, together)),
        [fr.frame] * 2 + [rows_of(live_rows)] * n2,
        [info, off, bases, coefs, *y_static],
        [SMEM] * 2 + [HBM],
        [
            pltpu.VMEM((27, SUB, LANES), F32),
            pltpu.VMEM((together * CHUNKS // SUB, SUB, LANES), F32),
            pltpu.VMEM((slots, nb, cells), F32),
            pltpu.SemaphoreType.DMA((slots,)),
        ],
        limit=16,
    )
    received = swap("gz", slabs)
    k0, f0, w0, k1, f1, w1 = call(
        part(static_end, fr),
        [fr.frame] * 6,
        [info, k0, f0, w0, *z_static, *x_static, *y_static],
        [SMEM],
        alias={1: 0, 2: 1, 3: 2},
        limit=16,
    )
    received, k1 = lax.optimization_barrier((received, k1))
    p0, p1, *slabs = call(
        part(coarse_y, fr),
        [fr.frame] * 2 + [rows_of(fr.live_x * (WIDE + 2))] * n1,
        [info, p0, p1, *received],
        [SMEM],
        alias={1: 0, 2: 1},
    )
    received = swap("gy", slabs)
    groups = slots // GROUP
    wt, scales, weights = call(
        part(couple, fr),
        [
            jax.ShapeDtypeStruct((groups, 6, PROWS, LANES), F32),
            jax.ShapeDtypeStruct((groups, PROWS, LANES), F32),
            jax.ShapeDtypeStruct((groups, PROWS, LANES), F32),
        ],
        [info, off, k0, k1, w0, w1],
        [SMEM] * 2,
        [pltpu.VMEM((PROWS + 2 * PIECE, LANES), F32)],
        limit=16,
    )
    received, wt = lax.optimization_barrier((received, wt))
    p0, p1, *slabs = call(
        part(coarse_x, fr),
        [fr.frame] * 2 + [rows_of(WIDE * fr.yf + -(-WIDE * fr.tiles // GROUP) * SUB)] * n0,
        [info, p0, p1, *received],
        [SMEM],
        alias={1: 0, 2: 1},
    )
    received = swap("gx", slabs)

    solve = pltpu.VMEM((2, PROWS, LANES), F32)
    padded = pltpu.VMEM((2, PROWS + 2 * PIECE, LANES), F32)
    core, solved, y_edge, x_edge, slab = call(
        part(enrich, fr),
        [
            rows_of(bx * by),
            jax.ShapeDtypeStruct((groups, 2, PROWS, LANES), F32),
            rows_of(fr.live_x * 2 * SUB),
            rows_of(2 * MARGIN * by),
            rows_of(live_rows),
        ],
        [info, off, p0, p1, k0, f0, k1, f1, wt, scales, weights, *received],
        [SMEM] * 2,
        [pltpu.VMEM((fr.rows, LANES), F32)] * 6 + [pltpu.VMEM((PROWS, LANES), F32), solve, padded, padded, pltpu.VMEM((6, PROWS, LANES), F32)],
        limit=32,
    )

    z_in = swap("gz", [slab] * n2)
    basis = call(
        lay_out,
        rows_of(slots * CHUNKS * 2),
        [info, solved],
        [SMEM],
        [pltpu.VMEM((groups, GROUP * CHUNKS * 2, LANES), F32), pltpu.SemaphoreType.DMA((groups,))],
        out_spec=ANY,
    )
    z_in, basis = lax.optimization_barrier((z_in, basis))
    slabs = call(
        part(fold_y, fr),
        [rows_of(fr.live_x * MARGIN)] * n1,
        [info, y_edge, *z_in],
        [SMEM],
        [pltpu.VMEM((fr.live_x * 2 * SUB, LANES), F32)],
    )
    y_in = swap("gy", slabs)
    slabs = call(
        part(fold_x, fr),
        [rows_of(MARGIN * by)] * n0,
        [info, x_edge, *z_in, *y_in],
        [SMEM],
        [pltpu.VMEM((2 * MARGIN * by, LANES), F32)],
    )
    x_in = swap("gx", slabs)
    update = call(part(finish, fr), rows_of(bx * by), [info, core, *z_in, *y_in, *x_in], [SMEM])
    new_basis = basis.reshape(slots, CHUNKS, 2, LANES).swapaxes(1, 2)
    return update.reshape(bx, by, bz), new_basis.reshape(1, 1, 1, slots, 2, cells)


def solution(mesh):
    brick = ("gx", "gy", "gz")
    return jax.shard_map(
        local,
        mesh=mesh,
        in_specs=(
            P(*brick),
            P(*brick),
            P(*brick),
            P(),
            P(),
            P(*brick, None, None),
            P(*brick, None, None),
            P(*brick, None, None),
            P(*brick),
            P(*brick, None, None, None),
        ),
        out_specs=(P(*brick), P(*brick, None, None, None)),
        check_vma=False,
    )
```

```python
import functools

import jax
import jax.numpy as jnp
from jax import lax
from jax.experimental import pallas as pl
from jax.experimental.pallas import tpu as pltpu
from jax.sharding import PartitionSpec as P

MARGIN = 4
PIECE = 16
SWEEPS = 20
DAMPING = 2.0 / 3.0

H = MARGIN + 1
WIDE = 2 * MARGIN + 1
LANES = 128
SUB = 8
TOP = 8
GROUP = LANES // PIECE
HALVES = PIECE // SUB
CHUNKS = PIECE * HALVES
PROWS = PIECE * PIECE
F32 = jnp.float32


def iotas():
    shape = (SUB, LANES)
    return lax.broadcasted_iota(jnp.int32, shape, 0), lax.broadcasted_iota(jnp.int32, shape, 1)


def loop(count, body, unroll=1):
    while count % unroll:
        unroll -= 1

    def step(i, _):
        for j in range(unroll):
            body(i * unroll + j)
        return 0

    lax.fori_loop(0, count // unroll, step, 0)


def pick(flag, a, b):
    return jnp.where(flag, a, b)


def pack_tiles(tiles, shift, lane):
    packed = jnp.zeros((SUB, LANES), F32)
    for j, tile in enumerate(tiles):
        packed = jnp.where((lane >> 4) == j, pltpu.roll(tile, (shift + PIECE * j) % LANES, 1), packed)
    return packed


def unpack_tile(packed, j, shift):
    return pltpu.roll(packed, (shift - PIECE * j + 2 * LANES) % LANES, 1)


def sum_rows(values, sub):
    for k in (1, 2, 4):
        low = (sub & k) == 0
        values = [
            jnp.where(low, a, b) + pltpu.roll(jnp.where(low, b, a), SUB - k, 0)
            for a, b in zip(values[0::2], values[1::2])
        ]
    return values[0]


def block_transpose(values, sub, lane):
    for k in (4, 2, 1):
        in_group = ((lane >> 4) & k) != 0
        in_sub = (sub & k) != 0
        moves = in_sub != in_group
        if k == 4:
            others = [pltpu.roll(v, 64, 1) for v in values]
            others = [pltpu.roll(v, 4, 0) for v in others]
        else:
            pairs = [(pltpu.roll(v, PIECE * k, 1), pltpu.roll(v, LANES - PIECE * k, 1)) for v in values]
            others = [jnp.where(in_group, q, p) for q, p in pairs]
            others = [jnp.where(in_sub, pltpu.roll(m, k, 0), pltpu.roll(m, SUB - k, 0)) for m in others]
        values = [jnp.where(moves, o, v) for o, v in zip(others, values)]
    return values


class Frame:
    def __init__(self, bx, by, bz, counts):
        self.bx, self.by, self.bz = bx, by, bz
        self.xf = bx + 2 * H
        self.yf = by + 2 * TOP
        self.tiles = self.yf // SUB
        self.blocks = -(-self.xf * self.tiles // GROUP)
        self.rows = self.blocks * GROUP * SUB
        self.live_x = bx + 2 * MARGIN
        self.live_blocks = self.live_x * self.tiles // GROUP
        self.counts = counts
        self.sides = [1 if n == 2 else 2 for n in counts]

        per = by // SUB
        self.z_rows = bx * per // GROUP * SUB
        self.x_pack = (H + 1) * per // GROUP * SUB
        self.y_rows = -(-self.xf * (2 * MARGIN + H) // SUB) * SUB
        self.y_pack = -(-self.xf // GROUP) * SUB

    @property
    def frame(self):
        return rows_of(self.rows)


def rows_of(count):
    return jax.ShapeDtypeStruct((-(-count // SUB) * SUB, LANES), F32)


def zero(ref):
    ref[...] = jnp.zeros(ref.shape, ref.dtype)


VMEM = pl.BlockSpec(memory_space=pltpu.VMEM)
SMEM = pl.BlockSpec(memory_space=pltpu.SMEM)
HBM = pl.BlockSpec(memory_space=pltpu.HBM)
ANY = pl.BlockSpec(memory_space=pl.ANY)


def call(kernel, outs, ins, specs=(), scratch=(), alias=None, limit=12, out_spec=VMEM):
    specs = list(specs) + [VMEM] * (len(ins) - len(specs))
    return pl.pallas_call(
        kernel,
        out_shape=outs,
        in_specs=specs,
        out_specs=out_spec if isinstance(out_spec, list) else jax.tree.map(lambda _: out_spec, outs),
        scratch_shapes=list(scratch),
        input_output_aliases=alias or {},
        compiler_params=pltpu.CompilerParams(vmem_limit_bytes=limit * 1024 * 1024),
    )(*ins)


def is_lower(info, axis, phase):
    return ((info[1 + axis] + phase) & 1) == 0


def swap(axis, slabs):
    count = lax.axis_size(axis)
    received = []
    for phase, slab in enumerate(slabs):
        pairs = [(i, i + 1) for i in range(phase, count - 1, 2)]
        received.append(lax.ppermute(slab, axis, pairs + [(j, i) for i, j in pairs]))
    return received


def look_up(labels, values, which):
    out = jnp.zeros(labels.shape, F32)
    for c in range(values.shape[1]):
        out = out + jnp.where(labels == c, values[which, c], 0.0)
    return out


FIELDS = ((0, H, H, 0), (1, MARGIN, WIDE, H), (2, MARGIN, WIDE + MARGIN, WIDE))
FIRST = (0, H, H + MARGIN)
DEPTH = (H, MARGIN, MARGIN)
WIDTH = H + 2 * MARGIN


def static_first(fr, info, contrast, channel, kappa, labels, forcing, coef, offsets, links, *rest):
    n = fr.sides[2]
    (kap, frc, wgt, own, table), slabs = rest[:5], rest[5 : 5 + n]
    k_buf, l_buf, c_buf, o_buf, i_buf, t_buf, sem = rest[5 + n :]
    _, lane = iotas()
    moves = (
        (contrast, t_buf.at[0]),
        (channel, t_buf.at[1]),
        (labels, l_buf),
        (kappa, k_buf),
        (forcing, frc),
        (coef, c_buf),
        (offsets, o_buf),
        (links, i_buf),
    )
    copies = [pltpu.make_async_copy(src, dst, sem.at[i]) for i, (src, dst) in enumerate(moves)]
    for copy in copies:
        copy.start()
    zero(own)
    zero(table)
    for copy in copies:
        copy.wait()
    own[0 : coef.shape[0], 0 : coef.shape[1]] = c_buf[...]
    for i in range(3):
        table[i : i + 1, 0 : offsets.shape[2]] = o_buf[i]
    table[4:8, 0 : links.shape[1]] = i_buf[...]
    group = lane & (PIECE - 1)

    def block(b):
        tiles = [[], [], []]
        for j in range(GROUP):
            at = pl.ds((b * GROUP + j) * SUB, SUB)
            label = l_buf[at, :]
            k, w = k_buf[at, :] * look_up(label, t_buf, 0), look_up(label, t_buf, 1)
            kap[at, :] = k
            wgt[at, :] = w
            for some, v in zip(tiles, (k, frc[at, :], w)):
                some.append(v)
        for i, slab in enumerate(slabs):
            lower = is_lower(info, 2, i)
            packs = [pack_tiles(tiles[m], pick(lower, high, low), lane) for m, _, high, low in FIELDS]
            mix = jnp.where(group < H, packs[0], jnp.where(group < WIDE, packs[1], packs[2]))
            slab[pl.ds(b * SUB, SUB), :] = mix

    count = fr.bx * fr.by // (GROUP * SUB)
    loop(count, block, 4)
    for slab in slabs:
        slab[count * SUB : (count + 1) * SUB, :] = own[...]


def static_x(fr, info, kap, frc, wgt, own, *rest):
    n0, n2 = fr.sides[0], fr.sides[2]
    z_in, coefs, slabs = rest[:n2], rest[n2], rest[n2 + 1 :]
    by = fr.by
    coefs[0:SUB, :] = own[...]
    for s, buf in enumerate(z_in):
        coefs[(1 + s) * SUB : (2 + s) * SUB, :] = buf[fr.z_rows : fr.z_rows + SUB, :]
    for i, slab in enumerate(slabs):
        lower = is_lower(info, 0, i)
        for ref, at, count in zip((kap, frc, wgt), FIRST, DEPTH):
            first = pl.multiple_of(pick(lower, (fr.bx - count) * by, 0), SUB)
            slab[at * by : (at + count) * by, :] = ref[pl.ds(first, count * by), :]
        first = pl.multiple_of(pick(lower, fr.z_rows - fr.x_pack, 0), SUB)
        row = WIDTH * by
        for buf in z_in:
            slab[row : row + fr.x_pack, :] = buf[pl.ds(first, fr.x_pack), :]
            row += fr.x_pack
        slab[row : row + coefs.shape[0], :] = coefs[...]


def x_margin(fr, info, phase):
    lower = is_lower(info, 0, phase)
    return pick(lower, fr.bx + H, 0), pick(lower, 0, 1)


def stack(fr, own, *rest):
    x_in, out = rest[:-1], rest[-1]
    each = own.shape[0]
    out[0:each, :] = own[...]
    row = WIDTH * fr.by + fr.sides[2] * fr.x_pack
    for i, buf in enumerate(x_in):
        out[(1 + i) * each : (2 + i) * each, :] = buf[row : row + each, :]


def static_y(fr, info, kap, frc, wgt, *rest):
    n0, n1, n2 = fr.sides
    z_in, x_in, (k0, f0, w0), rest = rest[:n2], rest[n2 : n0 + n2], rest[n0 + n2 : n0 + n2 + 3], rest[n0 + n2 + 3 :]
    slabs, tall = rest[:n1], rest[n1]
    _, lane = iotas()
    by, yf, per = fr.by, fr.yf, fr.by // SUB
    for ref in (k0, f0, w0):
        zero(ref)

    def core(x):
        for t in range(per):
            src = pl.ds(x * by + t * SUB, SUB)
            dst = pl.ds((x + H) * yf + TOP + t * SUB, SUB)
            for frame, ref in ((k0, kap), (f0, frc), (w0, wgt)):
                frame[dst, :] = ref[src, :]

    loop(fr.bx, core, 4)
    for i, buf in enumerate(x_in):
        lower = is_lower(info, 0, i)
        for frame, count, at in zip((k0, f0, w0), DEPTH, FIRST):
            first = pick(lower, fr.bx + H, H - count)
            for j in range(count):
                for t in range(per):
                    row = (at + j) * by + t * SUB
                    frame[pl.ds(pl.multiple_of((first + j) * yf + TOP + t * SUB, SUB), SUB), :] = buf[row : row + SUB, :]

    def plane(x):
        r, o = x * yf, x * WIDTH
        for i, slab in enumerate(slabs):
            lower = is_lower(info, 1, i)
            for frame, count, at in zip((k0, f0, w0), DEPTH, FIRST):
                first = r + pick(lower, TOP + by - count, TOP)
                slab[pl.ds(o + at, count), :] = frame[pl.ds(first, count), :]

    loop(fr.xf, plane, 6)

    narrow = lane < PIECE
    for i, slab in enumerate(slabs):
        t = pick(is_lower(info, 1, i), per - 1, 0)
        row = fr.y_rows
        for s, buf in enumerate(z_in):
            zero(tall)
            for x in range(fr.bx):
                pack, group = x * per // GROUP, x * per % GROUP + t
                v = unpack_tile(buf[pack * SUB : (pack + 1) * SUB, :], group, 0)
                tall[(x + H) * SUB : (x + H + 1) * SUB, :] = jnp.where(narrow, v, 0.0)
            for k, part in enumerate(x_in):
                first, skip = x_margin(fr, info, k)
                for j in range(H):
                    at = (j + skip) * per
                    start = WIDTH * by + s * fr.x_pack + (at // GROUP) * SUB
                    v = unpack_tile(part[pl.ds(pl.multiple_of(start, SUB), SUB), :], at % GROUP + t, 0)
                    to = pl.multiple_of((first + j) * SUB, SUB)
                    tall[pl.ds(to, SUB), :] = jnp.where(narrow, v, 0.0)
            for b in range(fr.y_pack // SUB):
                tiles = [tall[(b * GROUP + j) * SUB : (b * GROUP + j + 1) * SUB, :] for j in range(GROUP)]
                slab[row : row + SUB, :] = pack_tiles(tiles, 0, lane)
                row += SUB


def static_end(fr, info, k_in, f_in, w_in, *rest):
    n0, n1, n2 = fr.sides
    z_in, x_in, y_in = rest[:n2], rest[n2 : n0 + n2], rest[n0 + n2 : n0 + n1 + n2]
    k0, f0, w0, k1, f1, w1 = rest[n0 + n1 + n2 :]
    del k_in, f_in, w_in
    _, lane = iotas()
    by, yf, per = fr.by, fr.yf, fr.by // SUB

    def plane(x):
        r, o = x * yf, x * WIDTH
        for i, buf in enumerate(y_in):
            lower = is_lower(info, 1, i)
            for frame, count, at in zip((k0, f0, w0), DEPTH, FIRST):
                first = r + pick(lower, TOP + by, TOP - count)
                frame[pl.ds(first, count), :] = buf[pl.ds(o + at, count), :]

    loop(fr.xf, plane, 6)
    for ref in (k1, f1, w1):
        zero(ref)
    keeps, shifts = [], []
    for s in range(n2):
        lower = is_lower(info, 2, s)
        lows = [pick(lower, 0, LANES - width) for width in DEPTH]
        keeps.append([(lane >= low) & (lane < low + width) for low, width in zip(lows, DEPTH)])
        shifts.append([pick(lower, LANES - at, LANES - width - at) for at, width in zip(FIRST, DEPTH)])

    def put(row, packs, group):
        for m, ref in enumerate((k1, f1, w1)):
            value = 0.0
            for s, pack in enumerate(packs):
                value = value + jnp.where(keeps[s][m], unpack_tile(pack, group, shifts[s][m]), 0.0)
            ref[pl.ds(pl.multiple_of(row, SUB), SUB), :] = value

    def core(b):
        for i in range(4):
            at = i * per
            packs = [buf[pl.ds((b * 4 * per // GROUP + at // GROUP) * SUB, SUB), :] for buf in z_in]
            for t in range(per):
                put((4 * b + i + H) * yf + TOP + t * SUB, packs, at % GROUP + t)

    loop(fr.bx // 4, core, 2)
    for k, part in enumerate(x_in):
        first, skip = x_margin(fr, info, k)
        for j in range(H):
            at = (j + skip) * per
            starts = [WIDTH * by + s * fr.x_pack + (at // GROUP) * SUB for s in range(n2)]
            packs = [part[pl.ds(pl.multiple_of(start, SUB), SUB), :] for start in starts]
            for t in range(per):
                put((first + j) * yf + TOP + t * SUB, packs, at % GROUP + t)
    for i, part in enumerate(y_in):
        t = pick(is_lower(info, 1, i), fr.tiles - 1, 0)
        for x in range(fr.xf):
            starts = [fr.y_rows + s * fr.y_pack + x // GROUP * SUB for s in range(n2)]
            put(x * yf + t * SUB, [part[start : start + SUB, :] for start in starts], x % GROUP)


def place_masks(z0, lane):
    main = (lane >= z0) & (lane < z0 + PIECE)
    beyond = jnp.where(lane < LANES // 2, lane + LANES, lane - LANES)
    return main, (beyond >= z0) & (beyond < z0 + PIECE)


def corner(off, p):
    return off[0, p] + 1, off[1, p] + TOP - MARGIN, off[2, p] - MARGIN


def piece_rows(fr, off, p):
    x0, y0, _ = corner(off, p)
    base = x0 * fr.yf + y0
    return [pl.ds(base + (c // HALVES) * fr.yf + (c % HALVES) * SUB, SUB) for c in range(CHUNKS)]


def add_main(fr, off, p, valid, values, lane, ref):
    main, _ = place_masks(off[2, p] - MARGIN, lane)
    main = main & valid
    places = piece_rows(fr, off, p)
    new = [ref[a, :] + jnp.where(main, v, 0.0) for a, v in zip(places, values)]
    for a, v in zip(places, new):
        ref[a, :] = v


def add_beyond(fr, off, p, valid, get_values, lane, ref):
    z0 = off[2, p] - MARGIN

    @pl.when(valid & ((z0 < 0) | (z0 + PIECE > LANES)))
    def _():
        _, beyond = place_masks(z0, lane)
        places = piece_rows(fr, off, p)
        new = [ref[a, :] + jnp.where(beyond, v, 0.0) for a, v in zip(places, get_values())]
        for a, v in zip(places, new):
            ref[a, :] = v


def fetch(info, bases, out, sem):
    def copy(p):
        return pltpu.make_async_copy(bases.at[p], out.at[p], sem.at[p])

    def start(p, _):
        copy(p).start()
        return 0

    def wait(p, _):
        copy(p).wait()
        return 0

    lax.fori_loop(0, info[0], start, 0)
    lax.fori_loop(0, info[0], wait, 0)


def prolong(fr, shape, info, off, bases, own, *rest):
    nb, together = shape
    n, m = fr.sides[1], fr.sides[2]
    received, (p0, p1), slabs = rest[:n], rest[n : n + 2], rest[n + 2 : n + m + 2]
    table, keep = rest[n + m + 2 :]
    sub, lane = iotas()
    live = info[0]
    zero(p0)
    zero(p1)
    each = (1 + fr.sides[0]) * (1 + m)
    for i, ref in enumerate((own, *received)):
        for j in range(each):
            table[i * each + j] = ref[j * SUB : (j + 1) * SUB, :]

    def position(axis, step):
        came = 1 + ((info[1 + axis] + jnp.where(step == 0, 1, 0)) & 1)
        return jnp.where(step == 1, 0, came)

    def some(step, _):
        numbers = [step * together + i for i in range(together)]
        per = CHUNKS // SUB
        rows = []
        for p in numbers:
            at = [position(axis, off[4 + axis, p]) for axis in range(3)]
            row = table[(at[1] * (1 + fr.sides[0]) + at[0]) * (1 + m) + at[2]]
            coef = jnp.sum(jnp.where(lane == off[7, p], row, 0.0), axis=1, keepdims=True)
            coef = jnp.broadcast_to(coef, (SUB, LANES))[0:nb]
            for first in range(0, CHUNKS, SUB):
                parts = [bases[p, :, c * LANES : (c + 1) * LANES] * coef for c in range(first, first + SUB)]
                rows.append(sum_rows(parts, sub))
        rows = block_transpose(rows, sub, lane)
        for i, v in enumerate(rows):
            keep[i] = v

        def placed(i, p):
            z0 = off[2, p] - MARGIN
            return [
                pltpu.roll(keep[i * per + c // SUB], (z0 - PIECE * (c % SUB) + 2 * LANES) % LANES, 1)
                for c in range(CHUNKS)
            ]

        for i, p in enumerate(numbers):
            add_main(fr, off, p, p < live, placed(i, p), lane, p0)
        for i, p in enumerate(numbers):
            add_beyond(fr, off, p, p < live, functools.partial(placed, i, p), lane, p1)
        return 0

    lax.fori_loop(0, (live + together - 1) // together, some, 0)

    def block(b):
        tiles = []
        for j in range(GROUP):
            at = pl.ds(fr.yf + (b * GROUP + j) * SUB, SUB)
            tiles.append((p0[at, :], p1[at, :]))
        for i, slab in enumerate(slabs):
            lower = is_lower(info, 2, i)
            main = (lane >= LANES // 2) == lower
            near = [jnp.where(main, x, y) for x, y in tiles]
            slab[pl.ds(b * SUB, SUB), :] = pack_tiles(near, SUB, lane)

    loop(fr.live_blocks, block, 3)


def coarse_y(fr, info, p0_in, p1_in, *rest):
    n = fr.sides[2]
    received, (p0, p1), slabs = rest[:n], rest[n : n + 2], rest[n + 2 :]
    del p0_in, p1_in
    _, lane = iotas()
    packed = fr.live_x * WIDE

    def block(b):
        for i, buf in enumerate(received):
            lower = is_lower(info, 2, i)
            pack = buf[pl.ds(b * SUB, SUB), :]
            places = [pl.ds(fr.yf + (b * GROUP + j) * SUB, SUB) for j in range(GROUP)]
            values = [unpack_tile(pack, j, LANES - SUB) for j in range(GROUP)]
            to_main = ((lane >= LANES - SUB) & lower) | ((lane < SUB) & jnp.logical_not(lower))
            to_beyond = ((lane >= LANES - SUB) & jnp.logical_not(lower)) | ((lane < SUB) & lower)
            main = [p0[a, :] + jnp.where(to_main, v, 0.0) for a, v in zip(places, values)]
            beyond = [p1[a, :] + jnp.where(to_beyond, v, 0.0) for a, v in zip(places, values)]
            for a, v0, v1 in zip(places, main, beyond):
                p0[a, :] = v0
                p1[a, :] = v1

    loop(fr.live_blocks, block, 3)

    def plane(x):
        r = (x + 1) * fr.yf
        for i, slab in enumerate(slabs):
            first = r + pick(is_lower(info, 1, i), TOP + fr.by - H, TOP - MARGIN)
            slab[pl.ds(x * WIDE, WIDE), :] = p0[pl.ds(first, WIDE), :]

    loop(fr.live_x, plane, 8)

    def margin(b):
        for i, slab in enumerate(slabs):
            first = pick(is_lower(info, 1, i), fr.tiles - 2, 0)
            tiles = []
            for j in range(GROUP):
                row = (b * (GROUP // 2) + j // 2 + 1) * fr.yf + (first + j % 2) * SUB
                tiles.append(p1[pl.ds(row, SUB), :])
            slab[pl.ds(packed + b * SUB, SUB), :] = pack_tiles(tiles, SUB, lane)

    loop(fr.live_x * 2 // GROUP, margin, 5)


def coarse_x(fr, info, p0_in, p1_in, *rest):
    n = fr.sides[1]
    received, (p0, p1), slabs = rest[:n], rest[n : n + 2], rest[n + 2 :]
    del p0_in, p1_in
    _, lane = iotas()
    packed = fr.live_x * WIDE
    edge = (lane >= LANES - SUB) | (lane < SUB)

    def plane(x):
        r = (x + 1) * fr.yf
        for i, buf in enumerate(received):
            at = pl.ds(r + pick(is_lower(info, 1, i), TOP + fr.by - MARGIN, TOP - H), WIDE)
            p0[at, :] = p0[at, :] + buf[pl.ds(x * WIDE, WIDE), :]

    loop(fr.live_x, plane, 8)

    def margin(b):
        for i, buf in enumerate(received):
            first = pick(is_lower(info, 1, i), fr.tiles - 2, 0)
            pack = buf[pl.ds(packed + b * SUB, SUB), :]
            places = [
                pl.ds((b * (GROUP // 2) + j // 2 + 1) * fr.yf + (first + j % 2) * SUB, SUB) for j in range(GROUP)
            ]
            values = [jnp.where(edge, unpack_tile(pack, j, LANES - SUB), 0.0) for j in range(GROUP)]
            values = [p1[a, :] + v for a, v in zip(places, values)]
            for a, v in zip(places, values):
                p1[a, :] = v

    loop(fr.live_x * 2 // GROUP, margin, 5)
    main = WIDE * fr.yf
    for i, slab in enumerate(slabs):
        row = pl.multiple_of(pick(is_lower(info, 0, i), fr.xf - 1 - WIDE, 1) * fr.yf, SUB)
        slab[0:main, :] = p0[pl.ds(row, main), :]
        for b in range(-(-WIDE * fr.tiles // GROUP)):
            tiles = [p1[pl.ds(row + (b * GROUP + j) * SUB, SUB), :] for j in range(GROUP)]
            slab[main + b * SUB : main + (b + 1) * SUB, :] = pack_tiles(tiles, SUB, lane)


def gather_group(fr, off, first, live, fields, lane):
    places = []
    for g in range(GROUP):
        x0, y0, z0 = corner(off, first + g)
        slot = jnp.where(first + g < live, g, -1)
        places.append((x0 * fr.yf + y0, z0, (g * PIECE - z0 + LANES) % LANES, slot))

    def tiles_at(x, h):
        accs = [jnp.zeros((SUB, LANES), F32) for _ in fields]
        for base, z0, shift, slot in places:
            at = pl.ds(base + x * fr.yf + h * SUB, SUB)
            main = (lane >= z0) & (lane < z0 + PIECE)
            keep = (lane >> 4) == slot
            for j, (a, b) in enumerate(fields):
                v = pltpu.roll(jnp.where(main, a[at, :], b[at, :]), shift, 1)
                accs[j] = jnp.where(keep, v, accs[j])
        return accs

    return tiles_at


def couple(fr, part, info, off, k0, k1, w0, w1, *rest):
    wt, scales, weights, kb = rest[-4:]
    sub, lane = iotas()
    live = info[0]
    first_y, last_y = sub == 0, sub == SUB - 1
    z_cell = lane & (PIECE - 1)
    zero(kb)

    def one_group(group, _):
        tiles_at = gather_group(fr, off, group * GROUP, live, ((k0, k1), (w0, w1)), lane)

        def gather(x):
            for h in range(HALVES):
                r = x * PIECE + h * SUB
                kb[pl.ds(PIECE + r, SUB), :], weights[group, pl.ds(r, SUB), :] = tiles_at(x, h)

        loop(PIECE, gather, 4)

        def setup(x):
            for h in range(HALVES):
                r = x * PIECE + h * SUB
                kc = kb[pl.ds(PIECE + r, SUB), :]
                kn = [kb[pl.ds(PIECE + r + d, SUB), :] for d in (PIECE, -PIECE, 1, -1)]
                kn += [pltpu.roll(kc, LANES - 1, 1), pltpu.roll(kc, 1, 1)]
                if h == HALVES - 1:
                    kn[2] = jnp.where(last_y, 0.0, kn[2])
                if h == 0:
                    kn[3] = jnp.where(first_y, 0.0, kn[3])
                kn[4] = jnp.where(z_cell == PIECE - 1, 0.0, kn[4])
                kn[5] = jnp.where(z_cell == 0, 0.0, kn[5])
                faces, diag = [], jnp.zeros((SUB, LANES), F32)
                for k in kn:
                    there = k > 0
                    half = 0.5 * (kc + k)
                    faces.append(jnp.where(there, half, 0.0))
                    diag = diag + jnp.where(there, half, kc)
                inside = kc > 0
                scale = jnp.where(inside, DAMPING / jnp.where(inside, diag, 1.0), 0.0)
                for j, face in enumerate(faces):
                    wt[group, j, pl.ds(r, SUB), :] = face * scale
                scales[group, pl.ds(r, SUB), :] = scale

        loop(PIECE, setup, 8)
        return 0

    lax.fori_loop(part[0], jnp.minimum((live + GROUP - 1) // GROUP, part[1]), one_group, 0)


def residuals(fr, info, cf, kf, ff, rf, first, count, unroll):
    sub, lane = iotas()
    yf, tiles = fr.yf, fr.tiles

    def next_z(a, b):
        return pltpu.roll(jnp.where(lane == 0, b, a), LANES - 1, 1)

    def last_z(a, b):
        return pltpu.roll(jnp.where(lane == LANES - 1, b, a), 1, 1)

    def at_edge(axis, count, first, last, position):
        low = (position == first) & (info[1 + axis] == 0)
        high = (position == last) & (info[1 + axis] == count - 1)
        return jnp.where(low, 1.0, 0.0) + jnp.where(high, 1.0, 0.0)

    out_y = [at_edge(1, fr.counts[1], TOP, TOP + fr.by - 1, sub + t * SUB) for t in range(tiles)]
    out_z = at_edge(2, fr.counts[2], 0, LANES - 1, lane)

    def flux_x(x):
        fluxes = []
        for t in range(tiles):
            at, to = pl.ds(x * yf + t * SUB, SUB), pl.ds((x + 1) * yf + t * SUB, SUB)
            fluxes += [(k[at, :] + k[to, :]) * (c[at, :] - c[to, :]) for c, k in zip(cf, kf)]
        return fluxes

    def residual(x, before):
        r = x * yf
        after = flux_x(x)
        out_x = at_edge(0, fr.counts[0], H, H + fr.bx - 1, x)
        last_y = [jnp.zeros((SUB, LANES), F32)] * 2
        for t in range(tiles):
            at, to = pl.ds(r + t * SUB, SUB), pl.ds(r + t * SUB + 1, SUB)
            cs, ks = (cf[0][at, :], cf[1][at, :]), (kf[0][at, :], kf[1][at, :])
            fz = []
            for i in range(2):
                cn, kn = next_z(cs[i], cs[1 - i]), next_z(ks[i], ks[1 - i])
                fz.append((ks[i] + kn) * (cs[i] - cn))
            for i, (c, k, f, out) in enumerate(zip(cf, kf, ff, rf)):
                fy = pltpu.roll((ks[i] + k[to, :]) * (cs[i] - c[to, :]), 1, 0)
                fy_next = (ks[i] + k[to, :]) * (cs[i] - c[to, :])
                fy_last = jnp.where(sub == 0, last_y[i], fy)
                last_y[i] = fy
                outside = out_x + out_y[t] + (out_z if i == 0 else 0.0)
                total = (after[2 * t + i] - before[2 * t + i]) + (fy_next - fy_last)
                total = total + (fz[i] - last_z(fz[i], fz[1 - i])) + outside * (ks[i] * cs[i])
                out[at, :] = jnp.where(ks[i] > 0, f[at, :] - 0.5 * total, 0.0)
        return tuple(after)

    def some(i, before):
        for j in range(unroll):
            before = residual(first + i * unroll + j, before)
        return before

    lax.fori_loop(0, count // unroll, some, tuple(flux_x(first - 1)))


def masked(fr, cf, kf, first, count):
    def plane(x):
        for t in range(fr.tiles):
            at = pl.ds((first + x) * fr.yf + t * SUB, SUB)
            for c, k in zip(cf, kf):
                c[at, :] = jnp.where(k[at, :] > 0, c[at, :], 0.0)

    loop(count, plane, 3)


def middle(fr, info, p0_in, p1_in, k0, f0, k1, f1, p0, p1, r0, r1):
    del p0_in, p1_in
    masked(fr, (p0, p1), (k0, k1), WIDE, fr.xf - 2 * WIDE)
    residuals(fr, info, (p0, p1), (k0, k1), (f0, f1), (r0, r1), WIDE + 2, fr.xf - 2 * WIDE - 4, 4)


def enrich(fr, info, off, p0, p1, r0_in, r1_in, k0, f0, k1, f1, wt, scales, weights, *rest):
    n0 = fr.sides[0]
    x_in, rest = rest[:n0], rest[n0:]
    c0, c1, r0, r1, core, solved, y_edge, x_edge, slab = rest[:9]
    q0, q1, rb, base, va, vb, here = rest[9:]
    del p0, p1, r0_in, r1_in
    sub, lane = iotas()
    yf, tiles = fr.yf, fr.tiles
    live = info[0]
    main_rows = WIDE * yf
    edge = (lane >= LANES - SUB) | (lane < SUB)

    for i, buf in enumerate(x_in):
        row = pl.multiple_of(pick(is_lower(info, 0, i), fr.xf - WIDE, 0) * yf, SUB)
        a = pl.ds(row, main_rows)
        c0[a, :] = c0[a, :] + buf[0:main_rows, :]
        for b in range(-(-WIDE * tiles // GROUP)):
            pack = buf[main_rows + b * SUB : main_rows + (b + 1) * SUB, :]
            count = min(GROUP, WIDE * tiles - b * GROUP)
            places = [pl.ds(row + (b * GROUP + j) * SUB, SUB) for j in range(count)]
            values = [jnp.where(edge, unpack_tile(pack, j, LANES - SUB), 0.0) for j in range(count)]
            for a, v in zip(places, [c1[a, :] + v for a, v in zip(places, values)]):
                c1[a, :] = v

    for first in (0, fr.xf - WIDE):
        masked(fr, (c0, c1), (k0, k1), first, WIDE)
    for first in (1, fr.xf - 1 - WIDE - 1):
        residuals(fr, info, (c0, c1), (k0, k1), (f0, f1), (r0, r1), first, WIDE + 1, 5)

    zero(q0)
    zero(q1)
    for ref in (va, vb):
        zero(ref)

    z_cell = lane & (PIECE - 1)
    tz = tent(z_cell.astype(F32))
    ty = [tent(sub.astype(F32) + float(SUB * h)) * tz for h in range(HALVES)]

    def one_group(group, _):
        first = group * GROUP
        tiles_at = gather_group(fr, off, first, live, ((r0, r1),), lane)

        def gather(x):
            for h in range(HALVES):
                r = x * PIECE + h * SUB
                at = pl.ds(r, SUB)
                s = tiles_at(x, h)[0] * scales[group, at, :]
                s2 = s * weights[group, at, :]
                for i, v in enumerate((s, s2)):
                    base[i, at, :] = v
                    va[i, pl.ds(PIECE + r, SUB), :] = v

        loop(PIECE, gather, 8)
        here[...] = wt[group]

        def sweep(src, dst, out=None):
            for x in range(PIECE):
                for h in range(HALVES):
                    r = x * PIECE + h * SUB
                    a = PIECE + r
                    w = [here[j, r : r + SUB, :] for j in range(6)]
                    for s in range(2):
                        v = src[s, a : a + SUB, :]
                        total = base[s, r : r + SUB, :] + v * (1.0 - DAMPING)
                        if x < PIECE - 1:
                            total = total + w[0] * src[s, a + PIECE : a + PIECE + SUB, :]
                        if x > 0:
                            total = total + w[1] * src[s, a - PIECE : a - PIECE + SUB, :]
                        total = total + w[2] * src[s, a + 1 : a + 1 + SUB, :]
                        total = total + w[3] * src[s, a - 1 : a - 1 + SUB, :]
                        total = total + w[4] * pltpu.roll(v, LANES - 1, 1)
                        total = total + w[5] * pltpu.roll(v, 1, 1)
                        if out is None:
                            dst[s, a : a + SUB, :] = total
                        else:
                            out[group, s, r : r + SUB, :] = total

        def two(i, _):
            sweep(va, vb)
            sweep(vb, va)
            return 0

        lax.fori_loop(0, (SWEEPS - 2) // 2, two, 0)
        if SWEEPS % 2:
            sweep(va, vb)
            sweep(vb, None, solved)
        else:
            sweep(va, None, solved)

        for c in range(CHUNKS):
            a = slice(c * SUB, (c + 1) * SUB)
            weight = ty[c % HALVES] * float(tent(c // HALVES))
            rb[a, :] = (solved[group, 0, a, :] + solved[group, 1, a, :]) * weight

        def placed(g):
            shift = (off[2, first + g] - MARGIN - g * PIECE + 2 * LANES) % LANES
            return [pltpu.roll(rb[c * SUB : (c + 1) * SUB, :], shift, 1) for c in range(CHUNKS)]

        for g in range(GROUP):
            add_main(fr, off, first + g, first + g < live, placed(g), lane, q0)
        for g in range(GROUP):
            add_beyond(fr, off, first + g, first + g < live, functools.partial(placed, g), lane, q1)
        return 0

    lax.fori_loop(0, (live + GROUP - 1) // GROUP, one_group, 0)

    def block(b):
        part = [q1[pl.ds(yf + (b * GROUP + j) * SUB, SUB), :] for j in range(GROUP)]
        slab[pl.ds(b * SUB, SUB), :] = pack_tiles(part, SUB, lane)

    loop(fr.live_blocks, block, 5)

    def core_rows(x):
        for t in range(fr.by // SUB):
            at = pl.ds((x + H) * yf + TOP + t * SUB, SUB)
            core[pl.ds(x * fr.by + t * SUB, SUB), :] = c0[at, :] + q0[at, :]

    loop(fr.bx, core_rows, 4)

    def edge_rows(x):
        for j, t in enumerate((tiles - 1, 0)):
            y_edge[pl.ds((2 * x + j) * SUB, SUB), :] = q0[pl.ds((x + 1) * yf + t * SUB, SUB), :]

    loop(fr.live_x, edge_rows, 8)
    for i, x in enumerate(edge_planes(fr)):
        row = (x + 1) * yf + TOP
        x_edge[i * fr.by : (i + 1) * fr.by, :] = q0[row : row + fr.by, :]


def tent(t):
    return (t + 0.5) * (PIECE - t - 0.5) * (4.0 / (PIECE * PIECE))


def lay_out(info, solved, basis, buf, sem):
    sub, lane = iotas()
    count = GROUP * CHUNKS * 2
    copies = []
    for group in range(solved.shape[0]):
        some = group * GROUP < info[0]

        @pl.when(some)
        def _():
            for c in range(0, CHUNKS, SUB):
                values = []
                for i in range(c, c + SUB):
                    values += [solved[group, s, i * SUB : (i + 1) * SUB, :] for s in range(2)]
                for i, v in enumerate(block_transpose(values, sub, lane)):
                    buf[group, pl.ds(c * 2 + i, GROUP, stride=CHUNKS * 2), :] = v

        @pl.when(jnp.logical_not(some))
        def _():
            buf[group] = jnp.zeros((count, LANES), F32)

        copies.append(pltpu.make_async_copy(buf.at[group], basis.at[pl.ds(group * count, count)], sem.at[group]))
        copies[-1].start()
    for copy in copies:
        copy.wait()


def edge_planes(fr):
    return [*range(fr.live_x - MARGIN, fr.live_x), *range(MARGIN)]


def z_part(info, sides, received, pack, j, lane):
    total = 0.0
    for i, buf in enumerate(received):
        lower = is_lower(info, 2, i)
        keep = ((lane >= LANES - SUB) & lower) | ((lane < SUB) & jnp.logical_not(lower))
        v = unpack_tile(buf[pl.ds(pack * SUB, SUB), :], j, LANES - SUB)
        total = total + jnp.where(keep, v, 0.0)
    return total


def fold_y(fr, info, y_edge, *rest):
    n = fr.sides[2]
    received, slabs, tmp = rest[:n], rest[n:-1], rest[-1]
    _, lane = iotas()

    def planes(b):
        for i in range(4):
            for j, t in enumerate((fr.tiles - 1, 0)):
                m = i * fr.tiles + t
                at = pl.ds(((4 * b + i) * 2 + j) * SUB, SUB)
                part = z_part(info, n, received, b * (4 * fr.tiles // GROUP) + m // GROUP, m % GROUP, lane)
                tmp[at, :] = y_edge[at, :] + part

    loop(fr.live_x // 4, planes, 5)

    def plane(x):
        for i, slab in enumerate(slabs):
            first = x * 2 * SUB + pick(is_lower(info, 1, i), 0, SUB + MARGIN)
            slab[pl.ds(x * MARGIN, MARGIN), :] = tmp[pl.ds(first, MARGIN), :]

    loop(fr.live_x, plane, 8)


def fold_x(fr, info, x_edge, *rest):
    n1, n2 = fr.sides[1], fr.sides[2]
    z_in, y_in, slabs, tmp = rest[:n2], rest[n2 : n1 + n2], rest[n1 + n2 : -1], rest[-1]
    _, lane = iotas()
    by = fr.by
    for i, x in enumerate(edge_planes(fr)):
        for t in range(by // SUB):
            m = x * fr.tiles + t + 1
            a = slice(i * by + t * SUB, i * by + (t + 1) * SUB)
            tmp[a, :] = x_edge[a, :] + z_part(info, n2, z_in, m // GROUP, m % GROUP, lane)
        for k, buf in enumerate(y_in):
            a = pl.ds(i * by + pick(is_lower(info, 1, k), by - MARGIN, 0), MARGIN)
            tmp[a, :] = tmp[a, :] + buf[x * MARGIN : (x + 1) * MARGIN, :]
    count = MARGIN * by
    for i, slab in enumerate(slabs):
        slab[...] = tmp[pl.ds(pl.multiple_of(pick(is_lower(info, 0, i), 0, count), SUB), count), :]


def finish(fr, info, core, *rest):
    n1, n2 = fr.sides[1:]
    z_in, y_in, (out, edges, buf, sem) = rest[:n2], rest[n2 : n1 + n2], rest[n1 + n2 :]
    _, lane = iotas()
    by = fr.by

    def planes(b):
        for i in range(4):
            row = (4 * b + i) * by
            for t in range(by // SUB):
                m = i * fr.tiles + t + 1
                at = pl.ds(row + t * SUB, SUB)
                pack = (b + MARGIN // 4) * (4 * fr.tiles // GROUP) + m // GROUP
                buf[at, :] = core[at, :] + z_part(info, n2, z_in, pack, m % GROUP, lane)
            for k, part in enumerate(y_in):
                a = pl.ds(row + pick(is_lower(info, 1, k), by - MARGIN, 0), MARGIN)
                buf[a, :] = buf[a, :] + part[pl.ds((4 * b + i + MARGIN) * MARGIN, MARGIN), :]

    loop(fr.bx // 4, planes, 4)
    count = MARGIN * by
    inner = pl.ds(count, fr.bx * by - 2 * count)
    copy = pltpu.make_async_copy(buf.at[inner], out.at[inner], sem)
    copy.start()
    edges[0:count, :] = buf[0:count, :]
    edges[count : 2 * count, :] = buf[fr.bx * by - count : fr.bx * by, :]
    copy.wait()


def finish_x(fr, info, out_in, edges, *rest):
    x_in, (out, buf, sem) = rest[:-3], rest[-3:]
    del out_in
    count = MARGIN * fr.by
    buf[...] = edges[...]
    for i, part in enumerate(x_in):
        a = pl.ds(pl.multiple_of(pick(is_lower(info, 0, i), count, 0), SUB), count)
        buf[a, :] = buf[a, :] + part[...]
    places = (0, fr.bx * fr.by - count)
    copies = [
        pltpu.make_async_copy(buf.at[pl.ds(i * count, count)], out.at[pl.ds(row, count)], sem.at[i])
        for i, row in enumerate(places)
    ]
    for copy in copies:
        copy.start()
    for copy in copies:
        copy.wait()


def local(
    forcing,
    kappa_base,
    labels,
    contrast,
    channel_weight,
    coarse_coef,
    source_link,
    offsets,
    live_pieces,
    resident_bases,
):
    bx, by, bz = forcing.shape
    axes = ("gx", "gy", "gz")
    fr = Frame(bx, by, bz, [lax.axis_size(a) for a in axes])
    slots, nb = resident_bases.shape[3], resident_bases.shape[4]
    nd = coarse_coef.shape[3]
    cells = PIECE**3
    part = functools.partial
    n0, n1, n2 = fr.sides
    live_rows = fr.live_blocks * SUB

    info = jnp.stack([live_pieces[0, 0, 0]] + [lax.axis_index(a).astype(jnp.int32) for a in axes])

    def stays(a):
        return pltpu.with_memory_space_constraint(a, pltpu.HBM)

    raw = [stays(a.reshape(bx * by, bz)) for a in (kappa_base, labels, forcing)]
    raw += [
        stays(jnp.swapaxes(coarse_coef.reshape(nd, nb), 0, 1)),
        stays(jnp.swapaxes(offsets.reshape(slots, 1, 3), 0, 2).reshape(3, 1, slots)),
        stays(jnp.swapaxes(source_link.reshape(slots, 4), 0, 1)),
    ]
    bases = stays(resident_bases.reshape(slots, nb, cells))

    core = rows_of(bx * by)
    kap, frc, wgt, coefs, off, *slabs = call(
        part(static_first, fr),
        [core] * 3 + [rows_of(SUB), jax.ShapeDtypeStruct((SUB, LANES), jnp.int32)] + [rows_of(fr.z_rows + SUB)] * n2,
        [info, stays(contrast), stays(channel_weight), *raw],
        [SMEM] + [HBM] * 8,
        [
            pltpu.VMEM((bx * by, LANES), F32),
            pltpu.VMEM((bx * by, LANES), jnp.int32),
            pltpu.VMEM((nb, nd), F32),
            pltpu.VMEM((3, 1, slots), jnp.int32),
            pltpu.VMEM((4, slots), jnp.int32),
            pltpu.SMEM((2, contrast.shape[0]), F32),
            pltpu.SemaphoreType.DMA((8,)),
        ],
    )
    z_static = swap("gz", slabs)
    each = (1 + n2) * SUB
    coefs, *slabs = call(
        part(static_x, fr),
        [rows_of(each)] + [rows_of(WIDTH * by + n2 * fr.x_pack + each)] * n0,
        [info, kap, frc, wgt, coefs, *z_static],
        [SMEM],
    )
    x_static = swap("gx", slabs)
    bases = call(fetch, jax.ShapeDtypeStruct(bases.shape, F32), [info, bases], [SMEM, HBM], [pltpu.SemaphoreType.DMA((slots,))], limit=8)
    x_static, bases = lax.optimization_barrier((x_static, bases))
    coefs = call(part(stack, fr), rows_of(each * (1 + n0)), [coefs, *x_static])
    y_coefs = swap("gy", [coefs] * n1)
    kap, coefs = lax.optimization_barrier((kap, coefs))
    k0, f0, w0, *slabs = call(
        part(static_y, fr),
        [fr.frame] * 3 + [rows_of(fr.y_rows + n2 * fr.y_pack)] * n1,
        [info, kap, frc, wgt, *z_static, *x_static],
        [SMEM],
        [pltpu.VMEM((fr.y_pack * GROUP, LANES), F32)],
    )
    slabs, y_coefs = lax.optimization_barrier((slabs, y_coefs))
    y_static = swap("gy", slabs)

    together = 4 if slots % 4 == 0 else 1
    p0, p1, *slabs = call(
        part(prolong, fr, (nb, together)),
        [fr.frame] * 2 + [rows_of(live_rows)] * n2,
        [info, off, bases, coefs, *y_coefs],
        [SMEM] * 2,
        [
            pltpu.VMEM((27, SUB, LANES), F32),
            pltpu.VMEM((together * CHUNKS // SUB, SUB, LANES), F32),
        ],
        limit=16,
    )
    received = swap("gz", slabs)
    k0, f0, w0, k1, f1, w1 = call(
        part(static_end, fr),
        [fr.frame] * 6,
        [info, k0, f0, w0, *z_static, *x_static, *y_static],
        [SMEM],
        alias={1: 0, 2: 1, 3: 2},
        limit=16,
    )
    received, k1 = lax.optimization_barrier((received, k1))
    p0, p1, *slabs = call(
        part(coarse_y, fr),
        [fr.frame] * 2 + [rows_of(fr.live_x * (WIDE + 2))] * n1,
        [info, p0, p1, *received],
        [SMEM],
        alias={1: 0, 2: 1},
    )
    received = swap("gy", slabs)
    groups = slots // GROUP
    split = (groups + 1) // 2
    setup = [
        jax.ShapeDtypeStruct((groups, 6, PROWS, LANES), F32),
        jax.ShapeDtypeStruct((groups, PROWS, LANES), F32),
        jax.ShapeDtypeStruct((groups, PROWS, LANES), F32),
    ]
    fields = [info, off, k0, k1, w0, w1]
    buffer = [pltpu.VMEM((PROWS + 2 * PIECE, LANES), F32)]
    setup = call(part(couple, fr, (0, split)), setup, fields, [SMEM] * 2, buffer, limit=16)
    received, setup = lax.optimization_barrier((received, setup))
    p0, p1, *slabs = call(
        part(coarse_x, fr),
        [fr.frame] * 2 + [rows_of(WIDE * fr.yf + -(-WIDE * fr.tiles // GROUP) * SUB)] * n0,
        [info, p0, p1, *received],
        [SMEM],
        alias={1: 0, 2: 1},
    )
    received = swap("gx", slabs)

    kinds = [jax.ShapeDtypeStruct(a.shape, F32) for a in setup]
    setup = call(
        part(couple, fr, (split, groups)),
        kinds,
        [*fields, *setup],
        [SMEM] * 2,
        buffer,
        alias={6: 0, 7: 1, 8: 2},
        limit=16,
    )
    p0, p1, r0, r1 = call(
        part(middle, fr), [fr.frame] * 4, [info, p0, p1, k0, f0, k1, f1], [SMEM], alias={1: 0, 2: 1}, limit=16
    )

    solve = pltpu.VMEM((2, PROWS, LANES), F32)
    padded = pltpu.VMEM((2, PROWS + 2 * PIECE, LANES), F32)
    _, _, _, _, core, solved, y_edge, x_edge, slab = call(
        part(enrich, fr),
        [fr.frame] * 4
        + [
            rows_of(bx * by),
            jax.ShapeDtypeStruct((groups, 2, PROWS, LANES), F32),
            rows_of(fr.live_x * 2 * SUB),
            rows_of(2 * MARGIN * by),
            rows_of(live_rows),
        ],
        [info, off, p0, p1, r0, r1, k0, f0, k1, f1, *setup, *received],
        [SMEM] * 2,
        [pltpu.VMEM((fr.rows, LANES), F32)] * 2 + [pltpu.VMEM((PROWS, LANES), F32), solve, padded, padded, pltpu.VMEM((6, PROWS, LANES), F32)],
        alias={2: 0, 3: 1, 4: 2, 5: 3},
        limit=32,
    )

    z_in = swap("gz", [slab] * n2)
    basis = call(
        lay_out,
        rows_of(slots * CHUNKS * 2),
        [info, solved],
        [SMEM],
        [pltpu.VMEM((groups, GROUP * CHUNKS * 2, LANES), F32), pltpu.SemaphoreType.DMA((groups,))],
        out_spec=ANY,
    )
    z_in, basis = lax.optimization_barrier((z_in, basis))
    slabs = call(
        part(fold_y, fr),
        [rows_of(fr.live_x * MARGIN)] * n1,
        [info, y_edge, *z_in],
        [SMEM],
        [pltpu.VMEM((fr.live_x * 2 * SUB, LANES), F32)],
    )
    y_in = swap("gy", slabs)
    slabs = call(
        part(fold_x, fr),
        [rows_of(MARGIN * by)] * n0,
        [info, x_edge, *z_in, *y_in],
        [SMEM],
        [pltpu.VMEM((2 * MARGIN * by, LANES), F32)],
    )
    x_in = swap("gx", slabs)
    edge = rows_of(2 * MARGIN * by)
    update, edges = call(
        part(finish, fr),
        [rows_of(bx * by), edge],
        [info, core, *z_in, *y_in],
        [SMEM],
        [pltpu.VMEM((bx * by, LANES), F32), pltpu.SemaphoreType.DMA],
        out_spec=[ANY, VMEM],
    )
    update = call(
        part(finish_x, fr),
        rows_of(bx * by),
        [info, update, edges, *x_in],
        [SMEM, ANY],
        [pltpu.VMEM(edge.shape, F32), pltpu.SemaphoreType.DMA((2,))],
        alias={1: 0},
        out_spec=ANY,
    )
    new_basis = basis.reshape(slots, CHUNKS, 2, LANES).swapaxes(1, 2)
    return update.reshape(bx, by, bz), new_basis.reshape(1, 1, 1, slots, 2, cells)


def solution(mesh):
    brick = ("gx", "gy", "gz")
    return jax.shard_map(
        local,
        mesh=mesh,
        in_specs=(
            P(*brick),
            P(*brick),
            P(*brick),
            P(),
            P(),
            P(*brick, None, None),
            P(*brick, None, None),
            P(*brick, None, None),
            P(*brick),
            P(*brick, None, None, None),
        ),
        out_specs=(P(*brick), P(*brick, None, None, None)),
        check_vma=False,
    )
```

```python
import functools

import jax
import jax.numpy as jnp
from jax import lax
from jax.experimental import pallas as pl
from jax.experimental.pallas import tpu as pltpu
from jax.sharding import PartitionSpec as P

MARGIN = 4
PIECE = 16
SWEEPS = 20
DAMPING = 2.0 / 3.0

H = MARGIN + 1
WIDE = 2 * MARGIN + 1
LANES = 128
SUB = 8
TOP = 8
GROUP = LANES // PIECE
HALVES = PIECE // SUB
CHUNKS = PIECE * HALVES
PROWS = PIECE * PIECE
F32 = jnp.float32


def iotas():
    shape = (SUB, LANES)
    return lax.broadcasted_iota(jnp.int32, shape, 0), lax.broadcasted_iota(jnp.int32, shape, 1)


def loop(count, body, unroll=1):
    while count % unroll:
        unroll -= 1

    def step(i, _):
        for j in range(unroll):
            body(i * unroll + j)
        return 0

    lax.fori_loop(0, count // unroll, step, 0)


def pick(flag, a, b):
    return jnp.where(flag, a, b)


def pack_tiles(tiles, shift, lane):
    packed = jnp.zeros((SUB, LANES), F32)
    for j, tile in enumerate(tiles):
        packed = jnp.where((lane >> 4) == j, pltpu.roll(tile, (shift + PIECE * j) % LANES, 1), packed)
    return packed


def unpack_tile(packed, j, shift):
    return pltpu.roll(packed, (shift - PIECE * j + 2 * LANES) % LANES, 1)


def sum_rows(values, sub):
    for k in (1, 2, 4):
        low = (sub & k) == 0
        values = [
            jnp.where(low, a, b) + pltpu.roll(jnp.where(low, b, a), SUB - k, 0)
            for a, b in zip(values[0::2], values[1::2])
        ]
    return values[0]


def block_transpose(values, sub, lane):
    for k in (4, 2, 1):
        in_group = ((lane >> 4) & k) != 0
        in_sub = (sub & k) != 0
        moves = in_sub != in_group
        if k == 4:
            others = [pltpu.roll(v, 64, 1) for v in values]
            others = [pltpu.roll(v, 4, 0) for v in others]
        else:
            pairs = [(pltpu.roll(v, PIECE * k, 1), pltpu.roll(v, LANES - PIECE * k, 1)) for v in values]
            others = [jnp.where(in_group, q, p) for q, p in pairs]
            others = [jnp.where(in_sub, pltpu.roll(m, k, 0), pltpu.roll(m, SUB - k, 0)) for m in others]
        values = [jnp.where(moves, o, v) for o, v in zip(others, values)]
    return values


class Frame:
    def __init__(self, bx, by, bz, counts):
        self.bx, self.by, self.bz = bx, by, bz
        self.xf = bx + 2 * H
        self.yf = by + 2 * TOP
        self.tiles = self.yf // SUB
        self.blocks = -(-self.xf * self.tiles // GROUP)
        self.rows = self.blocks * GROUP * SUB
        self.live_x = bx + 2 * MARGIN
        self.live_blocks = self.live_x * self.tiles // GROUP
        self.counts = counts
        self.sides = [1 if n == 2 else 2 for n in counts]

        per = by // SUB
        self.z_rows = bx * per // GROUP * SUB
        self.x_pack = (H + 1) * per // GROUP * SUB
        self.y_rows = -(-self.xf * (2 * MARGIN + H) // SUB) * SUB
        self.y_pack = -(-self.xf // GROUP) * SUB

    @property
    def frame(self):
        return rows_of(self.rows)


def rows_of(count):
    return jax.ShapeDtypeStruct((-(-count // SUB) * SUB, LANES), F32)


def zero(ref):
    ref[...] = jnp.zeros(ref.shape, ref.dtype)


VMEM = pl.BlockSpec(memory_space=pltpu.VMEM)
SMEM = pl.BlockSpec(memory_space=pltpu.SMEM)
HBM = pl.BlockSpec(memory_space=pltpu.HBM)
ANY = pl.BlockSpec(memory_space=pl.ANY)


def call(kernel, outs, ins, specs=(), scratch=(), alias=None, limit=12, out_spec=VMEM):
    specs = list(specs) + [VMEM] * (len(ins) - len(specs))
    return pl.pallas_call(
        kernel,
        out_shape=outs,
        in_specs=specs,
        out_specs=out_spec if isinstance(out_spec, list) else jax.tree.map(lambda _: out_spec, outs),
        scratch_shapes=list(scratch),
        input_output_aliases=alias or {},
        compiler_params=pltpu.CompilerParams(vmem_limit_bytes=limit * 1024 * 1024),
    )(*ins)


def is_lower(info, axis, phase):
    return ((info[1 + axis] + phase) & 1) == 0


def swap(axis, slabs):
    count = lax.axis_size(axis)
    received = []
    for phase, slab in enumerate(slabs):
        pairs = [(i, i + 1) for i in range(phase, count - 1, 2)]
        received.append(lax.ppermute(slab, axis, pairs + [(j, i) for i, j in pairs]))
    return received


def look_up(labels, values, which):
    out = jnp.zeros(labels.shape, F32)
    for c in range(values.shape[1]):
        out = out + jnp.where(labels == c, values[which, c], 0.0)
    return out


FIELDS = ((0, H, H, 0), (1, MARGIN, WIDE, H), (2, MARGIN, WIDE + MARGIN, WIDE))
FIRST = (0, H, H + MARGIN)
DEPTH = (H, MARGIN, MARGIN)
WIDTH = H + 2 * MARGIN


def static_first(fr, info, contrast, channel, kappa, labels, forcing, coef, offsets, links, *rest):
    n = fr.sides[2]
    (kap, frc, wgt, own, table), slabs = rest[:5], rest[5 : 5 + n]
    k_buf, l_buf, c_buf, o_buf, i_buf, t_buf, sem = rest[5 + n :]
    _, lane = iotas()
    half = fr.bx * fr.by // 2
    halves = [pl.ds(i * half, half) for i in range(2)]
    pairs = ((labels, l_buf), (kappa, k_buf), (forcing, frc))
    moves = [(contrast, t_buf.at[0]), (channel, t_buf.at[1])]
    for rows in halves:
        moves += [(src.at[rows], dst.at[rows]) for src, dst in pairs]
    moves += [(coef, c_buf), (offsets, o_buf), (links, i_buf)]
    copies = [pltpu.make_async_copy(src, dst, sem.at[i]) for i, (src, dst) in enumerate(moves)]
    for copy in copies:
        copy.start()
    zero(own)
    zero(table)
    for copy in copies[8:]:
        copy.wait()
    own[0 : coef.shape[0], 0 : coef.shape[1]] = c_buf[...]
    for i in range(3):
        table[i : i + 1, 0 : offsets.shape[2]] = o_buf[i]
    table[4:8, 0 : links.shape[1]] = i_buf[...]
    group = lane & (PIECE - 1)

    def block(b):
        tiles = [[], [], []]
        for j in range(GROUP):
            at = pl.ds((b * GROUP + j) * SUB, SUB)
            label = l_buf[at, :]
            k, w = k_buf[at, :] * look_up(label, t_buf, 0), look_up(label, t_buf, 1)
            kap[at, :] = k
            wgt[at, :] = w
            for some, v in zip(tiles, (k, frc[at, :], w)):
                some.append(v)
        for i, slab in enumerate(slabs):
            lower = is_lower(info, 2, i)
            packs = [pack_tiles(tiles[m], pick(lower, high, low), lane) for m, _, high, low in FIELDS]
            mix = jnp.where(group < H, packs[0], jnp.where(group < WIDE, packs[1], packs[2]))
            slab[pl.ds(b * SUB, SUB), :] = mix

    count = fr.bx * fr.by // (GROUP * SUB)
    for copy in copies[:5]:
        copy.wait()
    loop(count // 2, block, 8)
    for copy in copies[5:8]:
        copy.wait()
    loop(count // 2, lambda b: block(b + count // 2), 8)
    for slab in slabs:
        slab[count * SUB : (count + 1) * SUB, :] = own[...]


def static_x(fr, info, kap, frc, wgt, own, *rest):
    n0, n2 = fr.sides[0], fr.sides[2]
    z_in, coefs, slabs = rest[:n2], rest[n2], rest[n2 + 1 :]
    by = fr.by
    coefs[0:SUB, :] = own[...]
    for s, buf in enumerate(z_in):
        coefs[(1 + s) * SUB : (2 + s) * SUB, :] = buf[fr.z_rows : fr.z_rows + SUB, :]
    for i, slab in enumerate(slabs):
        lower = is_lower(info, 0, i)
        for ref, at, count in zip((kap, frc, wgt), FIRST, DEPTH):
            first = pl.multiple_of(pick(lower, (fr.bx - count) * by, 0), SUB)
            slab[at * by : (at + count) * by, :] = ref[pl.ds(first, count * by), :]
        first = pl.multiple_of(pick(lower, fr.z_rows - fr.x_pack, 0), SUB)
        row = WIDTH * by
        for buf in z_in:
            slab[row : row + fr.x_pack, :] = buf[pl.ds(first, fr.x_pack), :]
            row += fr.x_pack
        slab[row : row + coefs.shape[0], :] = coefs[...]


def x_margin(fr, info, phase):
    lower = is_lower(info, 0, phase)
    return pick(lower, fr.bx + H, 0), pick(lower, 0, 1)


def stack(fr, own, *rest):
    x_in, out = rest[:-1], rest[-1]
    each = own.shape[0]
    out[0:each, :] = own[...]
    row = WIDTH * fr.by + fr.sides[2] * fr.x_pack
    for i, buf in enumerate(x_in):
        out[(1 + i) * each : (2 + i) * each, :] = buf[row : row + each, :]


def static_y(fr, info, kap, frc, wgt, *rest):
    n0, n1, n2 = fr.sides
    z_in, x_in, (k0, f0, w0), rest = rest[:n2], rest[n2 : n0 + n2], rest[n0 + n2 : n0 + n2 + 3], rest[n0 + n2 + 3 :]
    slabs, tall = rest[:n1], rest[n1]
    _, lane = iotas()
    by, yf, per = fr.by, fr.yf, fr.by // SUB
    for ref in (k0, f0, w0):
        zero(ref)

    def core(x):
        for t in range(per):
            src = pl.ds(x * by + t * SUB, SUB)
            dst = pl.ds((x + H) * yf + TOP + t * SUB, SUB)
            for frame, ref in ((k0, kap), (f0, frc), (w0, wgt)):
                frame[dst, :] = ref[src, :]

    loop(fr.bx, core, 4)
    for i, buf in enumerate(x_in):
        lower = is_lower(info, 0, i)
        for frame, count, at in zip((k0, f0, w0), DEPTH, FIRST):
            first = pick(lower, fr.bx + H, H - count)
            for j in range(count):
                for t in range(per):
                    row = (at + j) * by + t * SUB
                    frame[pl.ds(pl.multiple_of((first + j) * yf + TOP + t * SUB, SUB), SUB), :] = buf[row : row + SUB, :]

    def plane(x):
        r, o = x * yf, x * WIDTH
        for i, slab in enumerate(slabs):
            lower = is_lower(info, 1, i)
            for frame, count, at in zip((k0, f0, w0), DEPTH, FIRST):
                first = r + pick(lower, TOP + by - count, TOP)
                slab[pl.ds(o + at, count), :] = frame[pl.ds(first, count), :]

    loop(fr.xf, plane, 6)

    narrow = lane < PIECE
    for i, slab in enumerate(slabs):
        t = pick(is_lower(info, 1, i), per - 1, 0)
        row = fr.y_rows
        for s, buf in enumerate(z_in):
            zero(tall)
            for x in range(fr.bx):
                pack, group = x * per // GROUP, x * per % GROUP + t
                v = unpack_tile(buf[pack * SUB : (pack + 1) * SUB, :], group, 0)
                tall[(x + H) * SUB : (x + H + 1) * SUB, :] = jnp.where(narrow, v, 0.0)
            for k, part in enumerate(x_in):
                first, skip = x_margin(fr, info, k)
                for j in range(H):
                    at = (j + skip) * per
                    start = WIDTH * by + s * fr.x_pack + (at // GROUP) * SUB
                    v = unpack_tile(part[pl.ds(pl.multiple_of(start, SUB), SUB), :], at % GROUP + t, 0)
                    to = pl.multiple_of((first + j) * SUB, SUB)
                    tall[pl.ds(to, SUB), :] = jnp.where(narrow, v, 0.0)
            for b in range(fr.y_pack // SUB):
                tiles = [tall[(b * GROUP + j) * SUB : (b * GROUP + j + 1) * SUB, :] for j in range(GROUP)]
                slab[row : row + SUB, :] = pack_tiles(tiles, 0, lane)
                row += SUB


def static_end(fr, info, k_in, f_in, w_in, *rest):
    n0, n1, n2 = fr.sides
    z_in, x_in, y_in = rest[:n2], rest[n2 : n0 + n2], rest[n0 + n2 : n0 + n1 + n2]
    k0, f0, w0, k1, f1, w1 = rest[n0 + n1 + n2 :]
    del k_in, f_in, w_in
    _, lane = iotas()
    by, yf, per = fr.by, fr.yf, fr.by // SUB

    def plane(x):
        r, o = x * yf, x * WIDTH
        for i, buf in enumerate(y_in):
            lower = is_lower(info, 1, i)
            for frame, count, at in zip((k0, f0, w0), DEPTH, FIRST):
                first = r + pick(lower, TOP + by, TOP - count)
                frame[pl.ds(first, count), :] = buf[pl.ds(o + at, count), :]

    loop(fr.xf, plane, 6)
    for ref in (k1, f1, w1):
        zero(ref)
    keeps, shifts = [], []
    for s in range(n2):
        lower = is_lower(info, 2, s)
        lows = [pick(lower, 0, LANES - width) for width in DEPTH]
        keeps.append([(lane >= low) & (lane < low + width) for low, width in zip(lows, DEPTH)])
        shifts.append([pick(lower, LANES - at, LANES - width - at) for at, width in zip(FIRST, DEPTH)])

    def put(row, packs, group):
        for m, ref in enumerate((k1, f1, w1)):
            value = 0.0
            for s, pack in enumerate(packs):
                value = value + jnp.where(keeps[s][m], unpack_tile(pack, group, shifts[s][m]), 0.0)
            ref[pl.ds(pl.multiple_of(row, SUB), SUB), :] = value

    def core(b):
        for i in range(4):
            at = i * per
            packs = [buf[pl.ds((b * 4 * per // GROUP + at // GROUP) * SUB, SUB), :] for buf in z_in]
            for t in range(per):
                put((4 * b + i + H) * yf + TOP + t * SUB, packs, at % GROUP + t)

    loop(fr.bx // 4, core, 2)
    for k, part in enumerate(x_in):
        first, skip = x_margin(fr, info, k)
        for j in range(H):
            at = (j + skip) * per
            starts = [WIDTH * by + s * fr.x_pack + (at // GROUP) * SUB for s in range(n2)]
            packs = [part[pl.ds(pl.multiple_of(start, SUB), SUB), :] for start in starts]
            for t in range(per):
                put((first + j) * yf + TOP + t * SUB, packs, at % GROUP + t)
    for i, part in enumerate(y_in):
        t = pick(is_lower(info, 1, i), fr.tiles - 1, 0)
        for x in range(fr.xf):
            starts = [fr.y_rows + s * fr.y_pack + x // GROUP * SUB for s in range(n2)]
            put(x * yf + t * SUB, [part[start : start + SUB, :] for start in starts], x % GROUP)


def place_masks(z0, lane):
    main = (lane >= z0) & (lane < z0 + PIECE)
    beyond = jnp.where(lane < LANES // 2, lane + LANES, lane - LANES)
    return main, (beyond >= z0) & (beyond < z0 + PIECE)


def corner(off, p):
    return off[0, p] + 1, off[1, p] + TOP - MARGIN, off[2, p] - MARGIN


def piece_rows(fr, off, p):
    x0, y0, _ = corner(off, p)
    base = x0 * fr.yf + y0
    return [pl.ds(base + (c // HALVES) * fr.yf + (c % HALVES) * SUB, SUB) for c in range(CHUNKS)]


def add_main(fr, off, p, valid, values, lane, ref):
    main, _ = place_masks(off[2, p] - MARGIN, lane)
    main = main & valid
    places = piece_rows(fr, off, p)
    new = [ref[a, :] + jnp.where(main, v, 0.0) for a, v in zip(places, values)]
    for a, v in zip(places, new):
        ref[a, :] = v


def add_beyond(fr, off, p, valid, get_values, lane, ref):
    z0 = off[2, p] - MARGIN

    @pl.when(valid & ((z0 < 0) | (z0 + PIECE > LANES)))
    def _():
        _, beyond = place_masks(z0, lane)
        places = piece_rows(fr, off, p)
        new = [ref[a, :] + jnp.where(beyond, v, 0.0) for a, v in zip(places, get_values())]
        for a, v in zip(places, new):
            ref[a, :] = v


def fetch(info, bases, out, sem):
    def copy(p):
        return pltpu.make_async_copy(bases.at[p], out.at[p], sem.at[p])

    def start(p, _):
        copy(p).start()
        return 0

    def wait(p, _):
        copy(p).wait()
        return 0

    lax.fori_loop(0, info[0], start, 0)
    lax.fori_loop(0, info[0], wait, 0)


def prolong(fr, shape, info, off, bases, own, *rest):
    nb, together = shape
    n, m = fr.sides[1], fr.sides[2]
    received, (p0, p1), slabs = rest[:n], rest[n : n + 2], rest[n + 2 : n + m + 2]
    table, keep = rest[n + m + 2 :]
    sub, lane = iotas()
    live = info[0]
    zero(p0)
    zero(p1)
    each = (1 + fr.sides[0]) * (1 + m)
    for i, ref in enumerate((own, *received)):
        for j in range(each):
            table[i * each + j] = ref[j * SUB : (j + 1) * SUB, :]

    def position(axis, step):
        came = 1 + ((info[1 + axis] + jnp.where(step == 0, 1, 0)) & 1)
        return jnp.where(step == 1, 0, came)

    def some(step, _):
        numbers = [step * together + i for i in range(together)]
        per = CHUNKS // SUB
        rows = []
        for p in numbers:
            at = [position(axis, off[4 + axis, p]) for axis in range(3)]
            row = table[(at[1] * (1 + fr.sides[0]) + at[0]) * (1 + m) + at[2]]
            coef = jnp.sum(jnp.where(lane == off[7, p], row, 0.0), axis=1, keepdims=True)
            coef = jnp.broadcast_to(coef, (SUB, LANES))[0:nb]
            for first in range(0, CHUNKS, SUB):
                parts = [bases[p, :, c * LANES : (c + 1) * LANES] * coef for c in range(first, first + SUB)]
                rows.append(sum_rows(parts, sub))
        rows = block_transpose(rows, sub, lane)
        for i, v in enumerate(rows):
            keep[i] = v

        def placed(i, p):
            z0 = off[2, p] - MARGIN
            return [
                pltpu.roll(keep[i * per + c // SUB], (z0 - PIECE * (c % SUB) + 2 * LANES) % LANES, 1)
                for c in range(CHUNKS)
            ]

        for i, p in enumerate(numbers):
            add_main(fr, off, p, p < live, placed(i, p), lane, p0)
        for i, p in enumerate(numbers):
            add_beyond(fr, off, p, p < live, functools.partial(placed, i, p), lane, p1)
        return 0

    lax.fori_loop(0, (live + together - 1) // together, some, 0)

    def block(b):
        tiles = []
        for j in range(GROUP):
            at = pl.ds(fr.yf + (b * GROUP + j) * SUB, SUB)
            tiles.append((p0[at, :], p1[at, :]))
        for i, slab in enumerate(slabs):
            lower = is_lower(info, 2, i)
            main = (lane >= LANES // 2) == lower
            near = [jnp.where(main, x, y) for x, y in tiles]
            slab[pl.ds(b * SUB, SUB), :] = pack_tiles(near, SUB, lane)

    loop(fr.live_blocks, block, 10)


def coarse_y(fr, info, p0_in, p1_in, *rest):
    n = fr.sides[2]
    received, (p0, p1), slabs = rest[:n], rest[n : n + 2], rest[n + 2 :]
    del p0_in, p1_in
    _, lane = iotas()
    packed = fr.live_x * WIDE

    def block(b):
        for i, buf in enumerate(received):
            lower = is_lower(info, 2, i)
            pack = buf[pl.ds(b * SUB, SUB), :]
            places = [pl.ds(fr.yf + (b * GROUP + j) * SUB, SUB) for j in range(GROUP)]
            values = [unpack_tile(pack, j, LANES - SUB) for j in range(GROUP)]
            to_main = ((lane >= LANES - SUB) & lower) | ((lane < SUB) & jnp.logical_not(lower))
            to_beyond = ((lane >= LANES - SUB) & jnp.logical_not(lower)) | ((lane < SUB) & lower)
            main = [p0[a, :] + jnp.where(to_main, v, 0.0) for a, v in zip(places, values)]
            beyond = [p1[a, :] + jnp.where(to_beyond, v, 0.0) for a, v in zip(places, values)]
            for a, v0, v1 in zip(places, main, beyond):
                p0[a, :] = v0
                p1[a, :] = v1

    loop(fr.live_blocks, block, 10)

    def plane(x):
        r = (x + 1) * fr.yf
        for i, slab in enumerate(slabs):
            first = r + pick(is_lower(info, 1, i), TOP + fr.by - H, TOP - MARGIN)
            slab[pl.ds(x * WIDE, WIDE), :] = p0[pl.ds(first, WIDE), :]

    loop(fr.live_x, plane, 8)

    def margin(b):
        for i, slab in enumerate(slabs):
            first = pick(is_lower(info, 1, i), fr.tiles - 2, 0)
            tiles = []
            for j in range(GROUP):
                row = (b * (GROUP // 2) + j // 2 + 1) * fr.yf + (first + j % 2) * SUB
                tiles.append(p1[pl.ds(row, SUB), :])
            slab[pl.ds(packed + b * SUB, SUB), :] = pack_tiles(tiles, SUB, lane)

    loop(fr.live_x * 2 // GROUP, margin, 5)


def coarse_x(fr, info, p0_in, p1_in, *rest):
    n = fr.sides[1]
    received, (p0, p1), slabs = rest[:n], rest[n : n + 2], rest[n + 2 :]
    del p0_in, p1_in
    _, lane = iotas()
    packed = fr.live_x * WIDE
    edge = (lane >= LANES - SUB) | (lane < SUB)

    def plane(x):
        r = (x + 1) * fr.yf
        for i, buf in enumerate(received):
            at = pl.ds(r + pick(is_lower(info, 1, i), TOP + fr.by - MARGIN, TOP - H), WIDE)
            p0[at, :] = p0[at, :] + buf[pl.ds(x * WIDE, WIDE), :]

    loop(fr.live_x, plane, 8)

    def margin(b):
        for i, buf in enumerate(received):
            first = pick(is_lower(info, 1, i), fr.tiles - 2, 0)
            pack = buf[pl.ds(packed + b * SUB, SUB), :]
            places = [
                pl.ds((b * (GROUP // 2) + j // 2 + 1) * fr.yf + (first + j % 2) * SUB, SUB) for j in range(GROUP)
            ]
            values = [jnp.where(edge, unpack_tile(pack, j, LANES - SUB), 0.0) for j in range(GROUP)]
            values = [p1[a, :] + v for a, v in zip(places, values)]
            for a, v in zip(places, values):
                p1[a, :] = v

    loop(fr.live_x * 2 // GROUP, margin, 5)
    main = WIDE * fr.yf
    for i, slab in enumerate(slabs):
        row = pl.multiple_of(pick(is_lower(info, 0, i), fr.xf - 1 - WIDE, 1) * fr.yf, SUB)
        slab[0:main, :] = p0[pl.ds(row, main), :]
        for b in range(-(-WIDE * fr.tiles // GROUP)):
            tiles = [p1[pl.ds(row + (b * GROUP + j) * SUB, SUB), :] for j in range(GROUP)]
            slab[main + b * SUB : main + (b + 1) * SUB, :] = pack_tiles(tiles, SUB, lane)


def gather_group(fr, off, first, live, fields, lane):
    places = []
    for g in range(GROUP):
        x0, y0, z0 = corner(off, first + g)
        slot = jnp.where(first + g < live, g, -1)
        places.append((x0 * fr.yf + y0, z0, (g * PIECE - z0 + LANES) % LANES, slot))

    def tiles_at(x, h):
        accs = [jnp.zeros((SUB, LANES), F32) for _ in fields]
        for base, z0, shift, slot in places:
            at = pl.ds(base + x * fr.yf + h * SUB, SUB)
            main = (lane >= z0) & (lane < z0 + PIECE)
            keep = (lane >> 4) == slot
            for j, (a, b) in enumerate(fields):
                v = pltpu.roll(jnp.where(main, a[at, :], b[at, :]), shift, 1)
                accs[j] = jnp.where(keep, v, accs[j])
        return accs

    return tiles_at


def couple(fr, part, info, off, k0, k1, w0, w1, *rest):
    wt, scales, weights, kb = rest[-4:]
    sub, lane = iotas()
    live = info[0]
    first_y, last_y = sub == 0, sub == SUB - 1
    z_cell = lane & (PIECE - 1)
    zero(kb)

    def one_group(group, _):
        tiles_at = gather_group(fr, off, group * GROUP, live, ((k0, k1), (w0, w1)), lane)

        def gather(x):
            for h in range(HALVES):
                r = x * PIECE + h * SUB
                kb[pl.ds(PIECE + r, SUB), :], weights[group, pl.ds(r, SUB), :] = tiles_at(x, h)

        loop(PIECE, gather, 8)

        def setup(x):
            for h in range(HALVES):
                r = x * PIECE + h * SUB
                kc = kb[pl.ds(PIECE + r, SUB), :]
                kn = [kb[pl.ds(PIECE + r + d, SUB), :] for d in (PIECE, -PIECE, 1, -1)]
                kn += [pltpu.roll(kc, LANES - 1, 1), pltpu.roll(kc, 1, 1)]
                if h == HALVES - 1:
                    kn[2] = jnp.where(last_y, 0.0, kn[2])
                if h == 0:
                    kn[3] = jnp.where(first_y, 0.0, kn[3])
                kn[4] = jnp.where(z_cell == PIECE - 1, 0.0, kn[4])
                kn[5] = jnp.where(z_cell == 0, 0.0, kn[5])
                faces, diag = [], jnp.zeros((SUB, LANES), F32)
                for k in kn:
                    there = k > 0
                    half = 0.5 * (kc + k)
                    faces.append(jnp.where(there, half, 0.0))
                    diag = diag + jnp.where(there, half, kc)
                inside = kc > 0
                scale = jnp.where(inside, DAMPING / jnp.where(inside, diag, 1.0), 0.0)
                for j, face in enumerate(faces):
                    wt[group, j, pl.ds(r, SUB), :] = face * scale
                scales[group, pl.ds(r, SUB), :] = scale

        loop(PIECE, setup, 8)
        return 0

    lax.fori_loop(part[0], jnp.minimum((live + GROUP - 1) // GROUP, part[1]), one_group, 0)


def residuals(fr, info, cf, kf, ff, rf, first, count, unroll):
    sub, lane = iotas()
    yf, tiles = fr.yf, fr.tiles

    def next_z(a, b):
        return pltpu.roll(jnp.where(lane == 0, b, a), LANES - 1, 1)

    def last_z(a, b):
        return pltpu.roll(jnp.where(lane == LANES - 1, b, a), 1, 1)

    def at_edge(axis, count, first, last, position):
        low = (position == first) & (info[1 + axis] == 0)
        high = (position == last) & (info[1 + axis] == count - 1)
        return jnp.where(low, 1.0, 0.0) + jnp.where(high, 1.0, 0.0)

    out_y = [at_edge(1, fr.counts[1], TOP, TOP + fr.by - 1, sub + t * SUB) for t in range(tiles)]
    out_z = at_edge(2, fr.counts[2], 0, LANES - 1, lane)

    def flux_x(x):
        fluxes = []
        for t in range(tiles):
            at, to = pl.ds(x * yf + t * SUB, SUB), pl.ds((x + 1) * yf + t * SUB, SUB)
            fluxes += [(k[at, :] + k[to, :]) * (c[at, :] - c[to, :]) for c, k in zip(cf, kf)]
        return fluxes

    def residual(x, before):
        r = x * yf
        after = flux_x(x)
        out_x = at_edge(0, fr.counts[0], H, H + fr.bx - 1, x)
        last_y = [jnp.zeros((SUB, LANES), F32)] * 2
        for t in range(tiles):
            at, to = pl.ds(r + t * SUB, SUB), pl.ds(r + t * SUB + 1, SUB)
            cs, ks = (cf[0][at, :], cf[1][at, :]), (kf[0][at, :], kf[1][at, :])
            fz = []
            for i in range(2):
                cn, kn = next_z(cs[i], cs[1 - i]), next_z(ks[i], ks[1 - i])
                fz.append((ks[i] + kn) * (cs[i] - cn))
            for i, (c, k, f, out) in enumerate(zip(cf, kf, ff, rf)):
                fy = pltpu.roll((ks[i] + k[to, :]) * (cs[i] - c[to, :]), 1, 0)
                fy_next = (ks[i] + k[to, :]) * (cs[i] - c[to, :])
                fy_last = jnp.where(sub == 0, last_y[i], fy)
                last_y[i] = fy
                outside = out_x + out_y[t] + (out_z if i == 0 else 0.0)
                total = (after[2 * t + i] - before[2 * t + i]) + (fy_next - fy_last)
                total = total + (fz[i] - last_z(fz[i], fz[1 - i])) + outside * (ks[i] * cs[i])
                out[at, :] = jnp.where(ks[i] > 0, f[at, :] - 0.5 * total, 0.0)
        return tuple(after)

    def some(i, before):
        for j in range(unroll):
            before = residual(first + i * unroll + j, before)
        return before

    lax.fori_loop(0, count // unroll, some, tuple(flux_x(first - 1)))


def masked(fr, cf, kf, first, count):
    def plane(x):
        for t in range(fr.tiles):
            at = pl.ds((first + x) * fr.yf + t * SUB, SUB)
            for c, k in zip(cf, kf):
                c[at, :] = jnp.where(k[at, :] > 0, c[at, :], 0.0)

    loop(count, plane, 3)


def middle(fr, info, p0_in, p1_in, k0, f0, k1, f1, p0, p1, r0, r1):
    del p0_in, p1_in
    masked(fr, (p0, p1), (k0, k1), WIDE, fr.xf - 2 * WIDE)
    residuals(fr, info, (p0, p1), (k0, k1), (f0, f1), (r0, r1), WIDE + 2, fr.xf - 2 * WIDE - 4, 4)


def enrich(fr, info, off, p0, p1, r0_in, r1_in, k0, f0, k1, f1, wt, scales, weights, *rest):
    n0 = fr.sides[0]
    x_in, rest = rest[:n0], rest[n0:]
    c0, c1, r0, r1, core, solved, y_edge, x_edge, slab = rest[:9]
    q0, q1, rb, base, va, vb, here = rest[9:]
    del p0, p1, r0_in, r1_in
    sub, lane = iotas()
    yf, tiles = fr.yf, fr.tiles
    live = info[0]
    main_rows = WIDE * yf
    edge = (lane >= LANES - SUB) | (lane < SUB)

    for i, buf in enumerate(x_in):
        row = pl.multiple_of(pick(is_lower(info, 0, i), fr.xf - WIDE, 0) * yf, SUB)
        a = pl.ds(row, main_rows)
        c0[a, :] = c0[a, :] + buf[0:main_rows, :]
        for b in range(-(-WIDE * tiles // GROUP)):
            pack = buf[main_rows + b * SUB : main_rows + (b + 1) * SUB, :]
            count = min(GROUP, WIDE * tiles - b * GROUP)
            places = [pl.ds(row + (b * GROUP + j) * SUB, SUB) for j in range(count)]
            values = [jnp.where(edge, unpack_tile(pack, j, LANES - SUB), 0.0) for j in range(count)]
            for a, v in zip(places, [c1[a, :] + v for a, v in zip(places, values)]):
                c1[a, :] = v

    for first in (0, fr.xf - WIDE):
        masked(fr, (c0, c1), (k0, k1), first, WIDE)
    for first in (1, fr.xf - 1 - WIDE - 1):
        residuals(fr, info, (c0, c1), (k0, k1), (f0, f1), (r0, r1), first, WIDE + 1, 5)

    zero(q0)
    zero(q1)
    for ref in (va, vb):
        zero(ref)

    z_cell = lane & (PIECE - 1)
    tz = tent(z_cell.astype(F32))
    ty = [tent(sub.astype(F32) + float(SUB * h)) * tz for h in range(HALVES)]

    def one_group(group, _):
        first = group * GROUP
        tiles_at = gather_group(fr, off, first, live, ((r0, r1),), lane)

        def gather(x):
            for h in range(HALVES):
                r = x * PIECE + h * SUB
                at = pl.ds(r, SUB)
                s = tiles_at(x, h)[0] * scales[group, at, :]
                s2 = s * weights[group, at, :]
                for i, v in enumerate((s, s2)):
                    base[i, at, :] = v
                    va[i, pl.ds(PIECE + r, SUB), :] = v

        loop(PIECE, gather, 16)
        here[...] = wt[group]

        def sweep(src, dst, out=None):
            for x in range(PIECE):
                for h in range(HALVES):
                    r = x * PIECE + h * SUB
                    a = PIECE + r
                    w = [here[j, r : r + SUB, :] for j in range(6)]
                    for s in range(2):
                        v = src[s, a : a + SUB, :]
                        total = base[s, r : r + SUB, :] + v * (1.0 - DAMPING)
                        if x < PIECE - 1:
                            total = total + w[0] * src[s, a + PIECE : a + PIECE + SUB, :]
                        if x > 0:
                            total = total + w[1] * src[s, a - PIECE : a - PIECE + SUB, :]
                        total = total + w[2] * src[s, a + 1 : a + 1 + SUB, :]
                        total = total + w[3] * src[s, a - 1 : a - 1 + SUB, :]
                        total = total + w[4] * pltpu.roll(v, LANES - 1, 1)
                        total = total + w[5] * pltpu.roll(v, 1, 1)
                        if out is None:
                            dst[s, a : a + SUB, :] = total
                        else:
                            out[group, s, r : r + SUB, :] = total

        def two(i, _):
            sweep(va, vb)
            sweep(vb, va)
            return 0

        lax.fori_loop(0, (SWEEPS - 2) // 2, two, 0)
        if SWEEPS % 2:
            sweep(va, vb)
            sweep(vb, None, solved)
        else:
            sweep(va, None, solved)

        for c in range(CHUNKS):
            a = slice(c * SUB, (c + 1) * SUB)
            weight = ty[c % HALVES] * float(tent(c // HALVES))
            rb[a, :] = (solved[group, 0, a, :] + solved[group, 1, a, :]) * weight

        def placed(g):
            shift = (off[2, first + g] - MARGIN - g * PIECE + 2 * LANES) % LANES
            return [pltpu.roll(rb[c * SUB : (c + 1) * SUB, :], shift, 1) for c in range(CHUNKS)]

        for g in range(GROUP):
            add_main(fr, off, first + g, first + g < live, placed(g), lane, q0)
        for g in range(GROUP):
            add_beyond(fr, off, first + g, first + g < live, functools.partial(placed, g), lane, q1)
        return 0

    lax.fori_loop(0, (live + GROUP - 1) // GROUP, one_group, 0)

    def block(b):
        part = [q1[pl.ds(yf + (b * GROUP + j) * SUB, SUB), :] for j in range(GROUP)]
        slab[pl.ds(b * SUB, SUB), :] = pack_tiles(part, SUB, lane)

    loop(fr.live_blocks, block, 10)

    def core_rows(x):
        for t in range(fr.by // SUB):
            at = pl.ds((x + H) * yf + TOP + t * SUB, SUB)
            core[pl.ds(x * fr.by + t * SUB, SUB), :] = c0[at, :] + q0[at, :]

    loop(fr.bx, core_rows, 8)

    def edge_rows(x):
        for j, t in enumerate((tiles - 1, 0)):
            y_edge[pl.ds((2 * x + j) * SUB, SUB), :] = q0[pl.ds((x + 1) * yf + t * SUB, SUB), :]

    loop(fr.live_x, edge_rows, 8)
    for i, x in enumerate(edge_planes(fr)):
        row = (x + 1) * yf + TOP
        x_edge[i * fr.by : (i + 1) * fr.by, :] = q0[row : row + fr.by, :]


def tent(t):
    return (t + 0.5) * (PIECE - t - 0.5) * (4.0 / (PIECE * PIECE))


def lay_out(info, solved, basis, buf, sem):
    sub, lane = iotas()
    count = GROUP * CHUNKS * 2
    copies = []
    for group in range(solved.shape[0]):
        some = group * GROUP < info[0]

        @pl.when(some)
        def _():
            for c in range(0, CHUNKS, SUB):
                values = []
                for i in range(c, c + SUB):
                    values += [solved[group, s, i * SUB : (i + 1) * SUB, :] for s in range(2)]
                for i, v in enumerate(block_transpose(values, sub, lane)):
                    buf[group, pl.ds(c * 2 + i, GROUP, stride=CHUNKS * 2), :] = v

        @pl.when(jnp.logical_not(some))
        def _():
            buf[group] = jnp.zeros((count, LANES), F32)

        copies.append(pltpu.make_async_copy(buf.at[group], basis.at[pl.ds(group * count, count)], sem.at[group]))
        copies[-1].start()
    for copy in copies:
        copy.wait()


def edge_planes(fr):
    return [*range(fr.live_x - MARGIN, fr.live_x), *range(MARGIN)]


def z_part(info, sides, received, pack, j, lane):
    total = 0.0
    for i, buf in enumerate(received):
        lower = is_lower(info, 2, i)
        keep = ((lane >= LANES - SUB) & lower) | ((lane < SUB) & jnp.logical_not(lower))
        v = unpack_tile(buf[pl.ds(pack * SUB, SUB), :], j, LANES - SUB)
        total = total + jnp.where(keep, v, 0.0)
    return total


def fold_y(fr, info, y_edge, *rest):
    n = fr.sides[2]
    received, slabs, tmp = rest[:n], rest[n:-1], rest[-1]
    _, lane = iotas()

    def planes(b):
        for i in range(4):
            for j, t in enumerate((fr.tiles - 1, 0)):
                m = i * fr.tiles + t
                at = pl.ds(((4 * b + i) * 2 + j) * SUB, SUB)
                part = z_part(info, n, received, b * (4 * fr.tiles // GROUP) + m // GROUP, m % GROUP, lane)
                tmp[at, :] = y_edge[at, :] + part

    loop(fr.live_x // 4, planes, 5)

    def plane(x):
        for i, slab in enumerate(slabs):
            first = x * 2 * SUB + pick(is_lower(info, 1, i), 0, SUB + MARGIN)
            slab[pl.ds(x * MARGIN, MARGIN), :] = tmp[pl.ds(first, MARGIN), :]

    loop(fr.live_x, plane, 8)


def fold_x(fr, info, x_edge, *rest):
    n1, n2 = fr.sides[1], fr.sides[2]
    z_in, y_in, slabs, tmp = rest[:n2], rest[n2 : n1 + n2], rest[n1 + n2 : -1], rest[-1]
    _, lane = iotas()
    by = fr.by
    for i, x in enumerate(edge_planes(fr)):
        for t in range(by // SUB):
            m = x * fr.tiles + t + 1
            a = slice(i * by + t * SUB, i * by + (t + 1) * SUB)
            tmp[a, :] = x_edge[a, :] + z_part(info, n2, z_in, m // GROUP, m % GROUP, lane)
        for k, buf in enumerate(y_in):
            a = pl.ds(i * by + pick(is_lower(info, 1, k), by - MARGIN, 0), MARGIN)
            tmp[a, :] = tmp[a, :] + buf[x * MARGIN : (x + 1) * MARGIN, :]
    count = MARGIN * by
    for i, slab in enumerate(slabs):
        slab[...] = tmp[pl.ds(pl.multiple_of(pick(is_lower(info, 0, i), 0, count), SUB), count), :]


def finish(fr, info, core, *rest):
    n1, n2 = fr.sides[1:]
    z_in, y_in, (out, edges, buf, sem) = rest[:n2], rest[n2 : n1 + n2], rest[n1 + n2 :]
    _, lane = iotas()
    by = fr.by

    def planes(b):
        for i in range(4):
            row = (4 * b + i) * by
            for t in range(by // SUB):
                m = i * fr.tiles + t + 1
                at = pl.ds(row + t * SUB, SUB)
                pack = (b + MARGIN // 4) * (4 * fr.tiles // GROUP) + m // GROUP
                buf[at, :] = core[at, :] + z_part(info, n2, z_in, pack, m % GROUP, lane)
            for k, part in enumerate(y_in):
                a = pl.ds(row + pick(is_lower(info, 1, k), by - MARGIN, 0), MARGIN)
                buf[a, :] = buf[a, :] + part[pl.ds((4 * b + i + MARGIN) * MARGIN, MARGIN), :]

    loop(fr.bx // 4, planes, 4)
    count = MARGIN * by
    inner = pl.ds(count, fr.bx * by - 2 * count)
    copy = pltpu.make_async_copy(buf.at[inner], out.at[inner], sem)
    copy.start()
    edges[0:count, :] = buf[0:count, :]
    edges[count : 2 * count, :] = buf[fr.bx * by - count : fr.bx * by, :]
    copy.wait()


def finish_x(fr, info, out_in, edges, *rest):
    x_in, (out, buf, sem) = rest[:-3], rest[-3:]
    del out_in
    count = MARGIN * fr.by
    buf[...] = edges[...]
    for i, part in enumerate(x_in):
        a = pl.ds(pl.multiple_of(pick(is_lower(info, 0, i), count, 0), SUB), count)
        buf[a, :] = buf[a, :] + part[...]
    places = (0, fr.bx * fr.by - count)
    copies = [
        pltpu.make_async_copy(buf.at[pl.ds(i * count, count)], out.at[pl.ds(row, count)], sem.at[i])
        for i, row in enumerate(places)
    ]
    for copy in copies:
        copy.start()
    for copy in copies:
        copy.wait()


def local(
    forcing,
    kappa_base,
    labels,
    contrast,
    channel_weight,
    coarse_coef,
    source_link,
    offsets,
    live_pieces,
    resident_bases,
):
    bx, by, bz = forcing.shape
    axes = ("gx", "gy", "gz")
    fr = Frame(bx, by, bz, [lax.axis_size(a) for a in axes])
    slots, nb = resident_bases.shape[3], resident_bases.shape[4]
    nd = coarse_coef.shape[3]
    cells = PIECE**3
    part = functools.partial
    n0, n1, n2 = fr.sides
    live_rows = fr.live_blocks * SUB

    info = jnp.stack([live_pieces[0, 0, 0]] + [lax.axis_index(a).astype(jnp.int32) for a in axes])

    def stays(a):
        return pltpu.with_memory_space_constraint(a, pltpu.HBM)

    raw = [stays(a.reshape(bx * by, bz)) for a in (kappa_base, labels, forcing)]
    raw += [
        stays(jnp.swapaxes(coarse_coef.reshape(nd, nb), 0, 1)),
        stays(jnp.swapaxes(offsets.reshape(slots, 1, 3), 0, 2).reshape(3, 1, slots)),
        stays(jnp.swapaxes(source_link.reshape(slots, 4), 0, 1)),
    ]
    bases = stays(resident_bases.reshape(slots, nb, cells))

    core = rows_of(bx * by)
    kap, frc, wgt, coefs, off, *slabs = call(
        part(static_first, fr),
        [core] * 3 + [rows_of(SUB), jax.ShapeDtypeStruct((SUB, LANES), jnp.int32)] + [rows_of(fr.z_rows + SUB)] * n2,
        [info, stays(contrast), stays(channel_weight), *raw],
        [SMEM] + [HBM] * 8,
        [
            pltpu.VMEM((bx * by, LANES), F32),
            pltpu.VMEM((bx * by, LANES), jnp.int32),
            pltpu.VMEM((nb, nd), F32),
            pltpu.VMEM((3, 1, slots), jnp.int32),
            pltpu.VMEM((4, slots), jnp.int32),
            pltpu.SMEM((2, contrast.shape[0]), F32),
            pltpu.SemaphoreType.DMA((11,)),
        ],
    )
    z_static = swap("gz", slabs)
    each = (1 + n2) * SUB
    coefs, *slabs = call(
        part(static_x, fr),
        [rows_of(each)] + [rows_of(WIDTH * by + n2 * fr.x_pack + each)] * n0,
        [info, kap, frc, wgt, coefs, *z_static],
        [SMEM],
    )
    x_static = swap("gx", slabs)
    bases = call(fetch, jax.ShapeDtypeStruct(bases.shape, F32), [info, bases], [SMEM, HBM], [pltpu.SemaphoreType.DMA((slots,))], limit=8)
    x_static, bases = lax.optimization_barrier((x_static, bases))
    coefs = call(part(stack, fr), rows_of(each * (1 + n0)), [coefs, *x_static])
    y_coefs = swap("gy", [coefs] * n1)
    kap, coefs = lax.optimization_barrier((kap, coefs))
    k0, f0, w0, *slabs = call(
        part(static_y, fr),
        [fr.frame] * 3 + [rows_of(fr.y_rows + n2 * fr.y_pack)] * n1,
        [info, kap, frc, wgt, *z_static, *x_static],
        [SMEM],
        [pltpu.VMEM((fr.y_pack * GROUP, LANES), F32)],
    )
    slabs, y_coefs = lax.optimization_barrier((slabs, y_coefs))
    y_static = swap("gy", slabs)

    together = GROUP if slots % GROUP == 0 else 1
    p0, p1, *slabs = call(
        part(prolong, fr, (nb, together)),
        [fr.frame] * 2 + [rows_of(live_rows)] * n2,
        [info, off, bases, coefs, *y_coefs],
        [SMEM] * 2,
        [
            pltpu.VMEM((27, SUB, LANES), F32),
            pltpu.VMEM((together * CHUNKS // SUB, SUB, LANES), F32),
        ],
        limit=16,
    )
    received = swap("gz", slabs)
    k0, f0, w0, k1, f1, w1 = call(
        part(static_end, fr),
        [fr.frame] * 6,
        [info, k0, f0, w0, *z_static, *x_static, *y_static],
        [SMEM],
        alias={1: 0, 2: 1, 3: 2},
        limit=16,
    )
    groups = slots // GROUP
    cuts = (0, groups // 5, groups * 4 // 5, groups)
    kinds = [
        jax.ShapeDtypeStruct((groups, 6, PROWS, LANES), F32),
        jax.ShapeDtypeStruct((groups, PROWS, LANES), F32),
        jax.ShapeDtypeStruct((groups, PROWS, LANES), F32),
    ]

    def more(setup, first, last):
        return call(
            part(couple, fr, (first, last)),
            kinds,
            [info, off, k0, k1, w0, w1, *setup],
            [SMEM] * 2,
            [pltpu.VMEM((PROWS + 2 * PIECE, LANES), F32)],
            alias={6 + i: i for i in range(len(setup))},
            limit=16,
        )

    setup = more([], *cuts[0:2])
    received, setup = lax.optimization_barrier((received, setup))
    p0, p1, *slabs = call(
        part(coarse_y, fr),
        [fr.frame] * 2 + [rows_of(fr.live_x * (WIDE + 2))] * n1,
        [info, p0, p1, *received],
        [SMEM],
        alias={1: 0, 2: 1},
    )
    received = swap("gy", slabs)
    setup = more(setup, *cuts[1:3])
    received, setup = lax.optimization_barrier((received, setup))
    p0, p1, *slabs = call(
        part(coarse_x, fr),
        [fr.frame] * 2 + [rows_of(WIDE * fr.yf + -(-WIDE * fr.tiles // GROUP) * SUB)] * n0,
        [info, p0, p1, *received],
        [SMEM],
        alias={1: 0, 2: 1},
    )
    received = swap("gx", slabs)

    setup = more(setup, *cuts[2:4])
    p0, p1, r0, r1 = call(
        part(middle, fr), [fr.frame] * 4, [info, p0, p1, k0, f0, k1, f1], [SMEM], alias={1: 0, 2: 1}, limit=16
    )

    solve = pltpu.VMEM((2, PROWS, LANES), F32)
    padded = pltpu.VMEM((2, PROWS + 2 * PIECE, LANES), F32)
    _, _, _, _, core, solved, y_edge, x_edge, slab = call(
        part(enrich, fr),
        [fr.frame] * 4
        + [
            rows_of(bx * by),
            jax.ShapeDtypeStruct((groups, 2, PROWS, LANES), F32),
            rows_of(fr.live_x * 2 * SUB),
            rows_of(2 * MARGIN * by),
            rows_of(live_rows),
        ],
        [info, off, p0, p1, r0, r1, k0, f0, k1, f1, *setup, *received],
        [SMEM] * 2,
        [pltpu.VMEM((fr.rows, LANES), F32)] * 2 + [pltpu.VMEM((PROWS, LANES), F32), solve, padded, padded, pltpu.VMEM((6, PROWS, LANES), F32)],
        alias={2: 0, 3: 1, 4: 2, 5: 3},
        limit=32,
    )

    z_in = swap("gz", [slab] * n2)
    basis = call(
        lay_out,
        rows_of(slots * CHUNKS * 2),
        [info, solved],
        [SMEM],
        [pltpu.VMEM((groups, GROUP * CHUNKS * 2, LANES), F32), pltpu.SemaphoreType.DMA((groups,))],
        out_spec=ANY,
    )
    z_in, basis = lax.optimization_barrier((z_in, basis))
    slabs = call(
        part(fold_y, fr),
        [rows_of(fr.live_x * MARGIN)] * n1,
        [info, y_edge, *z_in],
        [SMEM],
        [pltpu.VMEM((fr.live_x * 2 * SUB, LANES), F32)],
    )
    y_in = swap("gy", slabs)
    slabs = call(
        part(fold_x, fr),
        [rows_of(MARGIN * by)] * n0,
        [info, x_edge, *z_in, *y_in],
        [SMEM],
        [pltpu.VMEM((2 * MARGIN * by, LANES), F32)],
    )
    x_in = swap("gx", slabs)
    edge = rows_of(2 * MARGIN * by)
    update, edges = call(
        part(finish, fr),
        [rows_of(bx * by), edge],
        [info, core, *z_in, *y_in],
        [SMEM],
        [pltpu.VMEM((bx * by, LANES), F32), pltpu.SemaphoreType.DMA],
        out_spec=[ANY, VMEM],
    )
    update = call(
        part(finish_x, fr),
        rows_of(bx * by),
        [info, update, edges, *x_in],
        [SMEM, ANY],
        [pltpu.VMEM(edge.shape, F32), pltpu.SemaphoreType.DMA((2,))],
        alias={1: 0},
        out_spec=ANY,
    )
    new_basis = basis.reshape(slots, CHUNKS, 2, LANES).swapaxes(1, 2)
    return update.reshape(bx, by, bz), new_basis.reshape(1, 1, 1, slots, 2, cells)


def solution(mesh):
    brick = ("gx", "gy", "gz")
    return jax.shard_map(
        local,
        mesh=mesh,
        in_specs=(
            P(*brick),
            P(*brick),
            P(*brick),
            P(),
            P(),
            P(*brick, None, None),
            P(*brick, None, None),
            P(*brick, None, None),
            P(*brick),
            P(*brick, None, None, None),
        ),
        out_specs=(P(*brick), P(*brick, None, None, None)),
        check_vma=False,
    )
```

```python
import functools

import jax
import jax.numpy as jnp
from jax import lax
from jax.experimental import pallas as pl
from jax.experimental.pallas import tpu as pltpu
from jax.sharding import PartitionSpec as P

MARGIN = 4
PIECE = 16
SWEEPS = 20
DAMPING = 2.0 / 3.0

H = MARGIN + 1
WIDE = 2 * MARGIN + 1
LANES = 128
SUB = 8
TOP = 8
GROUP = LANES // PIECE
HALVES = PIECE // SUB
CHUNKS = PIECE * HALVES
PROWS = PIECE * PIECE
F32 = jnp.float32


def iotas():
    shape = (SUB, LANES)
    return lax.broadcasted_iota(jnp.int32, shape, 0), lax.broadcasted_iota(jnp.int32, shape, 1)


def loop(count, body, unroll=1):
    while count % unroll:
        unroll -= 1

    def step(i, _):
        for j in range(unroll):
            body(i * unroll + j)
        return 0

    lax.fori_loop(0, count // unroll, step, 0)


def pick(flag, a, b):
    return jnp.where(flag, a, b)


def pack_tiles(tiles, shift, lane):
    packed = jnp.zeros((SUB, LANES), F32)
    for j, tile in enumerate(tiles):
        packed = jnp.where((lane >> 4) == j, pltpu.roll(tile, (shift + PIECE * j) % LANES, 1), packed)
    return packed


def unpack_tile(packed, j, shift):
    return pltpu.roll(packed, (shift - PIECE * j + 2 * LANES) % LANES, 1)


def sum_rows(values, sub):
    for k in (1, 2, 4):
        low = (sub & k) == 0
        values = [
            jnp.where(low, a, b) + pltpu.roll(jnp.where(low, b, a), SUB - k, 0)
            for a, b in zip(values[0::2], values[1::2])
        ]
    return values[0]


def block_transpose(values, sub, lane):
    for k in (4, 2, 1):
        in_group = ((lane >> 4) & k) != 0
        in_sub = (sub & k) != 0
        moves = in_sub != in_group
        if k == 4:
            others = [pltpu.roll(v, 64, 1) for v in values]
            others = [pltpu.roll(v, 4, 0) for v in others]
        else:
            pairs = [(pltpu.roll(v, PIECE * k, 1), pltpu.roll(v, LANES - PIECE * k, 1)) for v in values]
            others = [jnp.where(in_group, q, p) for q, p in pairs]
            others = [jnp.where(in_sub, pltpu.roll(m, k, 0), pltpu.roll(m, SUB - k, 0)) for m in others]
        values = [jnp.where(moves, o, v) for o, v in zip(others, values)]
    return values


class Frame:
    def __init__(self, bx, by, bz, counts):
        self.bx, self.by, self.bz = bx, by, bz
        self.xf = bx + 2 * H
        self.yf = by + 2 * TOP
        self.tiles = self.yf // SUB
        self.blocks = -(-self.xf * self.tiles // GROUP)
        self.rows = self.blocks * GROUP * SUB
        self.live_x = bx + 2 * MARGIN
        self.live_blocks = self.live_x * self.tiles // GROUP
        self.counts = counts
        self.sides = [1 if n == 2 else 2 for n in counts]

        self.used = by + 2 * H
        self.x_main = -(-WIDE * self.used // SUB) * SUB
        per = by // SUB
        self.z_rows = bx * per // GROUP * SUB
        self.x_pack = (H + 1) * per // GROUP * SUB
        self.y_rows = -(-self.xf * (2 * MARGIN + H) // SUB) * SUB
        self.y_pack = -(-self.xf // GROUP) * SUB

    @property
    def frame(self):
        return rows_of(self.rows)


def rows_of(count):
    return jax.ShapeDtypeStruct((-(-count // SUB) * SUB, LANES), F32)


def zero(ref):
    ref[...] = jnp.zeros(ref.shape, ref.dtype)


VMEM = pl.BlockSpec(memory_space=pltpu.VMEM)
SMEM = pl.BlockSpec(memory_space=pltpu.SMEM)
HBM = pl.BlockSpec(memory_space=pltpu.HBM)
ANY = pl.BlockSpec(memory_space=pl.ANY)


def call(kernel, outs, ins, specs=(), scratch=(), alias=None, limit=12, out_spec=VMEM):
    specs = list(specs) + [VMEM] * (len(ins) - len(specs))
    return pl.pallas_call(
        kernel,
        out_shape=outs,
        in_specs=specs,
        out_specs=out_spec if isinstance(out_spec, list) else jax.tree.map(lambda _: out_spec, outs),
        scratch_shapes=list(scratch),
        input_output_aliases=alias or {},
        compiler_params=pltpu.CompilerParams(vmem_limit_bytes=limit * 1024 * 1024),
    )(*ins)


def is_lower(info, axis, phase):
    return ((info[1 + axis] + phase) & 1) == 0


def swap(axis, slabs):
    count = lax.axis_size(axis)
    received = []
    for phase, slab in enumerate(slabs):
        pairs = [(i, i + 1) for i in range(phase, count - 1, 2)]
        received.append(lax.ppermute(slab, axis, pairs + [(j, i) for i, j in pairs]))
    return received


def look_up(labels, values, which):
    out = jnp.zeros(labels.shape, F32)
    for c in range(values.shape[1]):
        out = out + jnp.where(labels == c, values[which, c], 0.0)
    return out


FIELDS = ((0, H, H, 0), (1, MARGIN, WIDE, H), (2, MARGIN, WIDE + MARGIN, WIDE))
FIRST = (0, H, H + MARGIN)
DEPTH = (H, MARGIN, MARGIN)
WIDTH = H + 2 * MARGIN


def static_first(fr, info, contrast, channel, kappa, labels, forcing, coef, offsets, links, *rest):
    n = fr.sides[2]
    (kap, frc, wgt, own, table), slabs = rest[:5], rest[5 : 5 + n]
    k_buf, l_buf, c_buf, o_buf, i_buf, t_buf, sem = rest[5 + n :]
    _, lane = iotas()
    half = fr.bx * fr.by // 2
    halves = [pl.ds(i * half, half) for i in range(2)]
    pairs = ((labels, l_buf), (kappa, k_buf), (forcing, frc))
    moves = [(contrast, t_buf.at[0]), (channel, t_buf.at[1])]
    for rows in halves:
        moves += [(src.at[rows], dst.at[rows]) for src, dst in pairs]
    moves += [(coef, c_buf), (offsets, o_buf), (links, i_buf)]
    copies = [pltpu.make_async_copy(src, dst, sem.at[i]) for i, (src, dst) in enumerate(moves)]
    for copy in copies:
        copy.start()
    zero(own)
    zero(table)
    for copy in copies[8:]:
        copy.wait()
    own[0 : coef.shape[0], 0 : coef.shape[1]] = c_buf[...]
    for i in range(3):
        table[i : i + 1, 0 : offsets.shape[2]] = o_buf[i]
    table[4:8, 0 : links.shape[1]] = i_buf[...]
    group = lane & (PIECE - 1)

    def block(b):
        tiles = [[], [], []]
        for j in range(GROUP):
            at = pl.ds((b * GROUP + j) * SUB, SUB)
            label = l_buf[at, :]
            k, w = k_buf[at, :] * look_up(label, t_buf, 0), look_up(label, t_buf, 1)
            kap[at, :] = k
            wgt[at, :] = w
            for some, v in zip(tiles, (k, frc[at, :], w)):
                some.append(v)
        for i, slab in enumerate(slabs):
            lower = is_lower(info, 2, i)
            packs = [pack_tiles(tiles[m], pick(lower, high, low), lane) for m, _, high, low in FIELDS]
            mix = jnp.where(group < H, packs[0], jnp.where(group < WIDE, packs[1], packs[2]))
            slab[pl.ds(b * SUB, SUB), :] = mix

    count = fr.bx * fr.by // (GROUP * SUB)
    for copy in copies[:5]:
        copy.wait()
    loop(count // 2, block, 8)
    for copy in copies[5:8]:
        copy.wait()
    loop(count // 2, lambda b: block(b + count // 2), 8)
    for slab in slabs:
        slab[count * SUB : (count + 1) * SUB, :] = own[...]


def static_x(fr, info, kap, frc, wgt, own, *rest):
    n0, n2 = fr.sides[0], fr.sides[2]
    z_in, coefs, slabs = rest[:n2], rest[n2], rest[n2 + 1 :]
    by = fr.by
    coefs[0:SUB, :] = own[...]
    for s, buf in enumerate(z_in):
        coefs[(1 + s) * SUB : (2 + s) * SUB, :] = buf[fr.z_rows : fr.z_rows + SUB, :]
    for i, slab in enumerate(slabs):
        lower = is_lower(info, 0, i)
        for ref, at, count in zip((kap, frc, wgt), FIRST, DEPTH):
            first = pl.multiple_of(pick(lower, (fr.bx - count) * by, 0), SUB)
            slab[at * by : (at + count) * by, :] = ref[pl.ds(first, count * by), :]
        first = pl.multiple_of(pick(lower, fr.z_rows - fr.x_pack, 0), SUB)
        row = WIDTH * by
        for buf in z_in:
            slab[row : row + fr.x_pack, :] = buf[pl.ds(first, fr.x_pack), :]
            row += fr.x_pack
        slab[row : row + coefs.shape[0], :] = coefs[...]


def x_margin(fr, info, phase):
    lower = is_lower(info, 0, phase)
    return pick(lower, fr.bx + H, 0), pick(lower, 0, 1)


def stack(fr, own, *rest):
    x_in, out = rest[:-1], rest[-1]
    each = own.shape[0]
    out[0:each, :] = own[...]
    row = WIDTH * fr.by + fr.sides[2] * fr.x_pack
    for i, buf in enumerate(x_in):
        out[(1 + i) * each : (2 + i) * each, :] = buf[row : row + each, :]


def static_y(fr, info, kap, frc, wgt, *rest):
    n0, n1, n2 = fr.sides
    z_in, x_in, (k0, f0, w0), rest = rest[:n2], rest[n2 : n0 + n2], rest[n0 + n2 : n0 + n2 + 3], rest[n0 + n2 + 3 :]
    slabs, tall = rest[:n1], rest[n1]
    _, lane = iotas()
    by, yf, per = fr.by, fr.yf, fr.by // SUB
    for ref in (k0, f0, w0):
        zero(ref)

    def core(x):
        for t in range(per):
            src = pl.ds(x * by + t * SUB, SUB)
            dst = pl.ds((x + H) * yf + TOP + t * SUB, SUB)
            for frame, ref in ((k0, kap), (f0, frc), (w0, wgt)):
                frame[dst, :] = ref[src, :]

    loop(fr.bx, core, 4)
    for i, buf in enumerate(x_in):
        lower = is_lower(info, 0, i)
        for frame, count, at in zip((k0, f0, w0), DEPTH, FIRST):
            first = pick(lower, fr.bx + H, H - count)
            for j in range(count):
                for t in range(per):
                    row = (at + j) * by + t * SUB
                    frame[pl.ds(pl.multiple_of((first + j) * yf + TOP + t * SUB, SUB), SUB), :] = buf[row : row + SUB, :]

    def plane(x):
        r, o = x * yf, x * WIDTH
        for i, slab in enumerate(slabs):
            lower = is_lower(info, 1, i)
            for frame, count, at in zip((k0, f0, w0), DEPTH, FIRST):
                first = r + pick(lower, TOP + by - count, TOP)
                slab[pl.ds(o + at, count), :] = frame[pl.ds(first, count), :]

    loop(fr.xf, plane, 6)

    narrow = lane < PIECE
    for i, slab in enumerate(slabs):
        t = pick(is_lower(info, 1, i), per - 1, 0)
        row = fr.y_rows
        for s, buf in enumerate(z_in):
            zero(tall)
            for x in range(fr.bx):
                pack, group = x * per // GROUP, x * per % GROUP + t
                v = unpack_tile(buf[pack * SUB : (pack + 1) * SUB, :], group, 0)
                tall[(x + H) * SUB : (x + H + 1) * SUB, :] = jnp.where(narrow, v, 0.0)
            for k, part in enumerate(x_in):
                first, skip = x_margin(fr, info, k)
                for j in range(H):
                    at = (j + skip) * per
                    start = WIDTH * by + s * fr.x_pack + (at // GROUP) * SUB
                    v = unpack_tile(part[pl.ds(pl.multiple_of(start, SUB), SUB), :], at % GROUP + t, 0)
                    to = pl.multiple_of((first + j) * SUB, SUB)
                    tall[pl.ds(to, SUB), :] = jnp.where(narrow, v, 0.0)
            for b in range(fr.y_pack // SUB):
                tiles = [tall[(b * GROUP + j) * SUB : (b * GROUP + j + 1) * SUB, :] for j in range(GROUP)]
                slab[row : row + SUB, :] = pack_tiles(tiles, 0, lane)
                row += SUB


def static_end(fr, info, k_in, f_in, w_in, *rest):
    n0, n1, n2 = fr.sides
    z_in, x_in, y_in = rest[:n2], rest[n2 : n0 + n2], rest[n0 + n2 : n0 + n1 + n2]
    k0, f0, w0, k1, f1, w1 = rest[n0 + n1 + n2 :]
    del k_in, f_in, w_in
    _, lane = iotas()
    by, yf, per = fr.by, fr.yf, fr.by // SUB

    def plane(x):
        r, o = x * yf, x * WIDTH
        for i, buf in enumerate(y_in):
            lower = is_lower(info, 1, i)
            for frame, count, at in zip((k0, f0, w0), DEPTH, FIRST):
                first = r + pick(lower, TOP + by, TOP - count)
                frame[pl.ds(first, count), :] = buf[pl.ds(o + at, count), :]

    loop(fr.xf, plane, 6)
    for ref in (k1, f1, w1):
        zero(ref)
    keeps, shifts = [], []
    for s in range(n2):
        lower = is_lower(info, 2, s)
        lows = [pick(lower, 0, LANES - width) for width in DEPTH]
        keeps.append([(lane >= low) & (lane < low + width) for low, width in zip(lows, DEPTH)])
        shifts.append([pick(lower, LANES - at, LANES - width - at) for at, width in zip(FIRST, DEPTH)])

    def put(row, packs, group):
        for m, ref in enumerate((k1, f1, w1)):
            value = 0.0
            for s, pack in enumerate(packs):
                value = value + jnp.where(keeps[s][m], unpack_tile(pack, group, shifts[s][m]), 0.0)
            ref[pl.ds(pl.multiple_of(row, SUB), SUB), :] = value

    def core(b):
        for i in range(4):
            at = i * per
            packs = [buf[pl.ds((b * 4 * per // GROUP + at // GROUP) * SUB, SUB), :] for buf in z_in]
            for t in range(per):
                put((4 * b + i + H) * yf + TOP + t * SUB, packs, at % GROUP + t)

    loop(fr.bx // 4, core, 2)
    for k, part in enumerate(x_in):
        first, skip = x_margin(fr, info, k)
        for j in range(H):
            at = (j + skip) * per
            starts = [WIDTH * by + s * fr.x_pack + (at // GROUP) * SUB for s in range(n2)]
            packs = [part[pl.ds(pl.multiple_of(start, SUB), SUB), :] for start in starts]
            for t in range(per):
                put((first + j) * yf + TOP + t * SUB, packs, at % GROUP + t)
    for i, part in enumerate(y_in):
        t = pick(is_lower(info, 1, i), fr.tiles - 1, 0)
        for x in range(fr.xf):
            starts = [fr.y_rows + s * fr.y_pack + x // GROUP * SUB for s in range(n2)]
            put(x * yf + t * SUB, [part[start : start + SUB, :] for start in starts], x % GROUP)


def place_masks(z0, lane):
    main = (lane >= z0) & (lane < z0 + PIECE)
    beyond = jnp.where(lane < LANES // 2, lane + LANES, lane - LANES)
    return main, (beyond >= z0) & (beyond < z0 + PIECE)


def corner(off, p):
    return off[0, p] + 1, off[1, p] + TOP - MARGIN, off[2, p] - MARGIN


def piece_rows(fr, off, p):
    x0, y0, _ = corner(off, p)
    base = x0 * fr.yf + y0
    return [pl.ds(base + (c // HALVES) * fr.yf + (c % HALVES) * SUB, SUB) for c in range(CHUNKS)]


def add_main(fr, off, p, valid, values, lane, ref):
    main, _ = place_masks(off[2, p] - MARGIN, lane)
    main = main & valid
    places = piece_rows(fr, off, p)
    new = [ref[a, :] + jnp.where(main, v, 0.0) for a, v in zip(places, values)]
    for a, v in zip(places, new):
        ref[a, :] = v


def add_beyond(fr, off, p, valid, get_values, lane, ref):
    z0 = off[2, p] - MARGIN

    @pl.when(valid & ((z0 < 0) | (z0 + PIECE > LANES)))
    def _():
        _, beyond = place_masks(z0, lane)
        places = piece_rows(fr, off, p)
        new = [ref[a, :] + jnp.where(beyond, v, 0.0) for a, v in zip(places, get_values())]
        for a, v in zip(places, new):
            ref[a, :] = v


def fetch(info, bases, out, sem):
    def copy(p):
        return pltpu.make_async_copy(bases.at[p], out.at[p], sem.at[p])

    def start(p, _):
        copy(p).start()
        return 0

    def wait(p, _):
        copy(p).wait()
        return 0

    lax.fori_loop(0, info[0], start, 0)
    lax.fori_loop(0, info[0], wait, 0)


def prolong(fr, shape, info, off, bases, own, *rest):
    nb, together = shape
    n, m = fr.sides[1], fr.sides[2]
    received, (p0, p1), slabs = rest[:n], rest[n : n + 2], rest[n + 2 : n + m + 2]
    table, keep = rest[n + m + 2 :]
    sub, lane = iotas()
    live = info[0]
    zero(p0)
    zero(p1)
    each = (1 + fr.sides[0]) * (1 + m)
    for i, ref in enumerate((own, *received)):
        for j in range(each):
            table[i * each + j] = ref[j * SUB : (j + 1) * SUB, :]

    def position(axis, step):
        came = 1 + ((info[1 + axis] + jnp.where(step == 0, 1, 0)) & 1)
        return jnp.where(step == 1, 0, came)

    def some(step, _):
        numbers = [step * together + i for i in range(together)]
        per = CHUNKS // SUB
        rows = []
        for p in numbers:
            at = [position(axis, off[4 + axis, p]) for axis in range(3)]
            row = table[(at[1] * (1 + fr.sides[0]) + at[0]) * (1 + m) + at[2]]
            coef = jnp.sum(jnp.where(lane == off[7, p], row, 0.0), axis=1, keepdims=True)
            coef = jnp.broadcast_to(coef, (SUB, LANES))[0:nb]
            for first in range(0, CHUNKS, SUB):
                parts = [bases[p, :, c * LANES : (c + 1) * LANES] * coef for c in range(first, first + SUB)]
                rows.append(sum_rows(parts, sub))
        rows = block_transpose(rows, sub, lane)
        for i, v in enumerate(rows):
            keep[i] = v

        def placed(i, p):
            z0 = off[2, p] - MARGIN
            return [
                pltpu.roll(keep[i * per + c // SUB], (z0 - PIECE * (c % SUB) + 2 * LANES) % LANES, 1)
                for c in range(CHUNKS)
            ]

        for i, p in enumerate(numbers):
            add_main(fr, off, p, p < live, placed(i, p), lane, p0)
        for i, p in enumerate(numbers):
            add_beyond(fr, off, p, p < live, functools.partial(placed, i, p), lane, p1)
        return 0

    lax.fori_loop(0, (live + together - 1) // together, some, 0)

    def block(b):
        tiles = []
        for j in range(GROUP):
            at = pl.ds(fr.yf + (b * GROUP + j) * SUB, SUB)
            tiles.append((p0[at, :], p1[at, :]))
        for i, slab in enumerate(slabs):
            lower = is_lower(info, 2, i)
            main = (lane >= LANES // 2) == lower
            near = [jnp.where(main, x, y) for x, y in tiles]
            slab[pl.ds(b * SUB, SUB), :] = pack_tiles(near, SUB, lane)

    loop(fr.live_blocks, block, 10)


def coarse_y(fr, info, p0_in, p1_in, *rest):
    n = fr.sides[2]
    received, (p0, p1), slabs = rest[:n], rest[n : n + 2], rest[n + 2 :]
    del p0_in, p1_in
    _, lane = iotas()
    packed = fr.live_x * WIDE

    def block(b):
        for i, buf in enumerate(received):
            lower = is_lower(info, 2, i)
            pack = buf[pl.ds(b * SUB, SUB), :]
            places = [pl.ds(fr.yf + (b * GROUP + j) * SUB, SUB) for j in range(GROUP)]
            values = [unpack_tile(pack, j, LANES - SUB) for j in range(GROUP)]
            to_main = ((lane >= LANES - SUB) & lower) | ((lane < SUB) & jnp.logical_not(lower))
            to_beyond = ((lane >= LANES - SUB) & jnp.logical_not(lower)) | ((lane < SUB) & lower)
            main = [p0[a, :] + jnp.where(to_main, v, 0.0) for a, v in zip(places, values)]
            beyond = [p1[a, :] + jnp.where(to_beyond, v, 0.0) for a, v in zip(places, values)]
            for a, v0, v1 in zip(places, main, beyond):
                p0[a, :] = v0
                p1[a, :] = v1

    loop(fr.live_blocks, block, 10)

    def plane(x):
        r = (x + 1) * fr.yf
        for i, slab in enumerate(slabs):
            first = r + pick(is_lower(info, 1, i), TOP + fr.by - H, TOP - MARGIN)
            slab[pl.ds(x * WIDE, WIDE), :] = p0[pl.ds(first, WIDE), :]

    loop(fr.live_x, plane, 8)

    def margin(b):
        for i, slab in enumerate(slabs):
            first = pick(is_lower(info, 1, i), fr.tiles - 2, 0)
            tiles = []
            for j in range(GROUP):
                row = (b * (GROUP // 2) + j // 2 + 1) * fr.yf + (first + j % 2) * SUB
                tiles.append(p1[pl.ds(row, SUB), :])
            slab[pl.ds(packed + b * SUB, SUB), :] = pack_tiles(tiles, SUB, lane)

    loop(fr.live_x * 2 // GROUP, margin, 5)


def coarse_x(fr, info, p0_in, p1_in, *rest):
    n = fr.sides[1]
    received, (p0, p1), slabs = rest[:n], rest[n : n + 2], rest[n + 2 :]
    del p0_in, p1_in
    _, lane = iotas()
    packed = fr.live_x * WIDE
    edge = (lane >= LANES - SUB) | (lane < SUB)

    def plane(x):
        r = (x + 1) * fr.yf
        for i, buf in enumerate(received):
            at = pl.ds(r + pick(is_lower(info, 1, i), TOP + fr.by - MARGIN, TOP - H), WIDE)
            p0[at, :] = p0[at, :] + buf[pl.ds(x * WIDE, WIDE), :]

    loop(fr.live_x, plane, 8)

    def margin(b):
        for i, buf in enumerate(received):
            first = pick(is_lower(info, 1, i), fr.tiles - 2, 0)
            pack = buf[pl.ds(packed + b * SUB, SUB), :]
            places = [
                pl.ds((b * (GROUP // 2) + j // 2 + 1) * fr.yf + (first + j % 2) * SUB, SUB) for j in range(GROUP)
            ]
            values = [jnp.where(edge, unpack_tile(pack, j, LANES - SUB), 0.0) for j in range(GROUP)]
            values = [p1[a, :] + v for a, v in zip(places, values)]
            for a, v in zip(places, values):
                p1[a, :] = v

    loop(fr.live_x * 2 // GROUP, margin, 5)
    main = fr.x_main
    for i, slab in enumerate(slabs):
        row = pl.multiple_of(pick(is_lower(info, 0, i), fr.xf - 1 - WIDE, 1) * fr.yf, SUB)
        for x in range(WIDE):
            slab[x * fr.used : (x + 1) * fr.used, :] = p0[pl.ds(row + x * fr.yf + TOP - H, fr.used), :]
        for b in range(-(-WIDE * fr.tiles // GROUP)):
            tiles = [p1[pl.ds(row + (b * GROUP + j) * SUB, SUB), :] for j in range(GROUP)]
            slab[main + b * SUB : main + (b + 1) * SUB, :] = pack_tiles(tiles, SUB, lane)


def gather_group(fr, off, first, live, fields, lane):
    places = []
    for g in range(GROUP):
        x0, y0, z0 = corner(off, first + g)
        slot = jnp.where(first + g < live, g, -1)
        places.append((x0 * fr.yf + y0, z0, (g * PIECE - z0 + LANES) % LANES, slot))

    def tiles_at(x, h):
        accs = [jnp.zeros((SUB, LANES), F32) for _ in fields]
        for base, z0, shift, slot in places:
            at = pl.ds(base + x * fr.yf + h * SUB, SUB)
            main = (lane >= z0) & (lane < z0 + PIECE)
            keep = (lane >> 4) == slot
            for j, (a, b) in enumerate(fields):
                v = pltpu.roll(jnp.where(main, a[at, :], b[at, :]), shift, 1)
                accs[j] = jnp.where(keep, v, accs[j])
        return accs

    return tiles_at


def couple(fr, part, info, off, k0, k1, w0, w1, *rest):
    wt, scales, weights, kb = rest[-4:]
    sub, lane = iotas()
    live = info[0]
    first_y, last_y = sub == 0, sub == SUB - 1
    z_cell = lane & (PIECE - 1)
    zero(kb)

    def one_group(group, _):
        tiles_at = gather_group(fr, off, group * GROUP, live, ((k0, k1), (w0, w1)), lane)

        def gather(x):
            for h in range(HALVES):
                r = x * PIECE + h * SUB
                kb[pl.ds(PIECE + r, SUB), :], weights[group, pl.ds(r, SUB), :] = tiles_at(x, h)

        loop(PIECE, gather, 8)

        def setup(x):
            for h in range(HALVES):
                r = x * PIECE + h * SUB
                kc = kb[pl.ds(PIECE + r, SUB), :]
                kn = [kb[pl.ds(PIECE + r + d, SUB), :] for d in (PIECE, -PIECE, 1, -1)]
                kn += [pltpu.roll(kc, LANES - 1, 1), pltpu.roll(kc, 1, 1)]
                if h == HALVES - 1:
                    kn[2] = jnp.where(last_y, 0.0, kn[2])
                if h == 0:
                    kn[3] = jnp.where(first_y, 0.0, kn[3])
                kn[4] = jnp.where(z_cell == PIECE - 1, 0.0, kn[4])
                kn[5] = jnp.where(z_cell == 0, 0.0, kn[5])
                faces, diag = [], jnp.zeros((SUB, LANES), F32)
                for k in kn:
                    there = k > 0
                    half = 0.5 * (kc + k)
                    faces.append(jnp.where(there, half, 0.0))
                    diag = diag + jnp.where(there, half, kc)
                inside = kc > 0
                scale = jnp.where(inside, DAMPING / jnp.where(inside, diag, 1.0), 0.0)
                for j, face in enumerate(faces):
                    wt[group, j, pl.ds(r, SUB), :] = face * scale
                scales[group, pl.ds(r, SUB), :] = scale

        loop(PIECE, setup, 8)
        return 0

    lax.fori_loop(part[0], jnp.minimum((live + GROUP - 1) // GROUP, part[1]), one_group, 0)


def residuals(fr, info, cf, kf, ff, rf, first, count, unroll):
    sub, lane = iotas()
    yf, tiles = fr.yf, fr.tiles

    def next_z(a, b):
        return pltpu.roll(jnp.where(lane == 0, b, a), LANES - 1, 1)

    def last_z(a, b):
        return pltpu.roll(jnp.where(lane == LANES - 1, b, a), 1, 1)

    def at_edge(axis, count, first, last, position):
        low = (position == first) & (info[1 + axis] == 0)
        high = (position == last) & (info[1 + axis] == count - 1)
        return jnp.where(low, 1.0, 0.0) + jnp.where(high, 1.0, 0.0)

    out_y = [at_edge(1, fr.counts[1], TOP, TOP + fr.by - 1, sub + t * SUB) for t in range(tiles)]
    out_z = at_edge(2, fr.counts[2], 0, LANES - 1, lane)

    def flux_x(x):
        fluxes = []
        for t in range(tiles):
            at, to = pl.ds(x * yf + t * SUB, SUB), pl.ds((x + 1) * yf + t * SUB, SUB)
            fluxes += [(k[at, :] + k[to, :]) * (c[at, :] - c[to, :]) for c, k in zip(cf, kf)]
        return fluxes

    def residual(x, before):
        r = x * yf
        after = flux_x(x)
        out_x = at_edge(0, fr.counts[0], H, H + fr.bx - 1, x)
        last_y = [jnp.zeros((SUB, LANES), F32)] * 2
        for t in range(tiles):
            at, to = pl.ds(r + t * SUB, SUB), pl.ds(r + t * SUB + 1, SUB)
            cs, ks = (cf[0][at, :], cf[1][at, :]), (kf[0][at, :], kf[1][at, :])
            fz = []
            for i in range(2):
                cn, kn = next_z(cs[i], cs[1 - i]), next_z(ks[i], ks[1 - i])
                fz.append((ks[i] + kn) * (cs[i] - cn))
            for i, (c, k, f, out) in enumerate(zip(cf, kf, ff, rf)):
                fy = pltpu.roll((ks[i] + k[to, :]) * (cs[i] - c[to, :]), 1, 0)
                fy_next = (ks[i] + k[to, :]) * (cs[i] - c[to, :])
                fy_last = jnp.where(sub == 0, last_y[i], fy)
                last_y[i] = fy
                outside = out_x + out_y[t] + (out_z if i == 0 else 0.0)
                total = (after[2 * t + i] - before[2 * t + i]) + (fy_next - fy_last)
                total = total + (fz[i] - last_z(fz[i], fz[1 - i])) + outside * (ks[i] * cs[i])
                out[at, :] = jnp.where(ks[i] > 0, f[at, :] - 0.5 * total, 0.0)
        return tuple(after)

    def some(i, before):
        for j in range(unroll):
            before = residual(first + i * unroll + j, before)
        return before

    lax.fori_loop(0, count // unroll, some, tuple(flux_x(first - 1)))


def masked(fr, cf, kf, first, count):
    def plane(x):
        for t in range(fr.tiles):
            at = pl.ds((first + x) * fr.yf + t * SUB, SUB)
            for c, k in zip(cf, kf):
                c[at, :] = jnp.where(k[at, :] > 0, c[at, :], 0.0)

    loop(count, plane, 3)


def middle(fr, info, p0_in, p1_in, k0, f0, k1, f1, p0, p1, r0, r1):
    del p0_in, p1_in
    masked(fr, (p0, p1), (k0, k1), WIDE, fr.xf - 2 * WIDE)
    residuals(fr, info, (p0, p1), (k0, k1), (f0, f1), (r0, r1), WIDE + 2, fr.xf - 2 * WIDE - 4, 4)


def enrich(fr, info, off, p0, p1, r0_in, r1_in, k0, f0, k1, f1, wt, scales, weights, *rest):
    n0 = fr.sides[0]
    x_in, rest = rest[:n0], rest[n0:]
    c0, c1, r0, r1, core, solved, y_edge, x_edge, slab = rest[:9]
    q0, q1, rb, base, va, vb, here = rest[9:]
    del p0, p1, r0_in, r1_in
    sub, lane = iotas()
    yf, tiles = fr.yf, fr.tiles
    live = info[0]
    main_rows = fr.x_main
    edge = (lane >= LANES - SUB) | (lane < SUB)

    for i, buf in enumerate(x_in):
        row = pl.multiple_of(pick(is_lower(info, 0, i), fr.xf - WIDE, 0) * yf, SUB)
        for x in range(WIDE):
            a = pl.ds(row + x * yf + TOP - H, fr.used)
            c0[a, :] = c0[a, :] + buf[x * fr.used : (x + 1) * fr.used, :]
        for b in range(-(-WIDE * tiles // GROUP)):
            pack = buf[main_rows + b * SUB : main_rows + (b + 1) * SUB, :]
            count = min(GROUP, WIDE * tiles - b * GROUP)
            places = [pl.ds(row + (b * GROUP + j) * SUB, SUB) for j in range(count)]
            values = [jnp.where(edge, unpack_tile(pack, j, LANES - SUB), 0.0) for j in range(count)]
            for a, v in zip(places, [c1[a, :] + v for a, v in zip(places, values)]):
                c1[a, :] = v

    for first in (0, fr.xf - WIDE):
        masked(fr, (c0, c1), (k0, k1), first, WIDE)
    for first in (1, fr.xf - 1 - WIDE - 1):
        residuals(fr, info, (c0, c1), (k0, k1), (f0, f1), (r0, r1), first, WIDE + 1, 5)

    zero(q0)
    zero(q1)
    for ref in (va, vb):
        zero(ref)

    z_cell = lane & (PIECE - 1)
    tz = tent(z_cell.astype(F32))
    ty = [tent(sub.astype(F32) + float(SUB * h)) * tz for h in range(HALVES)]

    def one_group(group, _):
        first = group * GROUP
        tiles_at = gather_group(fr, off, first, live, ((r0, r1),), lane)

        def gather(x):
            for h in range(HALVES):
                r = x * PIECE + h * SUB
                at = pl.ds(r, SUB)
                s = tiles_at(x, h)[0] * scales[group, at, :]
                s2 = s * weights[group, at, :]
                for i, v in enumerate((s, s2)):
                    base[i, at, :] = v
                    va[i, pl.ds(PIECE + r, SUB), :] = v

        loop(PIECE, gather, 16)
        here[...] = wt[group]

        def sweep(src, dst, out=None):
            for x in range(PIECE):
                for h in range(HALVES):
                    r = x * PIECE + h * SUB
                    a = PIECE + r
                    w = [here[j, r : r + SUB, :] for j in range(6)]
                    for s in range(2):
                        v = src[s, a : a + SUB, :]
                        total = base[s, r : r + SUB, :] + v * (1.0 - DAMPING)
                        if x < PIECE - 1:
                            total = total + w[0] * src[s, a + PIECE : a + PIECE + SUB, :]
                        if x > 0:
                            total = total + w[1] * src[s, a - PIECE : a - PIECE + SUB, :]
                        total = total + w[2] * src[s, a + 1 : a + 1 + SUB, :]
                        total = total + w[3] * src[s, a - 1 : a - 1 + SUB, :]
                        total = total + w[4] * pltpu.roll(v, LANES - 1, 1)
                        total = total + w[5] * pltpu.roll(v, 1, 1)
                        if out is None:
                            dst[s, a : a + SUB, :] = total
                        else:
                            out[group, s, r : r + SUB, :] = total

        def two(i, _):
            sweep(va, vb)
            sweep(vb, va)
            return 0

        lax.fori_loop(0, (SWEEPS - 2) // 2, two, 0)
        if SWEEPS % 2:
            sweep(va, vb)
            sweep(vb, None, solved)
        else:
            sweep(va, None, solved)

        for c in range(CHUNKS):
            a = slice(c * SUB, (c + 1) * SUB)
            weight = ty[c % HALVES] * float(tent(c // HALVES))
            rb[a, :] = (solved[group, 0, a, :] + solved[group, 1, a, :]) * weight

        def placed(g):
            shift = (off[2, first + g] - MARGIN - g * PIECE + 2 * LANES) % LANES
            return [pltpu.roll(rb[c * SUB : (c + 1) * SUB, :], shift, 1) for c in range(CHUNKS)]

        for g in range(GROUP):
            add_main(fr, off, first + g, first + g < live, placed(g), lane, q0)
        for g in range(GROUP):
            add_beyond(fr, off, first + g, first + g < live, functools.partial(placed, g), lane, q1)
        return 0

    lax.fori_loop(0, (live + GROUP - 1) // GROUP, one_group, 0)

    def block(b):
        part = [q1[pl.ds(yf + (b * GROUP + j) * SUB, SUB), :] for j in range(GROUP)]
        slab[pl.ds(b * SUB, SUB), :] = pack_tiles(part, SUB, lane)

    loop(fr.live_blocks, block, 10)

    def core_rows(x):
        for t in range(fr.by // SUB):
            at = pl.ds((x + H) * yf + TOP + t * SUB, SUB)
            core[pl.ds(x * fr.by + t * SUB, SUB), :] = c0[at, :] + q0[at, :]

    loop(fr.bx, core_rows, 8)

    def edge_rows(x):
        for j, t in enumerate((tiles - 1, 0)):
            y_edge[pl.ds((2 * x + j) * SUB, SUB), :] = q0[pl.ds((x + 1) * yf + t * SUB, SUB), :]

    loop(fr.live_x, edge_rows, 8)
    for i, x in enumerate(edge_planes(fr)):
        row = (x + 1) * yf + TOP
        x_edge[i * fr.by : (i + 1) * fr.by, :] = q0[row : row + fr.by, :]


def tent(t):
    return (t + 0.5) * (PIECE - t - 0.5) * (4.0 / (PIECE * PIECE))


def lay_out(info, solved, basis, buf, sem):
    sub, lane = iotas()
    count = GROUP * CHUNKS * 2
    copies = []
    for group in range(solved.shape[0]):
        some = group * GROUP < info[0]

        @pl.when(some)
        def _():
            for c in range(0, CHUNKS, SUB):
                values = []
                for i in range(c, c + SUB):
                    values += [solved[group, s, i * SUB : (i + 1) * SUB, :] for s in range(2)]
                for i, v in enumerate(block_transpose(values, sub, lane)):
                    buf[group, pl.ds(c * 2 + i, GROUP, stride=CHUNKS * 2), :] = v

        @pl.when(jnp.logical_not(some))
        def _():
            buf[group] = jnp.zeros((count, LANES), F32)

        copies.append(pltpu.make_async_copy(buf.at[group], basis.at[pl.ds(group * count, count)], sem.at[group]))
        copies[-1].start()
    for copy in copies:
        copy.wait()


def edge_planes(fr):
    return [*range(fr.live_x - MARGIN, fr.live_x), *range(MARGIN)]


def z_part(info, sides, received, pack, j, lane):
    total = 0.0
    for i, buf in enumerate(received):
        lower = is_lower(info, 2, i)
        keep = ((lane >= LANES - SUB) & lower) | ((lane < SUB) & jnp.logical_not(lower))
        v = unpack_tile(buf[pl.ds(pack * SUB, SUB), :], j, LANES - SUB)
        total = total + jnp.where(keep, v, 0.0)
    return total


def fold_y(fr, info, y_edge, *rest):
    n = fr.sides[2]
    received, slabs, tmp = rest[:n], rest[n:-1], rest[-1]
    _, lane = iotas()

    def planes(b):
        for i in range(4):
            for j, t in enumerate((fr.tiles - 1, 0)):
                m = i * fr.tiles + t
                at = pl.ds(((4 * b + i) * 2 + j) * SUB, SUB)
                part = z_part(info, n, received, b * (4 * fr.tiles // GROUP) + m // GROUP, m % GROUP, lane)
                tmp[at, :] = y_edge[at, :] + part

    loop(fr.live_x // 4, planes, 5)

    def plane(x):
        for i, slab in enumerate(slabs):
            first = x * 2 * SUB + pick(is_lower(info, 1, i), 0, SUB + MARGIN)
            slab[pl.ds(x * MARGIN, MARGIN), :] = tmp[pl.ds(first, MARGIN), :]

    loop(fr.live_x, plane, 8)


def fold_x(fr, info, x_edge, *rest):
    n1, n2 = fr.sides[1], fr.sides[2]
    z_in, y_in, slabs, tmp = rest[:n2], rest[n2 : n1 + n2], rest[n1 + n2 : -1], rest[-1]
    _, lane = iotas()
    by = fr.by
    for i, x in enumerate(edge_planes(fr)):
        for t in range(by // SUB):
            m = x * fr.tiles + t + 1
            a = slice(i * by + t * SUB, i * by + (t + 1) * SUB)
            tmp[a, :] = x_edge[a, :] + z_part(info, n2, z_in, m // GROUP, m % GROUP, lane)
        for k, buf in enumerate(y_in):
            a = pl.ds(i * by + pick(is_lower(info, 1, k), by - MARGIN, 0), MARGIN)
            tmp[a, :] = tmp[a, :] + buf[x * MARGIN : (x + 1) * MARGIN, :]
    count = MARGIN * by
    for i, slab in enumerate(slabs):
        slab[...] = tmp[pl.ds(pl.multiple_of(pick(is_lower(info, 0, i), 0, count), SUB), count), :]


def finish(fr, info, core, *rest):
    n1, n2 = fr.sides[1:]
    z_in, y_in, (out, edges, buf, sem) = rest[:n2], rest[n2 : n1 + n2], rest[n1 + n2 :]
    _, lane = iotas()
    by = fr.by

    def planes(b):
        for i in range(4):
            row = (4 * b + i) * by
            for t in range(by // SUB):
                m = i * fr.tiles + t + 1
                at = pl.ds(row + t * SUB, SUB)
                pack = (b + MARGIN // 4) * (4 * fr.tiles // GROUP) + m // GROUP
                buf[at, :] = core[at, :] + z_part(info, n2, z_in, pack, m % GROUP, lane)
            for k, part in enumerate(y_in):
                a = pl.ds(row + pick(is_lower(info, 1, k), by - MARGIN, 0), MARGIN)
                buf[a, :] = buf[a, :] + part[pl.ds((4 * b + i + MARGIN) * MARGIN, MARGIN), :]

    loop(fr.bx // 4, planes, 4)
    count = MARGIN * by
    inner = pl.ds(count, fr.bx * by - 2 * count)
    copy = pltpu.make_async_copy(buf.at[inner], out.at[inner], sem)
    copy.start()
    edges[0:count, :] = buf[0:count, :]
    edges[count : 2 * count, :] = buf[fr.bx * by - count : fr.bx * by, :]
    copy.wait()


def finish_x(fr, info, out_in, edges, *rest):
    x_in, (out, buf, sem) = rest[:-3], rest[-3:]
    del out_in
    count = MARGIN * fr.by
    buf[...] = edges[...]
    for i, part in enumerate(x_in):
        a = pl.ds(pl.multiple_of(pick(is_lower(info, 0, i), count, 0), SUB), count)
        buf[a, :] = buf[a, :] + part[...]
    places = (0, fr.bx * fr.by - count)
    copies = [
        pltpu.make_async_copy(buf.at[pl.ds(i * count, count)], out.at[pl.ds(row, count)], sem.at[i])
        for i, row in enumerate(places)
    ]
    for copy in copies:
        copy.start()
    for copy in copies:
        copy.wait()


def local(
    forcing,
    kappa_base,
    labels,
    contrast,
    channel_weight,
    coarse_coef,
    source_link,
    offsets,
    live_pieces,
    resident_bases,
):
    bx, by, bz = forcing.shape
    axes = ("gx", "gy", "gz")
    fr = Frame(bx, by, bz, [lax.axis_size(a) for a in axes])
    slots, nb = resident_bases.shape[3], resident_bases.shape[4]
    nd = coarse_coef.shape[3]
    cells = PIECE**3
    part = functools.partial
    n0, n1, n2 = fr.sides
    live_rows = fr.live_blocks * SUB

    info = jnp.stack([live_pieces[0, 0, 0]] + [lax.axis_index(a).astype(jnp.int32) for a in axes])

    def stays(a):
        return pltpu.with_memory_space_constraint(a, pltpu.HBM)

    raw = [stays(a.reshape(bx * by, bz)) for a in (kappa_base, labels, forcing)]
    raw += [
        stays(jnp.swapaxes(coarse_coef.reshape(nd, nb), 0, 1)),
        stays(jnp.swapaxes(offsets.reshape(slots, 1, 3), 0, 2).reshape(3, 1, slots)),
        stays(jnp.swapaxes(source_link.reshape(slots, 4), 0, 1)),
    ]
    bases = stays(resident_bases.reshape(slots, nb, cells))

    core = rows_of(bx * by)
    kap, frc, wgt, coefs, off, *slabs = call(
        part(static_first, fr),
        [core] * 3 + [rows_of(SUB), jax.ShapeDtypeStruct((SUB, LANES), jnp.int32)] + [rows_of(fr.z_rows + SUB)] * n2,
        [info, stays(contrast), stays(channel_weight), *raw],
        [SMEM] + [HBM] * 8,
        [
            pltpu.VMEM((bx * by, LANES), F32),
            pltpu.VMEM((bx * by, LANES), jnp.int32),
            pltpu.VMEM((nb, nd), F32),
            pltpu.VMEM((3, 1, slots), jnp.int32),
            pltpu.VMEM((4, slots), jnp.int32),
            pltpu.SMEM((2, contrast.shape[0]), F32),
            pltpu.SemaphoreType.DMA((11,)),
        ],
    )
    z_static = swap("gz", slabs)
    each = (1 + n2) * SUB
    coefs, *slabs = call(
        part(static_x, fr),
        [rows_of(each)] + [rows_of(WIDTH * by + n2 * fr.x_pack + each)] * n0,
        [info, kap, frc, wgt, coefs, *z_static],
        [SMEM],
    )
    x_static = swap("gx", slabs)
    bases = call(fetch, jax.ShapeDtypeStruct(bases.shape, F32), [info, bases], [SMEM, HBM], [pltpu.SemaphoreType.DMA((slots,))], limit=8)
    x_static, bases = lax.optimization_barrier((x_static, bases))
    coefs = call(part(stack, fr), rows_of(each * (1 + n0)), [coefs, *x_static])
    y_coefs = swap("gy", [coefs] * n1)
    kap, coefs = lax.optimization_barrier((kap, coefs))
    k0, f0, w0, *slabs = call(
        part(static_y, fr),
        [fr.frame] * 3 + [rows_of(fr.y_rows + n2 * fr.y_pack)] * n1,
        [info, kap, frc, wgt, *z_static, *x_static],
        [SMEM],
        [pltpu.VMEM((fr.y_pack * GROUP, LANES), F32)],
    )
    slabs, y_coefs = lax.optimization_barrier((slabs, y_coefs))
    y_static = swap("gy", slabs)

    together = GROUP if slots % GROUP == 0 else 1
    p0, p1, *slabs = call(
        part(prolong, fr, (nb, together)),
        [fr.frame] * 2 + [rows_of(live_rows)] * n2,
        [info, off, bases, coefs, *y_coefs],
        [SMEM] * 2,
        [
            pltpu.VMEM((27, SUB, LANES), F32),
            pltpu.VMEM((together * CHUNKS // SUB, SUB, LANES), F32),
        ],
        limit=16,
    )
    received = swap("gz", slabs)
    k0, f0, w0, k1, f1, w1 = call(
        part(static_end, fr),
        [fr.frame] * 6,
        [info, k0, f0, w0, *z_static, *x_static, *y_static],
        [SMEM],
        alias={1: 0, 2: 1, 3: 2},
        limit=16,
    )
    groups = slots // GROUP
    cuts = (0, groups // 5, groups * 4 // 5, groups)
    kinds = [
        jax.ShapeDtypeStruct((groups, 6, PROWS, LANES), F32),
        jax.ShapeDtypeStruct((groups, PROWS, LANES), F32),
        jax.ShapeDtypeStruct((groups, PROWS, LANES), F32),
    ]

    def more(setup, first, last):
        return call(
            part(couple, fr, (first, last)),
            kinds,
            [info, off, k0, k1, w0, w1, *setup],
            [SMEM] * 2,
            [pltpu.VMEM((PROWS + 2 * PIECE, LANES), F32)],
            alias={6 + i: i for i in range(len(setup))},
            limit=16,
        )

    setup = more([], *cuts[0:2])
    received, setup = lax.optimization_barrier((received, setup))
    p0, p1, *slabs = call(
        part(coarse_y, fr),
        [fr.frame] * 2 + [rows_of(fr.live_x * (WIDE + 2))] * n1,
        [info, p0, p1, *received],
        [SMEM],
        alias={1: 0, 2: 1},
    )
    received = swap("gy", slabs)
    setup = more(setup, *cuts[1:3])
    received, setup = lax.optimization_barrier((received, setup))
    p0, p1, *slabs = call(
        part(coarse_x, fr),
        [fr.frame] * 2 + [rows_of(fr.x_main + -(-WIDE * fr.tiles // GROUP) * SUB)] * n0,
        [info, p0, p1, *received],
        [SMEM],
        alias={1: 0, 2: 1},
    )
    received = swap("gx", slabs)

    setup = more(setup, *cuts[2:4])
    p0, p1, r0, r1 = call(
        part(middle, fr), [fr.frame] * 4, [info, p0, p1, k0, f0, k1, f1], [SMEM], alias={1: 0, 2: 1}, limit=16
    )

    solve = pltpu.VMEM((2, PROWS, LANES), F32)
    padded = pltpu.VMEM((2, PROWS + 2 * PIECE, LANES), F32)
    _, _, _, _, core, solved, y_edge, x_edge, slab = call(
        part(enrich, fr),
        [fr.frame] * 4
        + [
            rows_of(bx * by),
            jax.ShapeDtypeStruct((groups, 2, PROWS, LANES), F32),
            rows_of(fr.live_x * 2 * SUB),
            rows_of(2 * MARGIN * by),
            rows_of(live_rows),
        ],
        [info, off, p0, p1, r0, r1, k0, f0, k1, f1, *setup, *received],
        [SMEM] * 2,
        [pltpu.VMEM((fr.rows, LANES), F32)] * 2 + [pltpu.VMEM((PROWS, LANES), F32), solve, padded, padded, pltpu.VMEM((6, PROWS, LANES), F32)],
        alias={2: 0, 3: 1, 4: 2, 5: 3},
        limit=32,
    )

    z_in = swap("gz", [slab] * n2)
    basis = call(
        lay_out,
        rows_of(slots * CHUNKS * 2),
        [info, solved],
        [SMEM],
        [pltpu.VMEM((groups, GROUP * CHUNKS * 2, LANES), F32), pltpu.SemaphoreType.DMA((groups,))],
        out_spec=ANY,
    )
    z_in, basis = lax.optimization_barrier((z_in, basis))
    slabs = call(
        part(fold_y, fr),
        [rows_of(fr.live_x * MARGIN)] * n1,
        [info, y_edge, *z_in],
        [SMEM],
        [pltpu.VMEM((fr.live_x * 2 * SUB, LANES), F32)],
    )
    y_in = swap("gy", slabs)
    slabs = call(
        part(fold_x, fr),
        [rows_of(MARGIN * by)] * n0,
        [info, x_edge, *z_in, *y_in],
        [SMEM],
        [pltpu.VMEM((2 * MARGIN * by, LANES), F32)],
    )
    x_in = swap("gx", slabs)
    edge = rows_of(2 * MARGIN * by)
    update, edges = call(
        part(finish, fr),
        [rows_of(bx * by), edge],
        [info, core, *z_in, *y_in],
        [SMEM],
        [pltpu.VMEM((bx * by, LANES), F32), pltpu.SemaphoreType.DMA],
        out_spec=[ANY, VMEM],
    )
    update = call(
        part(finish_x, fr),
        rows_of(bx * by),
        [info, update, edges, *x_in],
        [SMEM, ANY],
        [pltpu.VMEM(edge.shape, F32), pltpu.SemaphoreType.DMA((2,))],
        alias={1: 0},
        out_spec=ANY,
    )
    new_basis = basis.reshape(slots, CHUNKS, 2, LANES).swapaxes(1, 2)
    return update.reshape(bx, by, bz), new_basis.reshape(1, 1, 1, slots, 2, cells)


def solution(mesh):
    brick = ("gx", "gy", "gz")
    return jax.shard_map(
        local,
        mesh=mesh,
        in_specs=(
            P(*brick),
            P(*brick),
            P(*brick),
            P(),
            P(),
            P(*brick, None, None),
            P(*brick, None, None),
            P(*brick, None, None),
            P(*brick),
            P(*brick, None, None, None),
        ),
        out_specs=(P(*brick), P(*brick, None, None, None)),
        check_vma=False,
    )
```
